256 devices in a mesh: dp: 8 (over y_hi, x), pencil: 32 (over z, y_lo, core).
Axes of the slice: x: 4, y: 4 (y_hi: 2, y_lo: 2; y = y_hi * 2 + y_lo), z: 8, core: 2. Of those that a mesh axis runs over, the one named last changes fastest.
Arguments:
- field_in: bfloat16 [8, 128, 48, 8192], P('dp', 'pencil'), may hold values from -6 to 6
- grad_out: bfloat16 [8, 128, 48, 8192], P('dp', 'pencil'), may hold values from -6 to 6
- w_spec: float32 [2, 32, 16, 32, 2304], P(None, 'pencil', 'dp'), may hold values from -6 to 6
- w_local: bfloat16 [48, 48], replicated, may hold values from -0.875 to 0.875
Outputs:
- grad_in: bfloat16 [8, 128, 48, 8192], P('dp', 'pencil')
- grad_spec: float32 [2, 32, 16, 32, 2304], P(None, 'pencil', 'dp')
- grad_local: float32 [48, 48], replicated
The draws below stay inside these ranges and needn't reach their ends.
All inputs are finite; a program needn't handle non-finite values.
Results may differ from the reference program's by a relative error of at most 0.009.
Values sent between devices are 32-bit elements; how exact they have to be, the bound alone decides.
A program may use at most 192 MiB of HBM per device.

```python
import jax
import jax.numpy as jnp
from jax import lax

X = 128
Y = 128
Z = 64
C = 48
KX = 32
KY = 32
KZ = 16
SAMPLES = 8
PLANE = 8192


def level_of(own_key, dims, cuts, least, top_value):
    factor_of = 1.0
    for position, shards_of in cuts:
        steps = jax.random.uniform(jax.random.fold_in(jax.random.fold_in(own_key, 6), position), (shards_of,), jnp.float32, least / len(cuts), top_value / len(cuts))
        factor_of = factor_of * jnp.repeat(jnp.exp(steps), dims[position] // shards_of).reshape((-1,) + (1,) * (len(dims) - 1 - position))
    return factor_of


def gaussian(stream_key, dims, spread, most, shards=(), held_as=jnp.bfloat16):
    level = level_of(stream_key, dims, shards, -0.22, 0.18) if shards else 1.0
    array = jax.random.normal(stream_key, dims, jnp.float32) * spread * level
    return jnp.minimum(jnp.maximum(array, -most), most).astype(held_as)


def setup_inputs(seed: int = 0) -> dict:
    arg_keys = jax.random.split(jax.random.key(seed), 5)
    return {
        "field_in": gaussian(arg_keys[0], (SAMPLES, X, C, PLANE), 1.0, 6.0, ((0, 8), (1, 32))),
        "grad_out": gaussian(arg_keys[1], (SAMPLES, X, C, PLANE), 1.0, 6.0, ((0, 8), (1, 32))),
        "w_spec": gaussian(arg_keys[2], (2, KY, KZ, KX, C * C), 0.4, 6.0, ((1, 32), (2, 8)), jnp.float32),
        "w_local": gaussian(arg_keys[3], (C, C), C ** -0.5, 0.875),
    }


highest = lax.Precision.HIGHEST


def freq_index(length, count):
    return jnp.concatenate([jnp.arange(count // 2), jnp.arange(length - count // 2, length)]).astype(jnp.int32)


def analyse(values):
    spectrum = jnp.fft.rfft(values, axis=3)[..., :KZ]
    spectrum = jnp.fft.fft(spectrum, axis=2)[:, :, freq_index(Y, KY), :]
    spectrum = jnp.fft.fft(spectrum, axis=0)[freq_index(X, KX)]
    return spectrum.transpose(2, 3, 0, 1)


def synthesize(modes):
    spectrum = modes.transpose(2, 3, 0, 1)
    padded = jnp.zeros((X, C, KY, KZ), spectrum.dtype).at[freq_index(X, KX)].set(spectrum)
    spectrum = jnp.fft.ifft(padded, axis=0)
    padded = jnp.zeros((X, C, Y, KZ), spectrum.dtype).at[:, :, freq_index(Y, KY), :].set(spectrum)
    spectrum = jnp.fft.ifft(padded, axis=2)
    padded = jnp.zeros((X, C, Y, Z // 2 + 1), spectrum.dtype).at[..., :KZ].set(spectrum)
    return jnp.fft.irfft(padded, n=Z, axis=3)


def gelu_slope(values):
    cumul = 0.5 * (1.0 + lax.erf(values * 0.7071067811865476))
    density = jnp.exp(-0.5 * values * values) * 0.3989422804014327
    return cumul + values * density


def reference(field_in, grad_out, w_spec, w_local):
    weights = (w_spec[0] + 1j * w_spec[1]).reshape(KY, KZ, KX, C, C)
    local_w = w_local.astype(jnp.float32)
    z_weight = jnp.where(jnp.arange(KZ) == 0, 1.0, 2.0).astype(jnp.float32)
    volume = X * Y * Z

    def one_sample(pair):
        sample, upstream = pair
        values = sample.astype(jnp.float32)
        spec_in = analyse(values.reshape(X, C, Y, Z))
        mixed_modes = jnp.einsum("yzkc,yzkco->yzko", spec_in, weights, precision=highest)
        spectral = synthesize(mixed_modes).reshape(X, C, Y * Z)
        preact = spectral + jnp.einsum("xcp,co->xop", values, local_w, precision=highest)
        slopes = upstream.astype(jnp.float32) * gelu_slope(preact)
        slopes_half = slopes.astype(jnp.bfloat16)
        slopes_wide = slopes_half.astype(jnp.float32)
        spec_grad = analyse(slopes_wide.reshape(X, C, Y, Z)) * (z_weight / volume)[None, :, None, None]
        mode_grad = jnp.einsum("yzko,yzkco->yzkc", spec_grad, jnp.conj(weights), precision=highest)
        spatial = synthesize(mode_grad / z_weight[None, :, None, None]) * volume
        local_back = jnp.einsum("xop,co->xcp", slopes_wide, local_w, precision=highest)
        grad_sample = (spatial.reshape(X, C, Y * Z) + local_back).astype(jnp.bfloat16)
        local_terms = jnp.einsum("xcp,xop->co", values, slopes_wide, precision=highest)
        return grad_sample, spec_in, spec_grad, local_terms

    grad_in, spec_all, grad_all, local_all = lax.map(one_sample, (field_in, grad_out))
    product = jnp.einsum("nyzkc,nyzko->yzkco", jnp.conj(spec_all), grad_all, precision=highest)
    grad_spec = jnp.stack([jnp.real(product), jnp.imag(product)]).reshape(2, KY, KZ, KX, C * C)
    return grad_in, grad_spec, jnp.sum(local_all, axis=0)
```

```python
import functools

import jax
import jax.numpy as jnp
import ml_dtypes
import numpy as np
from jax import lax
from jax.experimental import pallas as pl
from jax.experimental.pallas import tpu as pltpu
from jax.sharding import PartitionSpec as P

X = 128
Y = 128
Z = 64
C = 48
KX = 32
KY = 32
KZ = 16
ROWS = 4
GROUP = 4
LANES = 128
LIMIT = 56 * 1024 * 1024

MESH = pl.DeviceIdType.MESH
f32 = jnp.float32
bf16 = jnp.bfloat16


def split(table):
    high = table.astype(np.float32).astype(ml_dtypes.bfloat16)
    low = (table - high.astype(np.float64)).astype(np.float32).astype(ml_dtypes.bfloat16)
    return high, low


def signed(count):
    freqs = np.arange(count)
    return np.where(freqs < count // 2, freqs, freqs - count)


def forward_table(length, count):
    angles = 2.0 * np.pi * (np.outer(signed(count), np.arange(length)) % length) / length
    cos, sin = np.cos(angles), np.sin(angles)
    table = np.zeros((2, count, length, 2))
    table[0, :, :, 0] = cos
    table[0, :, :, 1] = sin
    table[1, :, :, 0] = -sin
    table[1, :, :, 1] = cos
    return table.reshape(2 * count, length, 2)


def z_table(scale):
    angles = 2.0 * np.pi * (np.outer(np.arange(KZ), np.arange(Z)) % Z) / Z
    table = np.zeros((KZ, GROUP, 2, GROUP, Z))
    for place in range(GROUP):
        table[:, place, 0, place] = np.cos(angles) * scale[:, None]
        table[:, place, 1, place] = -np.sin(angles) * scale[:, None]
    return table.reshape(KZ * GROUP * 2, GROUP * Z)


def z_scale():
    return np.where(np.arange(KZ) == 0, 1.0, 2.0) / float(X * Y * Z)


def tall(table):
    return np.concatenate(split(table), axis=0)


def wide3(table):
    high, low = split(table)
    return np.concatenate([high, low, high], axis=1)


def y_forward():
    return forward_table(Y, KY).reshape(2 * KY, Y * 2)


def x_forward():
    table = forward_table(X, KX).reshape(2 * KX, X // ROWS, ROWS, 2)
    return table.transpose(0, 1, 3, 2).reshape(2 * KX, X * 2)


def nt(left, right):
    return lax.dot_general(left, right, (((1,), (1,)), ((), ())), preferred_element_type=f32)


def tn(left, right):
    return lax.dot_general(left, right, (((0,), (0,)), ((), ())), preferred_element_type=f32)


def nn(left, right):
    return jnp.dot(left, right, preferred_element_type=f32)


def halves(values):
    high = values.astype(bf16)
    low = (values - high.astype(f32)).astype(bf16)
    return high, low


def cells(ref, block):
    return ref[:, :, pl.ds(pl.multiple_of(block * GROUP * Z, GROUP * Z), GROUP * Z)].reshape(
        ROWS * C, GROUP * Z
    )


def z_forward(values, table, q_ref, block):
    both = nt(table, values)
    half = KZ * GROUP * 2
    part = both[:half] + both[half:]
    q_ref[:, pl.ds(pl.multiple_of(block * 8, 8), 8), :] = part.reshape(KZ, 8, ROWS * C)


def y_to_message(q_ref, dy_ref, o_ref, msg_ref):
    table = dy_ref[...]
    for kz in range(KZ):
        both = nn(table, q_ref[kz].astype(bf16))
        o_ref[kz] = both[: 2 * KY] + both[2 * KY :]
    for ri in range(2):
        for x in range(ROWS):
            row = jnp.concatenate(
                [
                    o_ref[kz, ri * KY : (ri + 1) * KY, x * C : (x + 1) * C]
                    for kz in range(KZ)
                ],
                axis=1,
            )
            for t in range(KZ * C // LANES):
                msg_ref[t, pl.ds(ri * ROWS + x, KY, stride=8), :] = row[
                    :, t * LANES : (t + 1) * LANES
                ]


def message_to_y(rb_ref, ey_ref, b_ref, q_ref):
    b_ref[...] = jnp.zeros_like(b_ref)
    for ri in range(2):
        for x in range(ROWS):
            row = jnp.concatenate(
                [
                    rb_ref[t, pl.ds(ri * ROWS + x, KY, stride=8), :]
                    for t in range(KZ * C // LANES)
                ],
                axis=1,
            )
            for kz in range(KZ):
                b_ref[kz, ri * KY : (ri + 1) * KY, x * C : (x + 1) * C] = row[
                    :, kz * C : (kz + 1) * C
                ]
    table = ey_ref[...]
    for kz in range(KZ):
        high, low = halves(b_ref[kz])
        q_ref[kz] = nn(table, jnp.concatenate([high, high, low], axis=0))


def z_backward(q_ref, table, block):
    part = q_ref[:, pl.ds(pl.multiple_of(block * 8, 8), 8), :]
    part = part.reshape(KZ * 8, q_ref.shape[2])
    turned = part.T[: ROWS * C].astype(bf16)
    return nn(jnp.concatenate([turned, turned], axis=1), table)


def gelu_slope(values):
    size = jnp.abs(values)
    bell = jnp.exp(values * values * -0.5)
    t = 1.0 / (1.0 + (0.3275911 * 0.7071067811865476) * size)
    poly = 0.5 * 1.061405429
    poly = poly * t + 0.5 * -1.453152027
    poly = poly * t + 0.5 * 1.421413741
    poly = poly * t + 0.5 * -0.284496736
    poly = poly * t + 0.5 * 0.254829592
    tail = poly * t * bell
    cumul = jnp.where(values >= 0.0, 1.0 - tail, tail)
    return cumul + values * bell * 0.3989422804014327


def first_kernel(x_ref, bdz_ref, dy_ref, msg_ref, q_ref, o_ref):
    table = bdz_ref[...]

    def step(block, carry):
        z_forward(cells(x_ref, block), table, q_ref, block)
        return carry

    lax.fori_loop(0, Y // GROUP, step, 0, unroll=4)
    y_to_message(q_ref, dy_ref, o_ref, msg_ref)


def middle_kernel(
    rb_ref, x_ref, go_ref, wl_ref, ey_ref, bdzs_ref, bdzg_ref, dy_ref,
    s_ref, msg_ref, gl_ref, b_ref, q2_ref, q_ref, o_ref, acc_ref,
):
    message_to_y(rb_ref, ey_ref, b_ref, q2_ref)
    synth = bdzs_ref[...]
    table = bdzg_ref[...]
    mixing = wl_ref[...]
    acc_ref[...] = jnp.zeros_like(acc_ref)

    def step(block, carry):
        values = cells(x_ref, block)
        preact = z_backward(q2_ref, synth, block) + nn(mixing, values)
        slopes = cells(go_ref, block).astype(f32) * gelu_slope(preact)
        half = slopes.astype(bf16)
        s_ref[:, :, pl.ds(pl.multiple_of(block * GROUP * Z, GROUP * Z), GROUP * Z)] = half.reshape(
            ROWS, C, GROUP * Z
        )
        z_forward(half, table, q_ref, block)
        acc_ref[...] += nt(values, half)
        return carry

    lax.fori_loop(0, Y // GROUP, step, 0)
    gl_ref[...] = jnp.zeros_like(gl_ref)
    total = acc_ref[0:C, 0:C]
    for x in range(1, ROWS):
        total = total + acc_ref[x * C : (x + 1) * C, x * C : (x + 1) * C]
    gl_ref[:, :, 0:C] = total.reshape(C // 8, 8, C)
    y_to_message(q_ref, dy_ref, o_ref, msg_ref)


def last_kernel(rb_ref, s_ref, wl_ref, ey_ref, bdzs_ref, out_ref, b_ref, q2_ref):
    message_to_y(rb_ref, ey_ref, b_ref, q2_ref)
    synth = bdzs_ref[...]
    mixing = wl_ref[...]

    def step(block, carry):
        values = cells(s_ref, block)
        total = z_backward(q2_ref, synth, block) + nn(mixing, values)
        out_ref[:, :, pl.ds(pl.multiple_of(block * GROUP * Z, GROUP * Z), GROUP * Z)] = (
            total.astype(bf16).reshape(ROWS, C, GROUP * Z)
        )
        return carry

    lax.fori_loop(0, Y // GROUP, step, 0, unroll=2)


def others(axis, count, body):
    me = lax.axis_index(axis)

    def step(k, carry):
        body(lax.rem(me + k, count))
        return carry

    lax.fori_loop(1, count, step, 0)


def enter(n, d):
    barrier = pltpu.get_barrier_semaphore()
    for axis, count in (("pencil", n), ("dp", d)):
        others(
            axis,
            count,
            lambda j, axis=axis: pl.semaphore_signal(
                barrier, inc=1, device_id={axis: j}, device_id_type=MESH
            ),
        )
    return barrier


def remote(src, dst, sems, kind, mine, axis, j):
    return pltpu.make_async_remote_copy(
        src_ref=src,
        dst_ref=dst,
        send_sem=sems.at[2 * kind, j],
        recv_sem=sems.at[2 * kind + 1, mine],
        device_id={axis: j},
        device_id_type=MESH,
    )


def waits(view, sems, kind, axis, count):
    def one(j):
        copy = pltpu.make_async_copy(view(j), view(j), sems.at[2 * kind + 1, j])
        copy.wait()

    others(axis, count, one)


def sent(view, sems, kind, axis, count):
    def one(j):
        copy = pltpu.make_async_copy(view(j), view(j), sems.at[2 * kind, j])
        copy.wait()

    others(axis, count, one)


def rows8(ref):
    return lambda j: ref.at[:, pl.ds(pl.multiple_of(j * 8, 8), 8), :]


def modes(ref):
    return lambda j: ref.at[pl.ds(pl.multiple_of(j * 2 * KX, 2 * KX), 2 * KX), :]


def swap(src, dst, sems, kind, axis, count):
    me = lax.axis_index(axis)
    others(axis, count, lambda j: remote(src(j), dst(me), sems, kind, me, axis, j).start())


def x_analyse(r_ref, dx_ref, g_ref, d):
    high, low = halves(jnp.concatenate([r_ref[t] for t in range(r_ref.shape[0])], axis=1))
    table = dx_ref[...]
    both = nn(table, high)
    spectrum = both[: 2 * KX] + both[2 * KX :] + nn(table[: 2 * KX], low)
    width = KZ * C // d
    pad = jnp.zeros((2 * KX, LANES - width), f32)
    for j in range(d):
        g_ref[j * 2 * KX : (j + 1) * 2 * KX, :] = jnp.concatenate(
            [spectrum[:, j * width : (j + 1) * width], pad], axis=1
        )


def x_synth(h_ref, ex_ref, mb_ref, d):
    width = KZ * C // d
    spectrum = jnp.concatenate(
        [h_ref[j * 2 * KX : (j + 1) * 2 * KX, 0:width] for j in range(d)], axis=1
    )
    high, low = halves(spectrum)
    rows = nn(ex_ref[...], jnp.concatenate([high, high, low], axis=0))
    for t in range(mb_ref.shape[0]):
        mb_ref[t] = rows[:, t * LANES : (t + 1) * LANES]


def pick(ref, kx, d):
    real = ref[pl.ds(kx, d, stride=2 * KX), :]
    imag = ref[pl.ds(KX + kx, d, stride=2 * KX), :]
    return real, imag


def forward_mix_kernel(
    n, d, msg_ref, dx_ref, ex_ref, wc_ref,
    rb_out, h_out,
    r_ref, g_ref, h_ref, g2_ref, h2_ref, mb_ref, rb_ref, psem, dsem,
):
    me, sample = lax.axis_index("pencil"), lax.axis_index("dp")
    barrier = enter(n, d)
    pl.semaphore_wait(barrier, n + d - 2)
    swap(rows8(msg_ref), rows8(r_ref), psem, 0, "pencil", n)
    mine = pl.ds(pl.multiple_of(me * 8, 8), 8)
    r_ref[:, mine, :] = msg_ref[:, mine, :]
    waits(rows8(r_ref), psem, 0, "pencil", n)
    x_analyse(r_ref, dx_ref, g_ref, d)
    own = pl.ds(pl.multiple_of(sample * 2 * KX, 2 * KX), 2 * KX)
    swap(modes(g_ref), modes(h_ref), dsem, 0, "dp", d)
    h_ref[own, :] = g_ref[own, :]
    waits(modes(h_ref), dsem, 0, "dp", d)

    def mix(kx, carry):
        real, imag = pick(h_ref, kx, d)
        high, low = halves(jnp.concatenate([real, imag], axis=0))
        left = jnp.concatenate(
            [
                jnp.concatenate([high, high], axis=1),
                jnp.concatenate([low, jnp.zeros_like(low)], axis=1),
            ],
            axis=0,
        )
        both = nn(left, wc_ref[kx])
        both = both[: 2 * d] + both[2 * d :]
        g2_ref[pl.ds(kx, d, stride=2 * KX), :] = both[:d, :LANES] - both[d:, LANES:]
        g2_ref[pl.ds(KX + kx, d, stride=2 * KX), :] = both[:d, LANES:] + both[d:, :LANES]
        return carry

    lax.fori_loop(0, KX, mix, 0, unroll=4)
    swap(modes(g2_ref), modes(h2_ref), dsem, 1, "dp", d)
    h2_ref[own, :] = g2_ref[own, :]
    h_out[...] = h_ref[...]
    waits(modes(h2_ref), dsem, 1, "dp", d)
    x_synth(h2_ref, ex_ref, mb_ref, d)
    swap(rows8(mb_ref), rows8(rb_ref), psem, 1, "pencil", n)
    rb_ref[:, mine, :] = mb_ref[:, mine, :]
    sent(rows8(msg_ref), psem, 0, "pencil", n)
    sent(modes(g_ref), dsem, 0, "dp", d)
    sent(modes(g2_ref), dsem, 1, "dp", d)
    waits(rows8(rb_ref), psem, 1, "pencil", n)
    rb_out[...] = rb_ref[...]
    sent(rows8(mb_ref), psem, 1, "pencil", n)


def backward_mix_kernel(
    n, d, msg_ref, dx_ref, ex_ref, wc_ref, si_ref, gl_ref,
    rb_out, gs_out, gl_out,
    r_ref, g_ref, h_ref, g2_ref, h2_ref, mb_ref, rb_ref,
    glr_ref, glp_ref, gld_ref, glt_ref, glf_ref, psem, dsem, qsem, esem,
):
    me, sample = lax.axis_index("pencil"), lax.axis_index("dp")
    tiles = C // 8
    keeper = me < tiles
    barrier = enter(n, d)
    pl.semaphore_wait(barrier, n + d - 2)
    swap(rows8(msg_ref), rows8(r_ref), psem, 0, "pencil", n)

    def to_keeper(j):
        @pl.when(j < tiles)
        def _():
            remote(gl_ref.at[j], glr_ref.at[me], qsem, 0, me, "pencil", j).start()

    others("pencil", n, to_keeper)
    mine = pl.ds(pl.multiple_of(me * 8, 8), 8)
    r_ref[:, mine, :] = msg_ref[:, mine, :]

    @pl.when(keeper)
    def _():
        glr_ref[me] = gl_ref[me]

    waits(rows8(r_ref), psem, 0, "pencil", n)
    x_analyse(r_ref, dx_ref, g_ref, d)
    own = pl.ds(pl.multiple_of(sample * 2 * KX, 2 * KX), 2 * KX)
    swap(modes(g_ref), modes(h_ref), dsem, 0, "dp", d)

    @pl.when(keeper)
    def _():
        waits(lambda j: glr_ref.at[j], qsem, 0, "pencil", n)
        glp_ref[...] = jnp.sum(glr_ref[...], axis=0)
        others(
            "dp",
            d,
            lambda j: remote(glp_ref, gld_ref.at[sample], esem, 0, sample, "dp", j).start(),
        )
        gld_ref[sample] = glp_ref[...]

    h_ref[own, :] = g_ref[own, :]
    waits(modes(h_ref), dsem, 0, "dp", d)

    def stacked(kx):
        real, imag = pick(h_ref, kx, d)
        return halves(
            jnp.concatenate(
                [
                    jnp.concatenate([real, imag], axis=1),
                    jnp.concatenate([imag, -real], axis=1),
                ],
                axis=0,
            )
        )

    def adjoint(kx, carry):
        high, low = stacked(kx)
        both = nt(jnp.concatenate([high, low], axis=0), wc_ref[kx])
        total = both[: 2 * d, :LANES] + both[: 2 * d, LANES:] + both[2 * d :, :LANES]
        g2_ref[pl.ds(kx, d, stride=2 * KX), :] = total[:d]
        g2_ref[pl.ds(KX + kx, d, stride=2 * KX), :] = total[d:]
        return carry

    lax.fori_loop(0, KX, adjoint, 0, unroll=4)
    swap(modes(g2_ref), modes(h2_ref), dsem, 1, "dp", d)
    h2_ref[own, :] = g2_ref[own, :]
    waits(modes(h2_ref), dsem, 1, "dp", d)
    x_synth(h2_ref, ex_ref, mb_ref, d)
    swap(rows8(mb_ref), rows8(rb_ref), psem, 1, "pencil", n)
    rb_ref[:, mine, :] = mb_ref[:, mine, :]

    @pl.when(keeper)
    def _():
        waits(lambda j: gld_ref.at[j], esem, 0, "dp", d)
        glt_ref[...] = jnp.sum(gld_ref[...], axis=0)
        others(
            "pencil",
            n,
            lambda j: remote(glt_ref, glf_ref.at[me], qsem, 1, me, "pencil", j).start(),
        )
        glf_ref[me] = glt_ref[...]

    def weight_grad(kx, carry):
        high, low = stacked(kx)
        real, imag = pick(si_ref, kx, d)
        shigh, slow = halves(jnp.concatenate([real, imag], axis=0))
        product = tn(
            jnp.concatenate([shigh, slow, shigh], axis=0),
            jnp.concatenate([high, high, low], axis=0),
        )
        for ri in range(2):
            for kz in range(2):
                gs_out[ri, kz, kx] = product[
                    kz * C : (kz + 1) * C, ri * LANES + kz * C : ri * LANES + (kz + 1) * C
                ]
        return carry

    lax.fori_loop(0, KX, weight_grad, 0, unroll=2)
    sent(rows8(msg_ref), psem, 0, "pencil", n)
    sent(modes(g_ref), dsem, 0, "dp", d)
    sent(modes(g2_ref), dsem, 1, "dp", d)

    def keeper_sent(j):
        @pl.when(j < tiles)
        def _():
            pltpu.make_async_copy(gl_ref.at[j], gl_ref.at[j], qsem.at[0, j]).wait()

    others("pencil", n, keeper_sent)

    def tile_arrived(j):
        @pl.when(j < tiles)
        def _():
            pltpu.make_async_copy(glf_ref.at[j], glf_ref.at[j], qsem.at[3, j]).wait()

    others("pencil", n, tile_arrived)
    gl_out[...] = glf_ref[...]

    @pl.when(keeper)
    def _():
        sent(lambda j: glp_ref, esem, 0, "dp", d)
        sent(lambda j: glt_ref, qsem, 1, "pencil", n)

    waits(rows8(rb_ref), psem, 1, "pencil", n)
    rb_out[...] = rb_ref[...]
    sent(rows8(mb_ref), psem, 1, "pencil", n)


def vmem(count):
    return [pl.BlockSpec(memory_space=pltpu.VMEM)] * count


def call(body, shapes, scratch, arguments, name, collective=None, flops=1_000_000_000):
    extra = {}
    if collective is not None:
        extra = {"collective_id": collective, "has_side_effects": True}
    return pl.pallas_call(
        body,
        out_shape=shapes,
        in_specs=vmem(len(arguments)),
        out_specs=jax.tree.map(lambda _: pl.BlockSpec(memory_space=pltpu.VMEM), shapes),
        scratch_shapes=scratch,
        compiler_params=pltpu.CompilerParams(vmem_limit_bytes=LIMIT, **extra),
        cost_estimate=pl.CostEstimate(flops=flops, bytes_accessed=4_000_000, transcendentals=0),
        name=name,
    )(*arguments)


def stage_weights(w_spec):
    shaped = w_spec.reshape(2, 2, KX, C, C)
    high = lax.reduce_precision(shaped, 8, 7)
    parts = jnp.stack([high, shaped - high]).astype(bf16)
    pad = LANES - 2 * C
    first = jnp.pad(parts[:, :, 0], ((0, 0), (0, 0), (0, 0), (0, C + pad), (0, C + pad)))
    second = jnp.pad(parts[:, :, 1], ((0, 0), (0, 0), (0, 0), (C, pad), (C, pad)))
    both = first + second
    return both.transpose(2, 0, 3, 1, 4).reshape(KX, 2 * LANES, 2 * LANES)


def local(n, d, field_in, grad_out, w_spec, w_local):
    sds = jax.ShapeDtypeStruct
    tiles = KZ * C // LANES
    values, upstream = field_in[0], grad_out[0]
    cells_shape = values.shape
    ones = np.ones((KZ,))
    scale = z_scale()
    bdz = tall(z_table(ones))
    bdz_grad = tall(z_table(scale))
    synth = tall(z_table(scale))
    synth_plain = tall(z_table(ones))
    dy = tall(y_forward())
    ey = wide3(y_forward().T)
    dx = tall(x_forward())
    ex = wide3(x_forward().T)
    eye = jnp.eye(ROWS, dtype=bf16)
    mixing_back = jnp.kron(eye, w_local)
    mixing = jnp.kron(eye, w_local.T)
    weights = stage_weights(w_spec)

    message = sds((tiles, n * 8, LANES), f32)
    q_shape = pltpu.VMEM((KZ, Y * 2, ROWS * C), f32)
    q2_shape = pltpu.VMEM((KZ, Y * 2, 2 * LANES), f32)
    o_shape = pltpu.VMEM((KZ, 2 * KY, ROWS * C), f32)
    b_shape = pltpu.VMEM((KZ, 2 * KY, 2 * LANES), f32)
    mode_shape = pltpu.VMEM((d * 2 * KX, LANES), f32)
    message_shape = pltpu.VMEM((tiles, n * 8, LANES), f32)
    exchange = [message_shape] + [mode_shape] * 4 + [message_shape] * 2

    msg = call(first_kernel, message, [q_shape, o_shape], (values, bdz, dy), "plane_analysis")
    rb, spec_in = call(
        functools.partial(forward_mix_kernel, n, d),
        (message, sds((d * 2 * KX, LANES), f32)),
        exchange + [pltpu.SemaphoreType.DMA((4, n)), pltpu.SemaphoreType.DMA((4, d))],
        (msg, dx, ex, weights),
        "forward_modes",
        collective=0,
    )
    slopes, msg, local_terms = call(
        middle_kernel,
        (sds(cells_shape, bf16), message, sds((C // 8, 8, LANES), f32)),
        [b_shape, q2_shape, q_shape, o_shape, pltpu.VMEM((ROWS * C, ROWS * C), f32)],
        (rb, values, upstream, mixing, ey, synth, bdz_grad, dy),
        "slopes_and_analysis",
    )
    tile = pltpu.VMEM((8, LANES), f32)
    rb, grad_modes, grad_local = call(
        functools.partial(backward_mix_kernel, n, d),
        (message, sds((2, 2, KX, C, C), f32), sds((C // 8, 8, LANES), f32)),
        exchange
        + [
            pltpu.VMEM((n, 8, LANES), f32),
            tile,
            pltpu.VMEM((d, 8, LANES), f32),
            tile,
            pltpu.VMEM((C // 8, 8, LANES), f32),
            pltpu.SemaphoreType.DMA((4, n)),
            pltpu.SemaphoreType.DMA((4, d)),
            pltpu.SemaphoreType.DMA((4, n)),
            pltpu.SemaphoreType.DMA((2, d)),
        ],
        (msg, dx, ex, weights, spec_in, local_terms),
        "backward_modes",
        collective=1,
    )
    grad_in = call(
        last_kernel,
        sds(cells_shape, bf16),
        [b_shape, q2_shape],
        (rb, slopes, mixing_back, ey, synth_plain),
        "plane_synthesis",
    )
    grad_spec = grad_modes.reshape(2, 1, 2, KX, C * C)
    return grad_in[None], grad_spec, grad_local.reshape(C, LANES)[:, :C]


def solution(mesh):
    n, d = mesh.shape["pencil"], mesh.shape["dp"]
    placed = (
        P("dp", "pencil", None, None),
        P("dp", "pencil", None, None),
        P(None, "pencil", "dp", None, None),
        P(),
    )
    return jax.shard_map(
        functools.partial(local, n, d),
        mesh=mesh,
        in_specs=placed,
        out_specs=(P("dp", "pencil", None, None), P(None, "pencil", "dp", None, None), P()),
        check_vma=False,
    )
```

```python
import functools

import jax
import jax.numpy as jnp
import ml_dtypes
import numpy as np
from jax import lax
from jax.experimental import pallas as pl
from jax.experimental.pallas import tpu as pltpu
from jax.sharding import PartitionSpec as P

X = 128
Y = 128
Z = 64
C = 48
KX = 32
KY = 32
KZ = 16
ROWS = 4
GROUP = 4
LANES = 128
LIMIT = 56 * 1024 * 1024

MESH = pl.DeviceIdType.MESH
f32 = jnp.float32
bf16 = jnp.bfloat16


def split(table):
    high = table.astype(np.float32).astype(ml_dtypes.bfloat16)
    low = (table - high.astype(np.float64)).astype(np.float32).astype(ml_dtypes.bfloat16)
    return high, low


def signed(count):
    freqs = np.arange(count)
    return np.where(freqs < count // 2, freqs, freqs - count)


def forward_table(length, count):
    angles = 2.0 * np.pi * (np.outer(signed(count), np.arange(length)) % length) / length
    cos, sin = np.cos(angles), np.sin(angles)
    table = np.zeros((2, count, length, 2))
    table[0, :, :, 0] = cos
    table[0, :, :, 1] = sin
    table[1, :, :, 0] = -sin
    table[1, :, :, 1] = cos
    return table.reshape(2 * count, length, 2)


def z_table(scale):
    angles = 2.0 * np.pi * (np.outer(np.arange(KZ), np.arange(Z)) % Z) / Z
    table = np.zeros((KZ, GROUP, 2, GROUP, Z))
    for place in range(GROUP):
        table[:, place, 0, place] = np.cos(angles) * scale[:, None]
        table[:, place, 1, place] = -np.sin(angles) * scale[:, None]
    return table.reshape(KZ * GROUP * 2, GROUP * Z)


def z_scale():
    return np.where(np.arange(KZ) == 0, 1.0, 2.0) / float(X * Y * Z)


def tall(table):
    return np.concatenate(split(table), axis=0)


def wide3(table):
    high, low = split(table)
    return np.concatenate([high, low, high], axis=1)


def y_forward():
    return forward_table(Y, KY).reshape(2 * KY, Y * 2)


def x_forward():
    table = forward_table(X, KX).reshape(2 * KX, X // ROWS, ROWS, 2)
    return table.transpose(0, 1, 3, 2).reshape(2 * KX, X * 2)


def nt(left, right):
    return lax.dot_general(left, right, (((1,), (1,)), ((), ())), preferred_element_type=f32)


def tn(left, right):
    return lax.dot_general(left, right, (((0,), (0,)), ((), ())), preferred_element_type=f32)


def nn(left, right):
    return jnp.dot(left, right, preferred_element_type=f32)


def halves(values):
    high = values.astype(bf16)
    low = (values - high.astype(f32)).astype(bf16)
    return high, low


def cells(ref, block):
    return ref[:, :, pl.ds(pl.multiple_of(block * GROUP * Z, GROUP * Z), GROUP * Z)].reshape(
        ROWS * C, GROUP * Z
    )


def z_forward(values, table, q_ref, block):
    half = KZ * GROUP * 2
    both = nt(table, values)
    part = both[:half] + both[half : 2 * half]
    q_ref[:, pl.ds(pl.multiple_of(block * 8, 8), 8), :] = part.reshape(KZ, 8, ROWS * C)
    return both[2 * half :]


def y_to_message(q_ref, dy_ref, o_ref, msg_ref, h):
    table = dy_ref[...]
    span = range(h * KZ // 2, (h + 1) * KZ // 2)
    for kz in span:
        both = nn(table, q_ref[kz].astype(bf16))
        o_ref[kz] = both[: 2 * KY] + both[2 * KY :]
    first, count = chunk_tiles(h)
    for ri in range(2):
        for x in range(ROWS):
            row = jnp.concatenate(
                [o_ref[kz, ri * KY : (ri + 1) * KY, x * C : (x + 1) * C] for kz in span], axis=1
            )
            for t in range(count):
                msg_ref[first + t, pl.ds(ri * ROWS + x, KY, stride=8), :] = row[
                    :, t * LANES : (t + 1) * LANES
                ]


def message_to_y(rb_ref, ey_ref, b_ref, q_ref, h):
    first, count = chunk_tiles(h)
    span = range(h * KZ // 2, (h + 1) * KZ // 2)
    for kz in span if ROWS * C < b_ref.shape[2] else ():
        b_ref[kz, :, ROWS * C :] = jnp.zeros((2 * KY, b_ref.shape[2] - ROWS * C), f32)
    for ri in range(2):
        for x in range(ROWS):
            row = jnp.concatenate(
                [
                    rb_ref[first + t, pl.ds(ri * ROWS + x, KY, stride=8), :]
                    for t in range(count)
                ],
                axis=1,
            )
            for i, kz in enumerate(span):
                b_ref[kz, ri * KY : (ri + 1) * KY, x * C : (x + 1) * C] = row[
                    :, i * C : (i + 1) * C
                ]
    table = ey_ref[...]
    for kz in span:
        high, low = halves(b_ref[kz])
        q_ref[kz] = nn(table, jnp.concatenate([high, high, low], axis=0))


def z_backward(q_ref, table, block):
    part = q_ref[:, pl.ds(pl.multiple_of(block * 8, 8), 8), :]
    part = part.reshape(KZ * 8, q_ref.shape[2])
    turned = part.T[: ROWS * C].astype(bf16)
    return nn(jnp.concatenate([turned, turned], axis=1), table)


def chunk_tiles(h):
    count = KZ * C // LANES // 2
    return h * count, count


def gelu_slope(values):
    size = jnp.abs(values)
    bell = jnp.exp(values * values * -0.5)
    t = 1.0 / (1.0 + (0.3275911 * 0.7071067811865476) * size)
    poly = 0.5 * 1.061405429
    poly = poly * t + 0.5 * -1.453152027
    poly = poly * t + 0.5 * 1.421413741
    poly = poly * t + 0.5 * -0.284496736
    poly = poly * t + 0.5 * 0.254829592
    tail = poly * t * bell
    cumul = jnp.where(values >= 0.0, 1.0 - tail, tail)
    return cumul + values * bell * 0.3989422804014327


def last_kernel(rb_ref, s_ref, wl_ref, ey_ref, bdzs_ref, out_ref, b_ref, q2_ref):
    for h in range(2):
        message_to_y(rb_ref, ey_ref, b_ref, q2_ref, h)
    synth = bdzs_ref[...]
    mixing = wl_ref[...]

    def step(block, carry):
        values = cells(s_ref, block)
        total = z_backward(q2_ref, synth, block) + nn(mixing, values)
        out_ref[:, :, pl.ds(pl.multiple_of(block * GROUP * Z, GROUP * Z), GROUP * Z)] = (
            total.astype(bf16).reshape(ROWS, C, GROUP * Z)
        )
        return carry

    lax.fori_loop(0, Y // GROUP, step, 0, unroll=2)


def others(axis, count, body):
    me = lax.axis_index(axis)

    def step(k, carry):
        body(lax.rem(me + k, count))
        return carry

    lax.fori_loop(1, count, step, 0)


def enter(n, d):
    barrier = pltpu.get_barrier_semaphore()
    for axis, count in (("pencil", n), ("dp", d)):
        others(
            axis,
            count,
            lambda j, axis=axis: pl.semaphore_signal(
                barrier, inc=1, device_id={axis: j}, device_id_type=MESH
            ),
        )
    return barrier


def remote(src, dst, sems, kind, mine, axis, j):
    return pltpu.make_async_remote_copy(
        src_ref=src,
        dst_ref=dst,
        send_sem=sems.at[2 * kind, j],
        recv_sem=sems.at[2 * kind + 1, mine],
        device_id={axis: j},
        device_id_type=MESH,
    )


def wait_one(view, sem):
    pltpu.make_async_copy(view, view, sem).wait()


def arrived(view, sems, kind, axis, count):
    others(axis, count, lambda j: wait_one(view(j), sems.at[2 * kind + 1, j]))


def sent(view, sems, kind, axis, count):
    others(axis, count, lambda j: wait_one(view(j), sems.at[2 * kind, j]))


def piece(ref, h):
    first, count = chunk_tiles(h)
    return lambda j: ref.at[pl.ds(first, count), pl.ds(pl.multiple_of(j * 8, 8), 8), :]


def modes(ref):
    return lambda j: ref.at[pl.ds(pl.multiple_of(j * 2 * KX, 2 * KX), 2 * KX), :]


def swap(src, dst, sems, kind, axis, count):
    me = lax.axis_index(axis)
    others(axis, count, lambda j: remote(src(j), dst(me), sems, kind, me, axis, j).start())


def send_chunk(n, src_ref, dst_ref, sems, kind, h):
    me = lax.axis_index("pencil")
    swap(piece(src_ref, h), piece(dst_ref, h), sems, kind, "pencil", n)
    first, count = chunk_tiles(h)
    mine = pl.ds(pl.multiple_of(me * 8, 8), 8)
    dst_ref[first : first + count, mine, :] = src_ref[first : first + count, mine, :]


def x_analyse(r_ref, dx_ref, g_ref, d, h):
    first, count = chunk_tiles(h)
    high, low = halves(jnp.concatenate([r_ref[first + t] for t in range(count)], axis=1))
    table = dx_ref[...]
    both = nn(table, high)
    spectrum = both[: 2 * KX] + both[2 * KX :] + nn(table[: 2 * KX], low)
    width = KZ * C // d
    for i in range(d // 2):
        j = h * d // 2 + i
        part = spectrum[:, i * width : (i + 1) * width]
        if width < LANES:
            part = jnp.concatenate([part, jnp.zeros((2 * KX, LANES - width), f32)], axis=1)
        g_ref[j * 2 * KX : (j + 1) * 2 * KX, :] = part


def x_synth(h_ref, ex_ref, mb_ref, d, h):
    width = KZ * C // d
    spectrum = jnp.concatenate(
        [
            h_ref[j * 2 * KX : (j + 1) * 2 * KX, 0:width]
            for j in range(h * d // 2, (h + 1) * d // 2)
        ],
        axis=1,
    )
    high, low = halves(spectrum)
    rows = nn(ex_ref[...], jnp.concatenate([high, high, low], axis=0))
    first, count = chunk_tiles(h)
    for t in range(count):
        mb_ref[first + t] = rows[:, t * LANES : (t + 1) * LANES]


def pick(ref, kx, d):
    real = ref[pl.ds(kx, d, stride=2 * KX), :]
    imag = ref[pl.ds(KX + kx, d, stride=2 * KX), :]
    return real, imag


def stage_weights(w_ref, w5_ref, wc_ref):
    for ri in range(2):
        for kz in range(2):
            for c in range(C):
                part = w_ref[ri, 0, kz, :, c * C : (c + 1) * C]
                parts = [part]
                if kz:
                    parts = [jnp.zeros((KX, C), f32), part]
                rest = LANES - C * len(parts)
                if rest:
                    parts = parts + [jnp.zeros((KX, rest), f32)]
                w5_ref[ri, kz, pl.ds(c, KX, stride=C), :] = jnp.concatenate(parts, axis=1)

    def pack(kx, carry):
        rows = pl.ds(pl.multiple_of(kx * C, 8), C)
        for ri in range(2):
            parts = [w5_ref[ri, 0, rows, :], w5_ref[ri, 1, rows, :]]
            if LANES > 2 * C:
                parts.append(jnp.zeros((LANES - 2 * C, LANES), f32))
            high, low = halves(jnp.concatenate(parts, axis=0))
            wc_ref[kx, 0:LANES, ri * LANES : (ri + 1) * LANES] = high
            wc_ref[kx, LANES : 2 * LANES, ri * LANES : (ri + 1) * LANES] = low
        return carry

    lax.fori_loop(0, KX, pack, 0)


def mix_modes(h_ref, wc_ref, g2_ref, d):
    def mix(kx, carry):
        real, imag = pick(h_ref, kx, d)
        high, low = halves(jnp.concatenate([real, imag], axis=0))
        left = jnp.concatenate(
            [
                jnp.concatenate([high, high], axis=1),
                jnp.concatenate([low, jnp.zeros_like(low)], axis=1),
            ],
            axis=0,
        )
        both = nn(left, wc_ref[kx])
        both = both[: 2 * d] + both[2 * d :]
        g2_ref[pl.ds(kx, d, stride=2 * KX), :] = both[:d, :LANES] - both[d:, LANES:]
        g2_ref[pl.ds(KX + kx, d, stride=2 * KX), :] = both[:d, LANES:] + both[d:, :LANES]
        return carry

    lax.fori_loop(0, KX, mix, 0, unroll=4)


def stacked(h_ref, kx, d):
    real, imag = pick(h_ref, kx, d)
    return halves(
        jnp.concatenate(
            [
                jnp.concatenate([real, imag], axis=1),
                jnp.concatenate([imag, -real], axis=1),
            ],
            axis=0,
        )
    )


def adjoint_modes(h_ref, wc_ref, g2_ref, d):
    def adjoint(kx, carry):
        high, low = stacked(h_ref, kx, d)
        both = nt(jnp.concatenate([high, low], axis=0), wc_ref[kx])
        total = both[: 2 * d, :LANES] + both[: 2 * d, LANES:] + both[2 * d :, :LANES]
        g2_ref[pl.ds(kx, d, stride=2 * KX), :] = total[:d]
        g2_ref[pl.ds(KX + kx, d, stride=2 * KX), :] = total[d:]
        return carry

    lax.fori_loop(0, KX, adjoint, 0, unroll=4)


def weight_grad(spec_ref, grad_ref, w5_ref, out_ref, d):
    def one(kx, carry):
        high, low = stacked(grad_ref, kx, d)
        real, imag = pick(spec_ref, kx, d)
        shigh, slow = halves(jnp.concatenate([real, imag], axis=0))
        product = tn(
            jnp.concatenate([shigh, slow, shigh], axis=0),
            jnp.concatenate([high, high, low], axis=0),
        )
        rows = pl.ds(pl.multiple_of(kx * C, 8), C)
        for ri in range(2):
            for kz in range(2):
                w5_ref[ri, kz, rows, :] = product[
                    kz * C : (kz + 1) * C, ri * LANES : (ri + 1) * LANES
                ]
        return carry

    lax.fori_loop(0, KX, one, 0, unroll=2)
    group = 8
    for ri in range(2):
        for kz in range(2):
            for first in range(0, C, group):
                out_ref[ri, 0, kz, :, first * C : (first + group) * C] = jnp.concatenate(
                    [
                        w5_ref[ri, kz, pl.ds(c, KX, stride=C), :][:, kz * C : (kz + 1) * C]
                        for c in range(first, first + group)
                    ],
                    axis=1,
                )


def mode_round(n, d, bufs, tables, psem, dsem, base, between, mixer, extra):
    r_ref, g_ref, h_ref, g2_ref, h2_ref, mb_ref, rb_ref = bufs
    dx_ref, ex_ref = tables
    sample = lax.axis_index("dp")
    half = d // 2
    own = pl.ds(pl.multiple_of(sample * 2 * KX, 2 * KX), 2 * KX)
    between()
    for h in range(2):
        arrived(piece(r_ref, h), psem, base + h, "pencil", n)
        x_analyse(r_ref, dx_ref, g_ref, d, h)

        def to_owner(j, h=h):
            @pl.when(j // half == h)
            def _():
                remote(
                    modes(g_ref)(j), modes(h_ref)(sample), dsem, base // 2, sample, "dp", j
                ).start()

        others("dp", d, to_owner)

        @pl.when(sample // half == h)
        def _():
            h_ref[own, :] = g_ref[own, :]
            arrived(modes(h_ref), dsem, base // 2, "dp", d)
            mixer(h_ref, g2_ref)
            swap(modes(g2_ref), modes(h2_ref), dsem, base // 2 + 1, "dp", d)
            h2_ref[own, :] = g2_ref[own, :]

        if h:
            extra()
    for h in range(2):

        def from_owner(j, h=h):
            @pl.when(j // half == h)
            def _():
                wait_one(modes(h2_ref)(j), dsem.at[2 * (base // 2 + 1) + 1, j])

        others("dp", d, from_owner)
        x_synth(h2_ref, ex_ref, mb_ref, d, h)
        send_chunk(n, mb_ref, rb_ref, psem, base + 2 + h, h)


def main_kernel(
    n, d,
    x_hbm, go_hbm, w_hbm, wl_ref, bdz_ref, bdzs_ref, bdzg_ref, dy_ref, ey_ref, dx_ref, ex_ref,
    s_hbm, rb_out, gs_out, gl_out,
    x_ref, go_ref, s_ref, w_ref, w5_ref, wc_ref, q_ref, q2_ref, o_ref, b_ref, acc_ref,
    msg1_ref, r1_ref, g1_ref, h1_ref, g21_ref, h21_ref, mb1_ref, rb1_ref,
    msg2_ref, r2_ref, g2_ref, h2_ref, g22_ref, h22_ref, mb2_ref, rb2_ref,
    gl_ref, glr_ref, glp_ref, gld_ref, glt_ref, glf_ref,
    psem, dsem, qsem, esem, load_sem,
):
    me, sample = lax.axis_index("pencil"), lax.axis_index("dp")
    tiles = C // 8
    keeper = me < tiles
    blocks = Y // GROUP
    parts = 4
    width = Y * Z // parts
    barrier = enter(n, d)
    loads = []
    for i in range(parts):
        view = (slice(None), slice(None), pl.ds(i * width, width))
        loads.append(
            pltpu.make_async_copy(x_hbm.at[view], x_ref.at[view], load_sem.at[i])
        )
    loads.append(pltpu.make_async_copy(w_hbm, w_ref, load_sem.at[parts]))
    loads.append(pltpu.make_async_copy(go_hbm, go_ref, load_sem.at[parts + 1]))
    for load in loads:
        load.start()
    table = bdz_ref[...]

    def analyse(block, carry):
        z_forward(cells(x_ref, block), table, q_ref, block)
        return carry

    for i in range(parts):
        loads[i].wait()
        lax.fori_loop(i * blocks // parts, (i + 1) * blocks // parts, analyse, 0, unroll=4)
    for h in range(2):
        y_to_message(q_ref, dy_ref, o_ref, msg1_ref, h)
        if h == 0:
            pl.semaphore_wait(barrier, n + d - 2)
        send_chunk(n, msg1_ref, r1_ref, psem, h, h)

    def stage():
        loads[parts].wait()
        stage_weights(w_ref, w5_ref, wc_ref)

    mode_round(
        n, d,
        (r1_ref, g1_ref, h1_ref, g21_ref, h21_ref, mb1_ref, rb1_ref),
        (dx_ref, ex_ref), psem, dsem, 0, stage,
        lambda src, dst: mix_modes(src, wc_ref, dst, d),
        lambda: None,
    )
    acc_ref[...] = jnp.zeros_like(acc_ref)
    loads[parts + 1].wait()
    for h in range(2):
        arrived(piece(rb1_ref, h), psem, 2 + h, "pencil", n)
        message_to_y(rb1_ref, ey_ref, b_ref, q2_ref, h)
    synth = bdzs_ref[...]
    grad_table = bdzg_ref[...]
    mixing = wl_ref[...]

    def slopes(block, carry):
        values = cells(x_ref, block)
        preact = z_backward(q2_ref, synth, block) + nn(mixing, values)
        half = (cells(go_ref, block).astype(f32) * gelu_slope(preact)).astype(bf16)
        s_ref[:, :, pl.ds(pl.multiple_of(block * GROUP * Z, GROUP * Z), GROUP * Z)] = half.reshape(
            ROWS, C, GROUP * Z
        )
        acc_ref[...] += z_forward(
            half, jnp.concatenate([grad_table, values], axis=0), q_ref, block
        )
        return carry

    lax.fori_loop(0, blocks, slopes, 0)
    for h in range(2):
        y_to_message(q_ref, dy_ref, o_ref, msg2_ref, h)
        send_chunk(n, msg2_ref, r2_ref, psem, 4 + h, h)
    store = pltpu.make_async_copy(s_ref, s_hbm, load_sem.at[0])
    store.start()

    def local_sum():
        gl_ref[...] = jnp.zeros_like(gl_ref)
        total = acc_ref[0:C, 0:C]
        for x in range(1, ROWS):
            total = total + acc_ref[x * C : (x + 1) * C, x * C : (x + 1) * C]
        gl_ref[:, :, 0:C] = total.reshape(tiles, 8, C)

        def to_keeper(j):
            @pl.when(j < tiles)
            def _():
                remote(gl_ref.at[j], glr_ref.at[me], qsem, 0, me, "pencil", j).start()

        others("pencil", n, to_keeper)

        @pl.when(keeper)
        def _():
            glr_ref[me] = gl_ref[me]
            arrived(lambda j: glr_ref.at[j], qsem, 0, "pencil", n)
            glp_ref[...] = jnp.sum(glr_ref[...], axis=0)
            others(
                "dp",
                d,
                lambda j: remote(glp_ref, gld_ref.at[sample], esem, 0, sample, "dp", j).start(),
            )
            gld_ref[sample] = glp_ref[...]

    def local_spread():
        @pl.when(keeper)
        def _():
            arrived(lambda j: gld_ref.at[j], esem, 0, "dp", d)
            glt_ref[...] = jnp.sum(gld_ref[...], axis=0)
            others(
                "pencil",
                n,
                lambda j: remote(glt_ref, glf_ref.at[me], qsem, 1, me, "pencil", j).start(),
            )
            glf_ref[me] = glt_ref[...]

    mode_round(
        n, d,
        (r2_ref, g2_ref, h2_ref, g22_ref, h22_ref, mb2_ref, rb2_ref),
        (dx_ref, ex_ref), psem, dsem, 4, local_sum,
        lambda src, dst: adjoint_modes(src, wc_ref, dst, d),
        local_spread,
    )
    weight_grad(h1_ref, h2_ref, w5_ref, gs_out, d)
    for base, (first, modes1, modes2, second) in (
        (0, (msg1_ref, g1_ref, g21_ref, mb1_ref)),
        (4, (msg2_ref, g2_ref, g22_ref, mb2_ref)),
    ):
        for h in range(2):
            sent(piece(first, h), psem, base + h, "pencil", n)
            sent(piece(second, h), psem, base + 2 + h, "pencil", n)
        sent(modes(modes1), dsem, base // 2, "dp", d)
        sent(modes(modes2), dsem, base // 2 + 1, "dp", d)

    def keeper_sent(j):
        @pl.when(j < tiles)
        def _():
            wait_one(gl_ref.at[j], qsem.at[0, j])
            wait_one(glf_ref.at[j], qsem.at[3, j])

    others("pencil", n, keeper_sent)
    gl_out[...] = glf_ref[...]

    @pl.when(keeper)
    def _():
        sent(lambda j: glp_ref, esem, 0, "dp", d)
        sent(lambda j: glt_ref, qsem, 1, "pencil", n)

    store.wait()
    for h in range(2):
        arrived(piece(rb2_ref, h), psem, 6 + h, "pencil", n)
    rb_out[...] = rb2_ref[...]


def call(body, shapes, scratch, arguments, name, places=None, outs=None, collective=None):
    extra = {}
    if collective is not None:
        extra = {"collective_id": collective, "has_side_effects": True}
    vmem = pl.BlockSpec(memory_space=pltpu.VMEM)
    return pl.pallas_call(
        body,
        out_shape=shapes,
        in_specs=places or [vmem] * len(arguments),
        out_specs=outs or jax.tree.map(lambda _: vmem, shapes),
        scratch_shapes=scratch,
        compiler_params=pltpu.CompilerParams(vmem_limit_bytes=LIMIT, **extra),
        cost_estimate=pl.CostEstimate(
            flops=1_000_000_000, bytes_accessed=4_000_000, transcendentals=0
        ),
        name=name,
    )(*arguments)


def local(n, d, field_in, grad_out, w_spec, w_local):
    sds = jax.ShapeDtypeStruct
    lane_tiles = KZ * C // LANES
    values, upstream = field_in[0], grad_out[0]
    cells_shape = values.shape
    ones = np.ones((KZ,))
    scale = z_scale()
    bdz = tall(z_table(ones))
    bdz_grad = tall(z_table(scale))
    synth = tall(z_table(scale))
    synth_plain = tall(z_table(ones))
    dy = tall(y_forward())
    ey = wide3(y_forward().T)
    dx = tall(x_forward())
    ex = wide3(x_forward().T)
    eye = jnp.eye(ROWS, dtype=bf16)
    mixing_back = jnp.kron(eye, w_local)
    mixing = jnp.kron(eye, w_local.T)

    message = sds((lane_tiles, n * 8, LANES), f32)
    q_shape = pltpu.VMEM((KZ, Y * 2, ROWS * C), f32)
    q2_shape = pltpu.VMEM((KZ, Y * 2, 2 * LANES), f32)
    o_shape = pltpu.VMEM((KZ, 2 * KY, ROWS * C), f32)
    b_shape = pltpu.VMEM((KZ, 2 * KY, 2 * LANES), f32)
    mode_shape = pltpu.VMEM((d * 2 * KX, LANES), f32)
    message_shape = pltpu.VMEM((lane_tiles, n * 8, LANES), f32)
    exchange = [message_shape] * 2 + [mode_shape] * 4 + [message_shape] * 2
    tile = pltpu.VMEM((8, LANES), f32)
    tile_count = C // 8
    anywhere = pl.BlockSpec(memory_space=pl.ANY)
    vmem = pl.BlockSpec(memory_space=pltpu.VMEM)
    slopes, rb, grad_spec, grad_local = call(
        functools.partial(main_kernel, n, d),
        (
            sds(cells_shape, bf16),
            message,
            sds(w_spec.shape, f32),
            sds((tile_count, 8, LANES), f32),
        ),
        [
            pltpu.VMEM(cells_shape, bf16),
            pltpu.VMEM(cells_shape, bf16),
            pltpu.VMEM(cells_shape, bf16),
            pltpu.VMEM(w_spec.shape, f32),
            pltpu.VMEM((2, 2, KX * C, LANES), f32),
            pltpu.VMEM((KX, 2 * LANES, 2 * LANES), bf16),
            q_shape,
            q2_shape,
            o_shape,
            b_shape,
            pltpu.VMEM((ROWS * C, ROWS * C), f32),
        ]
        + exchange * 2
        + [
            pltpu.VMEM((tile_count, 8, LANES), f32),
            pltpu.VMEM((n, 8, LANES), f32),
            tile,
            pltpu.VMEM((d, 8, LANES), f32),
            tile,
            pltpu.VMEM((tile_count, 8, LANES), f32),
            pltpu.SemaphoreType.DMA((16, n)),
            pltpu.SemaphoreType.DMA((8, d)),
            pltpu.SemaphoreType.DMA((4, n)),
            pltpu.SemaphoreType.DMA((2, d)),
            pltpu.SemaphoreType.DMA((6,)),
        ],
        (values, upstream, w_spec, mixing, bdz, synth, bdz_grad, dy, ey, dx, ex),
        "spectral_backward",
        places=[anywhere] * 3 + [vmem] * 8,
        outs=(anywhere, vmem, vmem, vmem),
        collective=0,
    )
    grad_in = call(
        last_kernel,
        sds(cells_shape, bf16),
        [b_shape, q2_shape],
        (rb, slopes, mixing_back, ey, synth_plain),
        "plane_synthesis",
    )
    return grad_in[None], grad_spec, grad_local.reshape(C, LANES)[:, :C]


def solution(mesh):
    n, d = mesh.shape["pencil"], mesh.shape["dp"]
    placed = (
        P("dp", "pencil", None, None),
        P("dp", "pencil", None, None),
        P(None, "pencil", "dp", None, None),
        P(),
    )
    return jax.shard_map(
        functools.partial(local, n, d),
        mesh=mesh,
        in_specs=placed,
        out_specs=(P("dp", "pencil", None, None), P(None, "pencil", "dp", None, None), P()),
        check_vma=False,
    )
```

```python
import functools

import jax
import jax.numpy as jnp
import ml_dtypes
import numpy as np
from jax import lax
from jax.experimental import pallas as pl
from jax.experimental.pallas import tpu as pltpu
from jax.sharding import PartitionSpec as P

X = 128
Y = 128
Z = 64
C = 48
KX = 32
KY = 32
KZ = 16
ROWS = 4
GROUP = 4
LANES = 128
LIMIT = 56 * 1024 * 1024

MESH = pl.DeviceIdType.MESH
f32 = jnp.float32
bf16 = jnp.bfloat16


def split(table):
    high = table.astype(np.float32).astype(ml_dtypes.bfloat16)
    low = (table - high.astype(np.float64)).astype(np.float32).astype(ml_dtypes.bfloat16)
    return high, low


def signed(count):
    freqs = np.arange(count)
    return np.where(freqs < count // 2, freqs, freqs - count)


def forward_table(length, count):
    angles = 2.0 * np.pi * (np.outer(signed(count), np.arange(length)) % length) / length
    cos, sin = np.cos(angles), np.sin(angles)
    table = np.zeros((2, count, length, 2))
    table[0, :, :, 0] = cos
    table[0, :, :, 1] = sin
    table[1, :, :, 0] = -sin
    table[1, :, :, 1] = cos
    return table.reshape(2 * count, length, 2)


def half_of(sample, d):
    return (sample // max(d // 4, 1)) % 2


def owner_order(d):
    return sorted(range(d), key=lambda j: (half_of(j, d), j))


def kz_order(d):
    return np.array([2 * j + k for j in owner_order(d) for k in range(2)])


def z_table(scale, d):
    order = kz_order(d)
    scale = scale[order]
    angles = 2.0 * np.pi * (np.outer(order, np.arange(Z)) % Z) / Z
    table = np.zeros((KZ, GROUP, 2, GROUP, Z))
    for place in range(GROUP):
        table[:, place, 0, place] = np.cos(angles) * scale[:, None]
        table[:, place, 1, place] = -np.sin(angles) * scale[:, None]
    return table.reshape(KZ * GROUP * 2, GROUP * Z)


def z_scale():
    return np.where(np.arange(KZ) == 0, 1.0, 2.0) / float(X * Y * Z)


def tall(table):
    return np.concatenate(split(table), axis=0)


def by_half(table):
    rows = table.shape[0] // 2
    return np.stack([tall(table[:rows]), tall(table[rows:])])


def wide3(table):
    high, low = split(table)
    return np.concatenate([high, low, high], axis=1)


def y_forward():
    return forward_table(Y, KY).reshape(2 * KY, Y * 2)


def x_forward():
    table = forward_table(X, KX).reshape(2 * KX, X // ROWS, ROWS, 2)
    return table.transpose(0, 1, 3, 2).reshape(2 * KX, X * 2)


def nt(left, right):
    return lax.dot_general(left, right, (((1,), (1,)), ((), ())), preferred_element_type=f32)


def tn(left, right):
    return lax.dot_general(left, right, (((0,), (0,)), ((), ())), preferred_element_type=f32)


def nn(left, right):
    return jnp.dot(left, right, preferred_element_type=f32)


def halves(values):
    high = values.astype(bf16)
    low = (values - high.astype(f32)).astype(bf16)
    return high, low


def cells(ref, block):
    return ref[:, :, pl.ds(pl.multiple_of(block * GROUP * Z, GROUP * Z), GROUP * Z)].reshape(
        ROWS * C, GROUP * Z
    )


def z_forward(values, table, q_ref, block, h):
    rows = KZ * GROUP
    both = nt(table, values)
    part = both[:rows] + both[rows:]
    q_ref[h * KZ // 2 : (h + 1) * KZ // 2, pl.ds(pl.multiple_of(block * 8, 8), 8), :] = (
        part.reshape(KZ // 2, 8, ROWS * C)
    )


def y_to_message(q_ref, dy_ref, o_ref, msg_ref, h):
    table = dy_ref[...]
    span = range(h * KZ // 2, (h + 1) * KZ // 2)
    for kz in span:
        both = nn(table, q_ref[kz].astype(bf16))
        o_ref[kz] = both[: 2 * KY] + both[2 * KY :]
    first, count = chunk_tiles(h)
    for ri in range(2):
        for x in range(ROWS):
            row = jnp.concatenate(
                [o_ref[kz, ri * KY : (ri + 1) * KY, x * C : (x + 1) * C] for kz in span], axis=1
            )
            for t in range(count):
                msg_ref[first + t, pl.ds(ri * ROWS + x, KY, stride=8), :] = row[
                    :, t * LANES : (t + 1) * LANES
                ]


def message_to_y(rb_ref, ey_ref, b_ref, q_ref, h):
    first, count = chunk_tiles(h)
    span = range(h * KZ // 2, (h + 1) * KZ // 2)
    for kz in span if ROWS * C < b_ref.shape[2] else ():
        b_ref[kz, :, ROWS * C :] = jnp.zeros((2 * KY, b_ref.shape[2] - ROWS * C), f32)
    for ri in range(2):
        for x in range(ROWS):
            row = jnp.concatenate(
                [
                    rb_ref[first + t, pl.ds(ri * ROWS + x, KY, stride=8), :]
                    for t in range(count)
                ],
                axis=1,
            )
            for i, kz in enumerate(span):
                b_ref[kz, ri * KY : (ri + 1) * KY, x * C : (x + 1) * C] = row[
                    :, i * C : (i + 1) * C
                ]
    table = ey_ref[...]
    for kz in span:
        high, low = halves(b_ref[kz])
        q_ref[kz] = nn(table, jnp.concatenate([high, high, low], axis=0))


def z_backward(q_ref, table, block):
    part = q_ref[:, pl.ds(pl.multiple_of(block * 8, 8), 8), :]
    part = part.reshape(KZ * 8, q_ref.shape[2])
    turned = part.T[: ROWS * C].astype(bf16)
    return nn(jnp.concatenate([turned, turned], axis=1), table)


def chunk_tiles(h):
    count = KZ * C // LANES // 2
    return h * count, count


def gelu_slope(values):
    size = jnp.abs(values)
    bell = jnp.exp(values * values * -0.5)
    t = 1.0 / (1.0 + (0.3275911 * 0.7071067811865476) * size)
    poly = 0.5 * 1.061405429
    poly = poly * t + 0.5 * -1.453152027
    poly = poly * t + 0.5 * 1.421413741
    poly = poly * t + 0.5 * -0.284496736
    poly = poly * t + 0.5 * 0.254829592
    tail = poly * t * bell
    cumul = jnp.where(values >= 0.0, 1.0 - tail, tail)
    return cumul + values * bell * 0.3989422804014327


def local_matrix(weights):
    rows = []
    for x in range(ROWS):
        parts = [weights]
        if x:
            parts = [jnp.zeros((C, x * C), f32)] + parts
        if x < ROWS - 1:
            parts = parts + [jnp.zeros((C, (ROWS - 1 - x) * C), f32)]
        rows.append(jnp.concatenate(parts, axis=1))
    return jnp.concatenate(rows, axis=0).astype(bf16)


def last_kernel(rb_ref, s_ref, wl_ref, ey_ref, bdzs_ref, out_ref, b_ref, q2_ref, mix_ref):
    part = pl.program_id(0)
    blocks = s_ref.shape[2] // (GROUP * Z)

    @pl.when(part == 0)
    def _():
        mix_ref[...] = local_matrix(wl_ref[...].astype(f32))
        for h in range(2):
            message_to_y(rb_ref, ey_ref, b_ref, q2_ref, h)

    synth = bdzs_ref[...]
    mixing = mix_ref[...]

    def step(block, carry):
        values = cells(s_ref, block)
        total = z_backward(q2_ref, synth, part * blocks + block) + nn(mixing, values)
        out_ref[:, :, pl.ds(pl.multiple_of(block * GROUP * Z, GROUP * Z), GROUP * Z)] = (
            total.astype(bf16).reshape(ROWS, C, GROUP * Z)
        )
        return carry

    lax.fori_loop(0, blocks, step, 0, unroll=True)


def others(axis, count, body):
    me = lax.axis_index(axis)

    def step(k, carry):
        body(lax.rem(me + k, count))
        return carry

    lax.fori_loop(1, count, step, 0)


def enter(n, d):
    barrier = pltpu.get_barrier_semaphore()
    for axis, count in (("pencil", n), ("dp", d)):
        others(
            axis,
            count,
            lambda j, axis=axis: pl.semaphore_signal(
                barrier, inc=1, device_id={axis: j}, device_id_type=MESH
            ),
        )
    return barrier


def remote(src, dst, sems, kind, mine, axis, j):
    return pltpu.make_async_remote_copy(
        src_ref=src,
        dst_ref=dst,
        send_sem=sems.at[2 * kind, j],
        recv_sem=sems.at[2 * kind + 1, mine],
        device_id={axis: j},
        device_id_type=MESH,
    )


def wait_one(view, sem):
    pltpu.make_async_copy(view, view, sem).wait()


def arrived(view, sems, kind, axis, count):
    others(axis, count, lambda j: wait_one(view(j), sems.at[2 * kind + 1, j]))


def sent(view, sems, kind, axis, count):
    others(axis, count, lambda j: wait_one(view(j), sems.at[2 * kind, j]))


def piece(ref, h):
    first, count = chunk_tiles(h)
    return lambda j: ref.at[pl.ds(first, count), pl.ds(pl.multiple_of(j * 8, 8), 8), :]


def modes(ref):
    return lambda j: ref.at[pl.ds(pl.multiple_of(j * 2 * KX, 2 * KX), 2 * KX), :]


def swap(src, dst, sems, kind, axis, count):
    me = lax.axis_index(axis)
    others(axis, count, lambda j: remote(src(j), dst(me), sems, kind, me, axis, j).start())


def send_chunk(n, src_ref, dst_ref, sems, kind, h):
    me = lax.axis_index("pencil")
    swap(piece(src_ref, h), piece(dst_ref, h), sems, kind, "pencil", n)
    first, count = chunk_tiles(h)
    mine = pl.ds(pl.multiple_of(me * 8, 8), 8)
    dst_ref[first : first + count, mine, :] = src_ref[first : first + count, mine, :]


def x_analyse(r_ref, dx_ref, g_ref, d, h):
    first, count = chunk_tiles(h)
    high, low = halves(jnp.concatenate([r_ref[first + t] for t in range(count)], axis=1))
    table = dx_ref[...]
    both = nn(table, high)
    spectrum = both[: 2 * KX] + both[2 * KX :] + nn(table[: 2 * KX], low)
    width = KZ * C // d
    for i in range(d // 2):
        j = owner_order(d)[h * d // 2 + i]
        part = spectrum[:, i * width : (i + 1) * width]
        if width < LANES:
            part = jnp.concatenate([part, jnp.zeros((2 * KX, LANES - width), f32)], axis=1)
        g_ref[j * 2 * KX : (j + 1) * 2 * KX, :] = part


def x_synth(h_ref, ex_ref, mb_ref, d, h):
    width = KZ * C // d
    spectrum = jnp.concatenate(
        [
            h_ref[j * 2 * KX : (j + 1) * 2 * KX, 0:width]
            for j in owner_order(d)[h * d // 2 : (h + 1) * d // 2]
        ],
        axis=1,
    )
    high, low = halves(spectrum)
    rows = nn(ex_ref[...], jnp.concatenate([high, high, low], axis=0))
    first, count = chunk_tiles(h)
    for t in range(count):
        mb_ref[first + t] = rows[:, t * LANES : (t + 1) * LANES]


def pick(ref, kx, d):
    real = ref[pl.ds(kx, d, stride=2 * KX), :]
    imag = ref[pl.ds(KX + kx, d, stride=2 * KX), :]
    return real, imag


def stage_weights(w_ref, w5_ref, wc_ref):
    for ri in range(2):
        for kz in range(2):
            for c in range(C):
                part = w_ref[ri, 0, kz, :, c * C : (c + 1) * C]
                parts = [part]
                if kz:
                    parts = [jnp.zeros((KX, C), f32), part]
                rest = LANES - C * len(parts)
                if rest:
                    parts = parts + [jnp.zeros((KX, rest), f32)]
                w5_ref[ri, kz, pl.ds(c, KX, stride=C), :] = jnp.concatenate(parts, axis=1)

    def pack(kx, carry):
        rows = pl.ds(pl.multiple_of(kx * C, 8), C)
        for ri in range(2):
            parts = [w5_ref[ri, 0, rows, :], w5_ref[ri, 1, rows, :]]
            if LANES > 2 * C:
                parts.append(jnp.zeros((LANES - 2 * C, LANES), f32))
            high, low = halves(jnp.concatenate(parts, axis=0))
            wc_ref[kx, 0:LANES, ri * LANES : (ri + 1) * LANES] = high
            wc_ref[kx, LANES : 2 * LANES, ri * LANES : (ri + 1) * LANES] = low
        return carry

    lax.fori_loop(0, KX, pack, 0)


def mix_modes(h_ref, wc_ref, g2_ref, d):
    def mix(kx, carry):
        real, imag = pick(h_ref, kx, d)
        high, low = halves(jnp.concatenate([real, imag], axis=0))
        left = jnp.concatenate(
            [
                jnp.concatenate([high, high], axis=1),
                jnp.concatenate([low, jnp.zeros_like(low)], axis=1),
            ],
            axis=0,
        )
        both = nn(left, wc_ref[kx])
        both = both[: 2 * d] + both[2 * d :]
        g2_ref[pl.ds(kx, d, stride=2 * KX), :] = both[:d, :LANES] - both[d:, LANES:]
        g2_ref[pl.ds(KX + kx, d, stride=2 * KX), :] = both[:d, LANES:] + both[d:, :LANES]
        return carry

    lax.fori_loop(0, KX, mix, 0, unroll=16)


def stacked(h_ref, kx, d):
    real, imag = pick(h_ref, kx, d)
    return halves(
        jnp.concatenate(
            [
                jnp.concatenate([real, imag], axis=1),
                jnp.concatenate([imag, -real], axis=1),
            ],
            axis=0,
        )
    )


def adjoint_modes(h_ref, wc_ref, g2_ref, d):
    def adjoint(kx, carry):
        high, low = stacked(h_ref, kx, d)
        both = nt(jnp.concatenate([high, low], axis=0), wc_ref[kx])
        total = both[: 2 * d, :LANES] + both[: 2 * d, LANES:] + both[2 * d :, :LANES]
        g2_ref[pl.ds(kx, d, stride=2 * KX), :] = total[:d]
        g2_ref[pl.ds(KX + kx, d, stride=2 * KX), :] = total[d:]
        return carry

    lax.fori_loop(0, KX, adjoint, 0, unroll=16)


def weight_grad(spec_ref, grad_ref, w5_ref, out_ref, d):
    def one(kx, carry):
        high, low = stacked(grad_ref, kx, d)
        real, imag = pick(spec_ref, kx, d)
        shigh, slow = halves(jnp.concatenate([real, imag], axis=0))
        product = tn(
            jnp.concatenate([shigh, slow, shigh], axis=0),
            jnp.concatenate([high, high, low], axis=0),
        )
        rows = pl.ds(pl.multiple_of(kx * C, 8), C)
        for ri in range(2):
            for kz in range(2):
                w5_ref[ri, kz, rows, :] = product[
                    kz * C : (kz + 1) * C, ri * LANES : (ri + 1) * LANES
                ]
        return carry

    lax.fori_loop(0, KX, one, 0, unroll=4)
    group = 8
    for ri in range(2):
        for kz in range(2):
            for first in range(0, C, group):
                out_ref[ri, 0, kz, :, first * C : (first + group) * C] = jnp.concatenate(
                    [
                        w5_ref[ri, kz, pl.ds(c, KX, stride=C), :][:, kz * C : (kz + 1) * C]
                        for c in range(first, first + group)
                    ],
                    axis=1,
                )


def mode_round(n, d, bufs, tables, psem, dsem, base, between, mixer, extra):
    r_ref, g_ref, h_ref, g2_ref, h2_ref, mb_ref, rb_ref = bufs
    dx_ref, ex_ref = tables
    sample = lax.axis_index("dp")
    out, back = base // 2, base // 2 + 1
    own = pl.ds(pl.multiple_of(sample * 2 * KX, 2 * KX), 2 * KX)

    def forward(h):
        arrived(piece(r_ref, h), psem, base + h, "pencil", n)
        x_analyse(r_ref, dx_ref, g_ref, d, h)

        def to_owner(j):
            @pl.when(half_of(j, d) == h)
            def _():
                remote(modes(g_ref)(j), modes(h_ref)(sample), dsem, out, sample, "dp", j).start()

        others("dp", d, to_owner)

    def mix(h):
        @pl.when(half_of(sample, d) == h)
        def _():
            h_ref[own, :] = g_ref[own, :]
            arrived(modes(h_ref), dsem, out, "dp", d)
            mixer(h_ref, g2_ref)
            swap(modes(g2_ref), modes(h2_ref), dsem, back, "dp", d)
            h2_ref[own, :] = g2_ref[own, :]

    def backward(h):
        def from_owner(j):
            @pl.when(half_of(j, d) == h)
            def _():
                wait_one(modes(h2_ref)(j), dsem.at[2 * back + 1, j])

        others("dp", d, from_owner)
        x_synth(h2_ref, ex_ref, mb_ref, d, h)
        send_chunk(n, mb_ref, rb_ref, psem, base + 2 + h, h)

    between()
    forward(0)
    mix(0)
    forward(1)
    extra()
    backward(0)
    mix(1)
    backward(1)


def main_kernel(
    n, d,
    x_hbm, go_hbm, w_hbm, wl_ref, bdz_ref, bdzs_ref, bdzg_ref, dy_ref, ey_ref, dx_ref, ex_ref,
    s_hbm, rb_out, gs_out, gl_out,
    x_ref, go_ref, s_ref, w_ref, w5_ref, wc_ref, q_ref, q2_ref, o_ref, b_ref,
    msg1_ref, r1_ref, g1_ref, h1_ref, g21_ref, h21_ref, mb1_ref, rb1_ref,
    msg2_ref, r2_ref, g2_ref, h2_ref, g22_ref, h22_ref, mb2_ref, rb2_ref,
    gl_ref, glr_ref, glp_ref, gld_ref, glt_ref, glf_ref,
    psem, dsem, qsem, esem, load_sem,
):
    me, sample = lax.axis_index("pencil"), lax.axis_index("dp")
    tiles = C // 8
    keeper = me < tiles
    blocks = Y // GROUP
    parts = 4
    width = Y * Z // parts
    barrier = enter(n, d)
    loads = []
    for i in range(parts):
        view = (slice(None), slice(None), pl.ds(i * width, width))
        loads.append(
            pltpu.make_async_copy(x_hbm.at[view], x_ref.at[view], load_sem.at[i])
        )
    loads.append(pltpu.make_async_copy(w_hbm, w_ref, load_sem.at[parts]))
    loads.append(pltpu.make_async_copy(go_hbm, go_ref, load_sem.at[parts + 1]))
    for load in loads:
        load.start()
    mixing = local_matrix(wl_ref[...].astype(f32).T)

    def analyse(values_ref, table_ref, h, first, last):
        def one(block, carry):
            z_forward(cells(values_ref, block), table_ref[h], q_ref, block, h)
            return carry

        lax.fori_loop(first, last, one, 0, unroll=8)

    for h in range(2):
        for i in range(parts):
            if h == 0:
                loads[i].wait()
            analyse(x_ref, bdz_ref, h, i * blocks // parts, (i + 1) * blocks // parts)
        y_to_message(q_ref, dy_ref, o_ref, msg1_ref, h)
        if h == 0:
            pl.semaphore_wait(barrier, n + d - 2)
        send_chunk(n, msg1_ref, r1_ref, psem, h, h)

    def stage():
        loads[parts].wait()
        stage_weights(w_ref, w5_ref, wc_ref)

    mode_round(
        n, d,
        (r1_ref, g1_ref, h1_ref, g21_ref, h21_ref, mb1_ref, rb1_ref),
        (dx_ref, ex_ref), psem, dsem, 0, stage,
        lambda src, dst: mix_modes(src, wc_ref, dst, d),
        lambda: None,
    )
    loads[parts + 1].wait()
    for h in range(2):
        arrived(piece(rb1_ref, h), psem, 2 + h, "pencil", n)
        message_to_y(rb1_ref, ey_ref, b_ref, q2_ref, h)
    synth = bdzs_ref[...]

    def slopes(block, carry):
        values = cells(x_ref, block)
        preact = z_backward(q2_ref, synth, block) + nn(mixing, values)
        half = (cells(go_ref, block).astype(f32) * gelu_slope(preact)).astype(bf16)
        s_ref[:, :, pl.ds(pl.multiple_of(block * GROUP * Z, GROUP * Z), GROUP * Z)] = half.reshape(
            ROWS, C, GROUP * Z
        )
        return carry

    lax.fori_loop(0, blocks, slopes, 0, unroll=4)
    for h in range(2):
        analyse(s_ref, bdzg_ref, h, 0, blocks)
        y_to_message(q_ref, dy_ref, o_ref, msg2_ref, h)
        send_chunk(n, msg2_ref, r2_ref, psem, 4 + h, h)
    store = pltpu.make_async_copy(s_ref, s_hbm, load_sem.at[0])
    store.start()

    def local_sum():
        gl_ref[...] = jnp.zeros_like(gl_ref)
        total = nt(x_ref[0], s_ref[0])
        for x in range(1, ROWS):
            total = total + nt(x_ref[x], s_ref[x])
        gl_ref[:, :, 0:C] = total.reshape(tiles, 8, C)

        def to_keeper(j):
            @pl.when(j < tiles)
            def _():
                remote(gl_ref.at[j], glr_ref.at[me], qsem, 0, me, "pencil", j).start()

        others("pencil", n, to_keeper)

        @pl.when(keeper)
        def _():
            glr_ref[me] = gl_ref[me]
            arrived(lambda j: glr_ref.at[j], qsem, 0, "pencil", n)
            glp_ref[...] = jnp.sum(glr_ref[...], axis=0)
            others(
                "dp",
                d,
                lambda j: remote(glp_ref, gld_ref.at[sample], esem, 0, sample, "dp", j).start(),
            )
            gld_ref[sample] = glp_ref[...]

    def local_spread():
        @pl.when(keeper)
        def _():
            arrived(lambda j: gld_ref.at[j], esem, 0, "dp", d)
            glt_ref[...] = jnp.sum(gld_ref[...], axis=0)
            others(
                "pencil",
                n,
                lambda j: remote(glt_ref, glf_ref.at[me], qsem, 1, me, "pencil", j).start(),
            )
            glf_ref[me] = glt_ref[...]

    mode_round(
        n, d,
        (r2_ref, g2_ref, h2_ref, g22_ref, h22_ref, mb2_ref, rb2_ref),
        (dx_ref, ex_ref), psem, dsem, 4, local_sum,
        lambda src, dst: adjoint_modes(src, wc_ref, dst, d),
        local_spread,
    )
    weight_grad(h1_ref, h2_ref, w5_ref, gs_out, d)
    for base, (first, modes1, modes2, second) in (
        (0, (msg1_ref, g1_ref, g21_ref, mb1_ref)),
        (4, (msg2_ref, g2_ref, g22_ref, mb2_ref)),
    ):
        for h in range(2):
            sent(piece(first, h), psem, base + h, "pencil", n)
            sent(piece(second, h), psem, base + 2 + h, "pencil", n)
        sent(modes(modes1), dsem, base // 2, "dp", d)
        sent(modes(modes2), dsem, base // 2 + 1, "dp", d)

    def keeper_sent(j):
        @pl.when(j < tiles)
        def _():
            wait_one(gl_ref.at[j], qsem.at[0, j])
            wait_one(glf_ref.at[j], qsem.at[3, j])

    others("pencil", n, keeper_sent)
    gl_out[...] = glf_ref[...].reshape(C, LANES)[:, :C]

    @pl.when(keeper)
    def _():
        sent(lambda j: glp_ref, esem, 0, "dp", d)
        sent(lambda j: glt_ref, qsem, 1, "pencil", n)

    store.wait()
    for h in range(2):
        arrived(piece(rb2_ref, h), psem, 6 + h, "pencil", n)
    rb_out[...] = rb2_ref[...]


def params(**extra):
    return {
        "compiler_params": pltpu.CompilerParams(vmem_limit_bytes=LIMIT, **extra),
        "cost_estimate": pl.CostEstimate(
            flops=1_000_000_000, bytes_accessed=4_000_000, transcendentals=0
        ),
    }


def local(n, d, field_in, grad_out, w_spec, w_local):
    sds = jax.ShapeDtypeStruct
    lane_tiles = KZ * C // LANES
    values, upstream = field_in[0], grad_out[0]
    cells_shape = values.shape
    ones = np.ones((KZ,))
    scale = z_scale()
    bdz = by_half(z_table(ones, d))
    bdz_grad = by_half(z_table(scale, d))
    synth = tall(z_table(scale, d))
    synth_plain = tall(z_table(ones, d))
    dy = tall(y_forward())
    ey = wide3(y_forward().T)
    dx = tall(x_forward())
    ex = wide3(x_forward().T)

    message = sds((lane_tiles, n * 8, LANES), f32)
    q_shape = pltpu.VMEM((KZ, Y * 2, ROWS * C), f32)
    q2_shape = pltpu.VMEM((KZ, Y * 2, 2 * LANES), f32)
    o_shape = pltpu.VMEM((KZ, 2 * KY, ROWS * C), f32)
    b_shape = pltpu.VMEM((KZ, 2 * KY, 2 * LANES), f32)
    mode_shape = pltpu.VMEM((d * 2 * KX, LANES), f32)
    message_shape = pltpu.VMEM((lane_tiles, n * 8, LANES), f32)
    exchange = [message_shape] * 2 + [mode_shape] * 4 + [message_shape] * 2
    tile = pltpu.VMEM((8, LANES), f32)
    tile_count = C // 8
    anywhere = pl.BlockSpec(memory_space=pl.ANY)
    vmem = pl.BlockSpec(memory_space=pltpu.VMEM)
    slopes, rb, grad_spec, grad_local = pl.pallas_call(
        functools.partial(main_kernel, n, d),
        out_shape=(
            sds(cells_shape, bf16),
            message,
            sds(w_spec.shape, f32),
            sds((C, C), f32),
        ),
        in_specs=[anywhere] * 3 + [vmem] * 8,
        out_specs=(anywhere, vmem, vmem, vmem),
        scratch_shapes=[
            pltpu.VMEM(cells_shape, bf16),
            pltpu.VMEM(cells_shape, bf16),
            pltpu.VMEM(cells_shape, bf16),
            pltpu.VMEM(w_spec.shape, f32),
            pltpu.VMEM((2, 2, KX * C, LANES), f32),
            pltpu.VMEM((KX, 2 * LANES, 2 * LANES), bf16),
            q_shape,
            q2_shape,
            o_shape,
            b_shape,
        ]
        + exchange * 2
        + [
            pltpu.VMEM((tile_count, 8, LANES), f32),
            pltpu.VMEM((n, 8, LANES), f32),
            tile,
            pltpu.VMEM((d, 8, LANES), f32),
            tile,
            pltpu.VMEM((tile_count, 8, LANES), f32),
            pltpu.SemaphoreType.DMA((16, n)),
            pltpu.SemaphoreType.DMA((8, d)),
            pltpu.SemaphoreType.DMA((4, n)),
            pltpu.SemaphoreType.DMA((2, d)),
            pltpu.SemaphoreType.DMA((6,)),
        ],
        name="spectral_backward",
        **params(collective_id=0, has_side_effects=True),
    )(values, upstream, w_spec, w_local, bdz, synth, bdz_grad, dy, ey, dx, ex)
    parts = 4
    strip = pl.BlockSpec((ROWS, C, Y * Z // parts), lambda i: (0, 0, i))
    whole = pl.BlockSpec(memory_space=pltpu.VMEM)
    grad_in = pl.pallas_call(
        last_kernel,
        out_shape=sds(cells_shape, bf16),
        grid=(parts,),
        in_specs=[whole, strip, whole, whole, whole],
        out_specs=strip,
        scratch_shapes=[b_shape, q2_shape, pltpu.VMEM((ROWS * C, ROWS * C), bf16)],
        name="plane_synthesis",
        **params(),
    )(rb, slopes, w_local, ey, synth_plain)
    return grad_in[None], grad_spec, grad_local


def solution(mesh):
    n, d = mesh.shape["pencil"], mesh.shape["dp"]
    placed = (
        P("dp", "pencil", None, None),
        P("dp", "pencil", None, None),
        P(None, "pencil", "dp", None, None),
        P(),
    )
    return jax.shard_map(
        functools.partial(local, n, d),
        mesh=mesh,
        in_specs=placed,
        out_specs=(P("dp", "pencil", None, None), P(None, "pencil", "dp", None, None), P()),
        check_vma=False,
    )
```

```python
import functools

import jax
import jax.numpy as jnp
import ml_dtypes
import numpy as np
from jax import lax
from jax.experimental import pallas as pl
from jax.experimental.pallas import tpu as pltpu
from jax.sharding import PartitionSpec as P

X = 128
Y = 128
Z = 64
C = 48
KX = 32
KY = 32
KZ = 16
ROWS = 4
GROUP = 4
LANES = 128
LIMIT = 56 * 1024 * 1024

MESH = pl.DeviceIdType.MESH
f32 = jnp.float32
bf16 = jnp.bfloat16


def split(table):
    high = table.astype(np.float32).astype(ml_dtypes.bfloat16)
    low = (table - high.astype(np.float64)).astype(np.float32).astype(ml_dtypes.bfloat16)
    return high, low


def signed(count):
    freqs = np.arange(count)
    return np.where(freqs < count // 2, freqs, freqs - count)


def forward_table(length, count):
    angles = 2.0 * np.pi * (np.outer(signed(count), np.arange(length)) % length) / length
    cos, sin = np.cos(angles), np.sin(angles)
    table = np.zeros((2, count, length, 2))
    table[0, :, :, 0] = cos
    table[0, :, :, 1] = sin
    table[1, :, :, 0] = -sin
    table[1, :, :, 1] = cos
    return table.reshape(2 * count, length, 2)


def half_of(sample, d):
    return (sample // max(d // 4, 1)) % 2


def owner_order(d):
    return sorted(range(d), key=lambda j: (half_of(j, d), j))


def kz_order(d):
    return np.array([2 * j + k for j in owner_order(d) for k in range(2)])


def z_table(scale, d):
    order = kz_order(d)
    scale = scale[order]
    angles = 2.0 * np.pi * (np.outer(order, np.arange(Z)) % Z) / Z
    table = np.zeros((KZ, GROUP, 2, GROUP, Z))
    for place in range(GROUP):
        table[:, place, 0, place] = np.cos(angles) * scale[:, None]
        table[:, place, 1, place] = -np.sin(angles) * scale[:, None]
    return table.reshape(KZ * GROUP * 2, GROUP * Z)


def z_scale():
    return np.where(np.arange(KZ) == 0, 1.0, 2.0) / float(X * Y * Z)


def tall(table):
    return np.concatenate(split(table), axis=0)


def by_half(table):
    rows = table.shape[0] // 2
    return np.stack([tall(table[:rows]), tall(table[rows:])])


def wide3(table):
    high, low = split(table)
    return np.concatenate([high, low, high], axis=1)


def y_forward():
    return forward_table(Y, KY).reshape(2 * KY, Y * 2)


def x_forward():
    table = forward_table(X, KX).reshape(2 * KX, X // ROWS, ROWS, 2)
    return table.transpose(0, 1, 3, 2).reshape(2 * KX, X * 2)


def nt(left, right):
    return lax.dot_general(left, right, (((1,), (1,)), ((), ())), preferred_element_type=f32)


def tn(left, right):
    return lax.dot_general(left, right, (((0,), (0,)), ((), ())), preferred_element_type=f32)


def nn(left, right):
    return jnp.dot(left, right, preferred_element_type=f32)


def halves(values):
    high = values.astype(bf16)
    low = (values - high.astype(f32)).astype(bf16)
    return high, low


def cells(ref, block):
    return ref[:, :, pl.ds(pl.multiple_of(block * GROUP * Z, GROUP * Z), GROUP * Z)].reshape(
        ROWS * C, GROUP * Z
    )


def z_forward(values, table, q_ref, block, h):
    rows = KZ * GROUP
    both = nt(table, values)
    part = both[:rows] + both[rows:]
    q_ref[h * KZ // 2 : (h + 1) * KZ // 2, pl.ds(pl.multiple_of(block * 8, 8), 8), :] = (
        part.reshape(KZ // 2, 8, ROWS * C)
    )


def y_to_message(q_ref, dy_ref, o_ref, msg_ref, h):
    table = dy_ref[...]
    span = range(h * KZ // 2, (h + 1) * KZ // 2)
    for kz in span:
        both = nn(table, q_ref[kz].astype(bf16))
        o_ref[kz] = both[: 2 * KY] + both[2 * KY :]
    first, count = chunk_tiles(h)
    for ri in range(2):
        for x in range(ROWS):
            row = jnp.concatenate(
                [o_ref[kz, ri * KY : (ri + 1) * KY, x * C : (x + 1) * C] for kz in span], axis=1
            )
            for t in range(count):
                msg_ref[first + t, pl.ds(ri * ROWS + x, KY, stride=8), :] = row[
                    :, t * LANES : (t + 1) * LANES
                ]


def message_to_y(rb_ref, ey_ref, b_ref, q_ref, h):
    first, count = chunk_tiles(h)
    span = range(h * KZ // 2, (h + 1) * KZ // 2)
    for kz in span if ROWS * C < b_ref.shape[2] else ():
        b_ref[kz, :, ROWS * C :] = jnp.zeros((2 * KY, b_ref.shape[2] - ROWS * C), f32)
    for ri in range(2):
        for x in range(ROWS):
            row = jnp.concatenate(
                [
                    rb_ref[first + t, pl.ds(ri * ROWS + x, KY, stride=8), :]
                    for t in range(count)
                ],
                axis=1,
            )
            for i, kz in enumerate(span):
                b_ref[kz, ri * KY : (ri + 1) * KY, x * C : (x + 1) * C] = row[
                    :, i * C : (i + 1) * C
                ]
    table = ey_ref[...]
    for kz in span:
        high, low = halves(b_ref[kz])
        q_ref[kz] = nn(table, jnp.concatenate([high, high, low], axis=0))


def z_backward(q_ref, table, block):
    part = q_ref[:, pl.ds(pl.multiple_of(block * 8, 8), 8), :]
    part = part.reshape(KZ * 8, q_ref.shape[2])
    turned = part.T[: ROWS * C].astype(bf16)
    return nn(jnp.concatenate([turned, turned], axis=1), table)


def chunk_tiles(h):
    count = KZ * C // LANES // 2
    return h * count, count


def gelu_slope(values):
    size = jnp.abs(values)
    bell = jnp.exp(values * values * -0.5)
    t = 1.0 / (1.0 + (0.3275911 * 0.7071067811865476) * size)
    poly = 0.5 * 1.061405429
    poly = poly * t + 0.5 * -1.453152027
    poly = poly * t + 0.5 * 1.421413741
    poly = poly * t + 0.5 * -0.284496736
    poly = poly * t + 0.5 * 0.254829592
    tail = poly * t * bell
    cumul = jnp.where(values >= 0.0, 1.0 - tail, tail)
    return cumul + values * bell * 0.3989422804014327


def local_matrix(weights):
    rows = []
    for x in range(ROWS):
        parts = [weights]
        if x:
            parts = [jnp.zeros((C, x * C), f32)] + parts
        if x < ROWS - 1:
            parts = parts + [jnp.zeros((C, (ROWS - 1 - x) * C), f32)]
        rows.append(jnp.concatenate(parts, axis=1))
    return jnp.concatenate(rows, axis=0).astype(bf16)


def last_kernel(
    rb_ref, s_ref, wl_ref, ey_ref, bdzs_ref, gs_ref, gl_ref,
    out_ref, gs_out, gl_out, b_ref, q2_ref, mix_ref,
):
    part = pl.program_id(0)
    gs_out[...] = gs_ref[...]
    blocks = s_ref.shape[2] // (GROUP * Z)

    @pl.when(part == 0)
    def _():
        gl_out[...] = gl_ref[...]
        mix_ref[...] = local_matrix(wl_ref[...].astype(f32))
        for h in range(2):
            message_to_y(rb_ref, ey_ref, b_ref, q2_ref, h)

    synth = bdzs_ref[...]
    mixing = mix_ref[...]

    def step(block, carry):
        values = cells(s_ref, block)
        total = z_backward(q2_ref, synth, part * blocks + block) + nn(mixing, values)
        out_ref[:, :, pl.ds(pl.multiple_of(block * GROUP * Z, GROUP * Z), GROUP * Z)] = (
            total.astype(bf16).reshape(ROWS, C, GROUP * Z)
        )
        return carry

    lax.fori_loop(0, blocks, step, 0, unroll=True)


def others(axis, count, body):
    me = lax.axis_index(axis)

    def step(k, carry):
        body(lax.rem(me + k, count))
        return carry

    lax.fori_loop(1, count, step, 0)


def enter(n, d):
    barrier = pltpu.get_barrier_semaphore()
    for axis, count in (("pencil", n), ("dp", d)):
        others(
            axis,
            count,
            lambda j, axis=axis: pl.semaphore_signal(
                barrier, inc=1, device_id={axis: j}, device_id_type=MESH
            ),
        )
    return barrier


def remote(src, dst, sems, kind, mine, axis, j):
    return pltpu.make_async_remote_copy(
        src_ref=src,
        dst_ref=dst,
        send_sem=sems.at[2 * kind, j],
        recv_sem=sems.at[2 * kind + 1, mine],
        device_id={axis: j},
        device_id_type=MESH,
    )


def wait_one(view, sem):
    pltpu.make_async_copy(view, view, sem).wait()


def arrived(view, sems, kind, axis, count):
    others(axis, count, lambda j: wait_one(view(j), sems.at[2 * kind + 1, j]))


def sent(view, sems, kind, axis, count):
    others(axis, count, lambda j: wait_one(view(j), sems.at[2 * kind, j]))


def piece(ref, h):
    first, count = chunk_tiles(h)
    return lambda j: ref.at[pl.ds(first, count), pl.ds(pl.multiple_of(j * 8, 8), 8), :]


def modes(ref):
    return lambda j: ref.at[pl.ds(pl.multiple_of(j * 2 * KX, 2 * KX), 2 * KX), :]


def swap(src, dst, sems, kind, axis, count):
    me = lax.axis_index(axis)
    others(axis, count, lambda j: remote(src(j), dst(me), sems, kind, me, axis, j).start())


def send_chunk(n, src_ref, dst_ref, sems, kind, h):
    me = lax.axis_index("pencil")
    swap(piece(src_ref, h), piece(dst_ref, h), sems, kind, "pencil", n)
    first, count = chunk_tiles(h)
    mine = pl.ds(pl.multiple_of(me * 8, 8), 8)
    dst_ref[first : first + count, mine, :] = src_ref[first : first + count, mine, :]


def x_analyse(r_ref, dx_ref, g_ref, d, h):
    first, count = chunk_tiles(h)
    high, low = halves(jnp.concatenate([r_ref[first + t] for t in range(count)], axis=1))
    table = dx_ref[...]
    both = nn(table, high)
    spectrum = both[: 2 * KX] + both[2 * KX :] + nn(table[: 2 * KX], low)
    width = KZ * C // d
    for i in range(d // 2):
        j = owner_order(d)[h * d // 2 + i]
        part = spectrum[:, i * width : (i + 1) * width]
        if width < LANES:
            part = jnp.concatenate([part, jnp.zeros((2 * KX, LANES - width), f32)], axis=1)
        g_ref[j * 2 * KX : (j + 1) * 2 * KX, :] = part


def x_synth(h_ref, ex_ref, mb_ref, d, h):
    width = KZ * C // d
    spectrum = jnp.concatenate(
        [
            h_ref[j * 2 * KX : (j + 1) * 2 * KX, 0:width]
            for j in owner_order(d)[h * d // 2 : (h + 1) * d // 2]
        ],
        axis=1,
    )
    high, low = halves(spectrum)
    rows = nn(ex_ref[...], jnp.concatenate([high, high, low], axis=0))
    first, count = chunk_tiles(h)
    for t in range(count):
        mb_ref[first + t] = rows[:, t * LANES : (t + 1) * LANES]


def pick(ref, kx, d):
    real = ref[pl.ds(kx, d, stride=2 * KX), :]
    imag = ref[pl.ds(KX + kx, d, stride=2 * KX), :]
    return real, imag


def stage_weights(w_ref, w5_ref, wc_ref):
    for ri in range(2):
        for kz in range(2):
            for c in range(C):
                part = w_ref[ri, 0, kz, :, c * C : (c + 1) * C]
                parts = [part]
                if kz:
                    parts = [jnp.zeros((KX, C), f32), part]
                rest = LANES - C * len(parts)
                if rest:
                    parts = parts + [jnp.zeros((KX, rest), f32)]
                w5_ref[ri, kz, pl.ds(c, KX, stride=C), :] = jnp.concatenate(parts, axis=1)

    def pack(kx, carry):
        rows = pl.ds(pl.multiple_of(kx * C, 8), C)
        for ri in range(2):
            parts = [w5_ref[ri, 0, rows, :], w5_ref[ri, 1, rows, :]]
            if LANES > 2 * C:
                parts.append(jnp.zeros((LANES - 2 * C, LANES), f32))
            high, low = halves(jnp.concatenate(parts, axis=0))
            wc_ref[kx, 0:LANES, ri * LANES : (ri + 1) * LANES] = high
            wc_ref[kx, LANES : 2 * LANES, ri * LANES : (ri + 1) * LANES] = low
        return carry

    lax.fori_loop(0, KX, pack, 0)


def mix_modes(h_ref, wc_ref, g2_ref, d):
    def mix(kx, carry):
        real, imag = pick(h_ref, kx, d)
        high, low = halves(jnp.concatenate([real, imag], axis=0))
        left = jnp.concatenate(
            [
                jnp.concatenate([high, high], axis=1),
                jnp.concatenate([low, jnp.zeros_like(low)], axis=1),
            ],
            axis=0,
        )
        both = nn(left, wc_ref[kx])
        both = both[: 2 * d] + both[2 * d :]
        g2_ref[pl.ds(kx, d, stride=2 * KX), :] = both[:d, :LANES] - both[d:, LANES:]
        g2_ref[pl.ds(KX + kx, d, stride=2 * KX), :] = both[:d, LANES:] + both[d:, :LANES]
        return carry

    lax.fori_loop(0, KX, mix, 0, unroll=16)


def stacked(h_ref, kx, d):
    real, imag = pick(h_ref, kx, d)
    return halves(
        jnp.concatenate(
            [
                jnp.concatenate([real, imag], axis=1),
                jnp.concatenate([imag, -real], axis=1),
            ],
            axis=0,
        )
    )


def adjoint_modes(h_ref, wc_ref, g2_ref, d):
    def adjoint(kx, carry):
        high, low = stacked(h_ref, kx, d)
        both = nt(jnp.concatenate([high, low], axis=0), wc_ref[kx])
        total = both[: 2 * d, :LANES] + both[: 2 * d, LANES:] + both[2 * d :, :LANES]
        g2_ref[pl.ds(kx, d, stride=2 * KX), :] = total[:d]
        g2_ref[pl.ds(KX + kx, d, stride=2 * KX), :] = total[d:]
        return carry

    lax.fori_loop(0, KX, adjoint, 0, unroll=16)


def weight_grad(spec_ref, grad_ref, w5_ref, out_ref, d):
    def one(kx, carry):
        high, low = stacked(grad_ref, kx, d)
        real, imag = pick(spec_ref, kx, d)
        shigh, slow = halves(jnp.concatenate([real, imag], axis=0))
        product = tn(
            jnp.concatenate([shigh, slow, shigh], axis=0),
            jnp.concatenate([high, high, low], axis=0),
        )
        rows = pl.ds(pl.multiple_of(kx * C, 8), C)
        for ri in range(2):
            for kz in range(2):
                w5_ref[ri, kz, rows, :] = product[
                    kz * C : (kz + 1) * C, ri * LANES : (ri + 1) * LANES
                ]
        return carry

    lax.fori_loop(0, KX, one, 0, unroll=4)
    group = 8
    for ri in range(2):
        for kz in range(2):
            for first in range(0, C, group):
                out_ref[ri, 0, kz, :, first * C : (first + group) * C] = jnp.concatenate(
                    [
                        w5_ref[ri, kz, pl.ds(c, KX, stride=C), :][:, kz * C : (kz + 1) * C]
                        for c in range(first, first + group)
                    ],
                    axis=1,
                )


def mode_round(n, d, bufs, tables, psem, dsem, base, between, mixer, extra):
    r_ref, g_ref, h_ref, g2_ref, h2_ref, mb_ref, rb_ref = bufs
    dx_ref, ex_ref = tables
    sample = lax.axis_index("dp")
    out, back = base // 2, base // 2 + 1
    own = pl.ds(pl.multiple_of(sample * 2 * KX, 2 * KX), 2 * KX)

    def forward(h):
        arrived(piece(r_ref, h), psem, base + h, "pencil", n)
        x_analyse(r_ref, dx_ref, g_ref, d, h)

        def to_owner(j):
            @pl.when(half_of(j, d) == h)
            def _():
                remote(modes(g_ref)(j), modes(h_ref)(sample), dsem, out, sample, "dp", j).start()

        others("dp", d, to_owner)

    def mix(h):
        @pl.when(half_of(sample, d) == h)
        def _():
            h_ref[own, :] = g_ref[own, :]
            arrived(modes(h_ref), dsem, out, "dp", d)
            mixer(h_ref, g2_ref)
            swap(modes(g2_ref), modes(h2_ref), dsem, back, "dp", d)
            h2_ref[own, :] = g2_ref[own, :]

    def backward(h):
        def from_owner(j):
            @pl.when(half_of(j, d) == h)
            def _():
                wait_one(modes(h2_ref)(j), dsem.at[2 * back + 1, j])

        others("dp", d, from_owner)
        x_synth(h2_ref, ex_ref, mb_ref, d, h)
        send_chunk(n, mb_ref, rb_ref, psem, base + 2 + h, h)

    between()
    forward(0)
    mix(0)
    forward(1)
    extra()
    backward(0)
    mix(1)
    backward(1)


def main_kernel(
    n, d,
    x_hbm, go_hbm, w_hbm, wl_ref, bdz_ref, bdzs_ref, bdzg_ref, dy_ref, ey_ref, dx_ref, ex_ref,
    s_hbm, rb_out, gs_out, gl_out,
    x_ref, go_ref, s_ref, w_ref, w5_ref, wc_ref, q_ref, q2_ref, o_ref, b_ref,
    msg1_ref, r1_ref, g1_ref, h1_ref, g21_ref, h21_ref, mb1_ref, rb1_ref,
    msg2_ref, r2_ref, g2_ref, h2_ref, g22_ref, h22_ref, mb2_ref, rb2_ref,
    gl_ref, glr_ref, glp_ref, gld_ref, glt_ref, glf_ref,
    psem, dsem, qsem, esem, load_sem,
):
    me, sample = lax.axis_index("pencil"), lax.axis_index("dp")
    tiles = C // 8
    keeper = me < tiles
    blocks = Y // GROUP
    parts = 4
    width = Y * Z // parts
    barrier = enter(n, d)
    loads = []
    for i in range(parts):
        view = (slice(None), slice(None), pl.ds(i * width, width))
        loads.append(
            pltpu.make_async_copy(x_hbm.at[view], x_ref.at[view], load_sem.at[i])
        )
    loads.append(pltpu.make_async_copy(w_hbm, w_ref, load_sem.at[parts]))
    loads.append(pltpu.make_async_copy(go_hbm, go_ref, load_sem.at[parts + 1]))
    for load in loads:
        load.start()
    mixing = local_matrix(wl_ref[...].astype(f32).T)

    def analyse(values_ref, table_ref, h, first, last):
        def one(block, carry):
            z_forward(cells(values_ref, block), table_ref[h], q_ref, block, h)
            return carry

        lax.fori_loop(first, last, one, 0, unroll=8)

    for h in range(2):
        for i in range(parts):
            if h == 0:
                loads[i].wait()
            analyse(x_ref, bdz_ref, h, i * blocks // parts, (i + 1) * blocks // parts)
        y_to_message(q_ref, dy_ref, o_ref, msg1_ref, h)
        if h == 0:
            pl.semaphore_wait(barrier, n + d - 2)
        send_chunk(n, msg1_ref, r1_ref, psem, h, h)

    def stage():
        loads[parts].wait()
        stage_weights(w_ref, w5_ref, wc_ref)

    mode_round(
        n, d,
        (r1_ref, g1_ref, h1_ref, g21_ref, h21_ref, mb1_ref, rb1_ref),
        (dx_ref, ex_ref), psem, dsem, 0, stage,
        lambda src, dst: mix_modes(src, wc_ref, dst, d),
        lambda: None,
    )
    loads[parts + 1].wait()
    for h in range(2):
        arrived(piece(rb1_ref, h), psem, 2 + h, "pencil", n)
        message_to_y(rb1_ref, ey_ref, b_ref, q2_ref, h)
    synth = bdzs_ref[...]

    def slopes(block, carry):
        values = cells(x_ref, block)
        preact = z_backward(q2_ref, synth, block) + nn(mixing, values)
        half = (cells(go_ref, block).astype(f32) * gelu_slope(preact)).astype(bf16)
        s_ref[:, :, pl.ds(pl.multiple_of(block * GROUP * Z, GROUP * Z), GROUP * Z)] = half.reshape(
            ROWS, C, GROUP * Z
        )
        return carry

    lax.fori_loop(0, blocks, slopes, 0, unroll=4)
    for h in range(2):
        analyse(s_ref, bdzg_ref, h, 0, blocks)
        y_to_message(q_ref, dy_ref, o_ref, msg2_ref, h)
        send_chunk(n, msg2_ref, r2_ref, psem, 4 + h, h)
    store = pltpu.make_async_copy(s_ref, s_hbm, load_sem.at[0])
    store.start()

    def local_sum():
        gl_ref[...] = jnp.zeros_like(gl_ref)
        total = nt(x_ref[0], s_ref[0])
        for x in range(1, ROWS):
            total = total + nt(x_ref[x], s_ref[x])
        gl_ref[:, :, 0:C] = total.reshape(tiles, 8, C)

        def to_keeper(j):
            @pl.when(j < tiles)
            def _():
                remote(gl_ref.at[j], glr_ref.at[me], qsem, 0, me, "pencil", j).start()

        others("pencil", n, to_keeper)

    def local_reduce():
        @pl.when(keeper)
        def _():
            glr_ref[me] = gl_ref[me]
            arrived(lambda j: glr_ref.at[j], qsem, 0, "pencil", n)
            glp_ref[...] = jnp.sum(glr_ref[...], axis=0)
            others(
                "dp",
                d,
                lambda j: remote(glp_ref, gld_ref.at[sample], esem, 0, sample, "dp", j).start(),
            )
            gld_ref[sample] = glp_ref[...]

    def local_spread():
        @pl.when(keeper)
        def _():
            arrived(lambda j: gld_ref.at[j], esem, 0, "dp", d)
            glt_ref[...] = jnp.sum(gld_ref[...], axis=0)
            others(
                "pencil",
                n,
                lambda j: remote(glt_ref, glf_ref.at[me], qsem, 1, me, "pencil", j).start(),
            )
            glf_ref[me] = glt_ref[...]

    mode_round(
        n, d,
        (r2_ref, g2_ref, h2_ref, g22_ref, h22_ref, mb2_ref, rb2_ref),
        (dx_ref, ex_ref), psem, dsem, 4, local_sum,
        lambda src, dst: adjoint_modes(src, wc_ref, dst, d),
        local_reduce,
    )
    local_spread()
    weight_grad(h1_ref, h2_ref, w5_ref, gs_out, d)
    for base, (first, modes1, modes2, second) in (
        (0, (msg1_ref, g1_ref, g21_ref, mb1_ref)),
        (4, (msg2_ref, g2_ref, g22_ref, mb2_ref)),
    ):
        for h in range(2):
            sent(piece(first, h), psem, base + h, "pencil", n)
            sent(piece(second, h), psem, base + 2 + h, "pencil", n)
        sent(modes(modes1), dsem, base // 2, "dp", d)
        sent(modes(modes2), dsem, base // 2 + 1, "dp", d)

    def keeper_sent(j):
        @pl.when(j < tiles)
        def _():
            wait_one(gl_ref.at[j], qsem.at[0, j])
            wait_one(glf_ref.at[j], qsem.at[3, j])

    others("pencil", n, keeper_sent)
    gl_out[...] = glf_ref[...].reshape(C, LANES)[:, :C]

    @pl.when(keeper)
    def _():
        sent(lambda j: glp_ref, esem, 0, "dp", d)
        sent(lambda j: glt_ref, qsem, 1, "pencil", n)

    store.wait()
    for h in range(2):
        arrived(piece(rb2_ref, h), psem, 6 + h, "pencil", n)
    rb_out[...] = rb2_ref[...]


def params(**extra):
    return {
        "compiler_params": pltpu.CompilerParams(vmem_limit_bytes=LIMIT, **extra),
        "cost_estimate": pl.CostEstimate(
            flops=1_000_000_000, bytes_accessed=4_000_000, transcendentals=0
        ),
    }


def local(n, d, field_in, grad_out, w_spec, w_local):
    sds = jax.ShapeDtypeStruct
    lane_tiles = KZ * C // LANES
    values, upstream = field_in[0], grad_out[0]
    cells_shape = values.shape
    ones = np.ones((KZ,))
    scale = z_scale()
    bdz = by_half(z_table(ones, d))
    bdz_grad = by_half(z_table(scale, d))
    synth = tall(z_table(scale, d))
    synth_plain = tall(z_table(ones, d))
    dy = tall(y_forward())
    ey = wide3(y_forward().T)
    dx = tall(x_forward())
    ex = wide3(x_forward().T)

    message = sds((lane_tiles, n * 8, LANES), f32)
    q_shape = pltpu.VMEM((KZ, Y * 2, ROWS * C), f32)
    q2_shape = pltpu.VMEM((KZ, Y * 2, 2 * LANES), f32)
    o_shape = pltpu.VMEM((KZ, 2 * KY, ROWS * C), f32)
    b_shape = pltpu.VMEM((KZ, 2 * KY, 2 * LANES), f32)
    mode_shape = pltpu.VMEM((d * 2 * KX, LANES), f32)
    message_shape = pltpu.VMEM((lane_tiles, n * 8, LANES), f32)
    exchange = [message_shape] * 2 + [mode_shape] * 4 + [message_shape] * 2
    tile = pltpu.VMEM((8, LANES), f32)
    tile_count = C // 8
    anywhere = pl.BlockSpec(memory_space=pl.ANY)
    vmem = pl.BlockSpec(memory_space=pltpu.VMEM)
    slopes, rb, grad_spec, grad_local = pl.pallas_call(
        functools.partial(main_kernel, n, d),
        out_shape=(
            sds(cells_shape, bf16),
            message,
            sds(w_spec.shape, f32),
            sds((C, C), f32),
        ),
        in_specs=[anywhere] * 3 + [vmem] * 8,
        out_specs=(anywhere, vmem, vmem, vmem),
        scratch_shapes=[
            pltpu.VMEM(cells_shape, bf16),
            pltpu.VMEM(cells_shape, bf16),
            pltpu.VMEM(cells_shape, bf16),
            pltpu.VMEM(w_spec.shape, f32),
            pltpu.VMEM((2, 2, KX * C, LANES), f32),
            pltpu.VMEM((KX, 2 * LANES, 2 * LANES), bf16),
            q_shape,
            q2_shape,
            o_shape,
            b_shape,
        ]
        + exchange * 2
        + [
            pltpu.VMEM((tile_count, 8, LANES), f32),
            pltpu.VMEM((n, 8, LANES), f32),
            tile,
            pltpu.VMEM((d, 8, LANES), f32),
            tile,
            pltpu.VMEM((tile_count, 8, LANES), f32),
            pltpu.SemaphoreType.DMA((16, n)),
            pltpu.SemaphoreType.DMA((8, d)),
            pltpu.SemaphoreType.DMA((4, n)),
            pltpu.SemaphoreType.DMA((2, d)),
            pltpu.SemaphoreType.DMA((6,)),
        ],
        name="spectral_backward",
        **params(collective_id=0, has_side_effects=True),
    )(values, upstream, w_spec, w_local, bdz, synth, bdz_grad, dy, ey, dx, ex)
    parts = 4
    strip = pl.BlockSpec((ROWS, C, Y * Z // parts), lambda i: (0, 0, i))
    whole = pl.BlockSpec(memory_space=pltpu.VMEM)
    modes_strip = pl.BlockSpec(
        w_spec.shape[:3] + (KX // parts, C * C), lambda i: (0, 0, 0, i, 0)
    )
    grad_in, grad_spec, grad_local = pl.pallas_call(
        last_kernel,
        out_shape=(sds(cells_shape, bf16), sds(w_spec.shape, f32), sds((C, C), f32)),
        grid=(parts,),
        in_specs=[whole, strip, whole, whole, whole, modes_strip, whole],
        out_specs=(strip, modes_strip, whole),
        scratch_shapes=[b_shape, q2_shape, pltpu.VMEM((ROWS * C, ROWS * C), bf16)],
        name="plane_synthesis",
        **params(),
    )(rb, slopes, w_local, ey, synth_plain, grad_spec, grad_local)
    return grad_in[None], grad_spec, grad_local


def solution(mesh):
    n, d = mesh.shape["pencil"], mesh.shape["dp"]
    placed = (
        P("dp", "pencil", None, None),
        P("dp", "pencil", None, None),
        P(None, "pencil", "dp", None, None),
        P(),
    )
    return jax.shard_map(
        functools.partial(local, n, d),
        mesh=mesh,
        in_specs=placed,
        out_specs=(P("dp", "pencil", None, None), P(None, "pencil", "dp", None, None), P()),
        check_vma=False,
    )
```

```python
import functools

import jax
import jax.numpy as jnp
import ml_dtypes
import numpy as np
from jax import lax
from jax.experimental import pallas as pl
from jax.experimental.pallas import tpu as pltpu
from jax.sharding import PartitionSpec as P

X = 128
Y = 128
Z = 64
C = 48
KX = 32
KY = 32
KZ = 16
ROWS = 4
GROUP = 4
LANES = 128
LIMIT = 56 * 1024 * 1024

MESH = pl.DeviceIdType.MESH
f32 = jnp.float32
bf16 = jnp.bfloat16


def split(table):
    high = table.astype(np.float32).astype(ml_dtypes.bfloat16)
    low = (table - high.astype(np.float64)).astype(np.float32).astype(ml_dtypes.bfloat16)
    return high, low


def signed(count):
    freqs = np.arange(count)
    return np.where(freqs < count // 2, freqs, freqs - count)


def forward_table(length, count):
    angles = 2.0 * np.pi * (np.outer(signed(count), np.arange(length)) % length) / length
    cos, sin = np.cos(angles), np.sin(angles)
    table = np.zeros((2, count, length, 2))
    table[0, :, :, 0] = cos
    table[0, :, :, 1] = sin
    table[1, :, :, 0] = -sin
    table[1, :, :, 1] = cos
    return table.reshape(2 * count, length, 2)


def half_of(sample, d):
    return (sample // max(d // 4, 1)) % 2


def owner_order(d):
    return sorted(range(d), key=lambda j: (half_of(j, d), j))


def kz_order(d):
    return np.array([2 * j + k for j in owner_order(d) for k in range(2)])


def z_table(scale, d):
    order = kz_order(d)
    scale = scale[order]
    angles = 2.0 * np.pi * (np.outer(order, np.arange(Z)) % Z) / Z
    table = np.zeros((KZ, GROUP, 2, GROUP, Z))
    for place in range(GROUP):
        table[:, place, 0, place] = np.cos(angles) * scale[:, None]
        table[:, place, 1, place] = -np.sin(angles) * scale[:, None]
    return table.reshape(KZ * GROUP * 2, GROUP * Z)


def z_scale():
    return np.where(np.arange(KZ) == 0, 1.0, 2.0) / float(X * Y * Z)


def tall(table):
    return np.concatenate(split(table), axis=0)


def by_half(table):
    rows = table.shape[0] // 2
    return np.stack([tall(table[:rows]), tall(table[rows:])])


def wide3(table):
    high, low = split(table)
    return np.concatenate([high, low, high], axis=1)


def y_forward():
    return forward_table(Y, KY).reshape(2 * KY, Y * 2)


def x_forward():
    table = forward_table(X, KX).reshape(2 * KX, X // ROWS, ROWS, 2)
    return table.transpose(0, 1, 3, 2).reshape(2 * KX, X * 2)


def nt(left, right):
    return lax.dot_general(left, right, (((1,), (1,)), ((), ())), preferred_element_type=f32)


def tn(left, right):
    return lax.dot_general(left, right, (((0,), (0,)), ((), ())), preferred_element_type=f32)


def nn(left, right):
    return jnp.dot(left, right, preferred_element_type=f32)


def halves(values):
    high = values.astype(bf16)
    low = (values - high.astype(f32)).astype(bf16)
    return high, low


def cells(ref, block):
    return ref[:, :, pl.ds(pl.multiple_of(block * GROUP * Z, GROUP * Z), GROUP * Z)].reshape(
        ROWS * C, GROUP * Z
    )


def z_forward(values, table, q_ref, block, h):
    rows = KZ * GROUP
    both = nt(table, values)
    part = both[:rows] + both[rows:]
    q_ref[h * KZ // 2 : (h + 1) * KZ // 2, pl.ds(pl.multiple_of(block * 8, 8), 8), :] = (
        part.reshape(KZ // 2, 8, ROWS * C)
    )


def y_to_message(q_ref, dy_ref, o_ref, msg_ref, h):
    table = dy_ref[...]
    span = range(h * KZ // 2, (h + 1) * KZ // 2)
    for kz in span:
        both = nn(table, q_ref[kz].astype(bf16))
        o_ref[kz] = both[: 2 * KY] + both[2 * KY :]
    first, count = chunk_tiles(h)
    for ri in range(2):
        for x in range(ROWS):
            row = jnp.concatenate(
                [o_ref[kz, ri * KY : (ri + 1) * KY, x * C : (x + 1) * C] for kz in span], axis=1
            )
            for t in range(count):
                msg_ref[first + t, pl.ds(ri * ROWS + x, KY, stride=8), :] = row[
                    :, t * LANES : (t + 1) * LANES
                ]


def message_to_y(rb_ref, ey_ref, b_ref, q_ref, h):
    first, count = chunk_tiles(h)
    span = range(h * KZ // 2, (h + 1) * KZ // 2)
    for kz in span if ROWS * C < b_ref.shape[2] else ():
        b_ref[kz, :, ROWS * C :] = jnp.zeros((2 * KY, b_ref.shape[2] - ROWS * C), f32)
    for ri in range(2):
        for x in range(ROWS):
            row = jnp.concatenate(
                [
                    rb_ref[first + t, pl.ds(ri * ROWS + x, KY, stride=8), :]
                    for t in range(count)
                ],
                axis=1,
            )
            for i, kz in enumerate(span):
                b_ref[kz, ri * KY : (ri + 1) * KY, x * C : (x + 1) * C] = row[
                    :, i * C : (i + 1) * C
                ]
    table = ey_ref[...]
    for kz in span:
        high, low = halves(b_ref[kz])
        q_ref[kz] = nn(table, jnp.concatenate([high, high, low], axis=0))


def z_backward(q_ref, table_ref, block, h):
    rows = pl.ds(pl.multiple_of(block * 8, 8), 8)
    part = q_ref[h * KZ // 2 : (h + 1) * KZ // 2, rows, :]
    part = part.reshape(KZ * 4, q_ref.shape[2])
    turned = part.T[: ROWS * C].astype(bf16)
    return nn(jnp.concatenate([turned, turned], axis=1), table_ref[h])


def chunk_tiles(h):
    count = KZ * C // LANES // 2
    return h * count, count


def gelu_slope(values):
    size = jnp.abs(values)
    bell = jnp.exp(values * values * -0.5)
    t = 1.0 / (1.0 + (0.3275911 * 0.7071067811865476) * size)
    poly = 0.5 * 1.061405429
    poly = poly * t + 0.5 * -1.453152027
    poly = poly * t + 0.5 * 1.421413741
    poly = poly * t + 0.5 * -0.284496736
    poly = poly * t + 0.5 * 0.254829592
    tail = poly * t * bell
    cumul = jnp.where(values >= 0.0, 1.0 - tail, tail)
    return cumul + values * bell * 0.3989422804014327


def local_matrix(weights):
    rows = []
    for x in range(ROWS):
        parts = [weights]
        if x:
            parts = [jnp.zeros((C, x * C), f32)] + parts
        if x < ROWS - 1:
            parts = parts + [jnp.zeros((C, (ROWS - 1 - x) * C), f32)]
        rows.append(jnp.concatenate(parts, axis=1))
    return jnp.concatenate(rows, axis=0).astype(bf16)


def others(axis, count, body):
    me = lax.axis_index(axis)

    def step(k, carry):
        body(lax.rem(me + k, count))
        return carry

    lax.fori_loop(1, count, step, 0)


def enter(n, d):
    barrier = pltpu.get_barrier_semaphore()
    for axis, count in (("pencil", n), ("dp", d)):
        others(
            axis,
            count,
            lambda j, axis=axis: pl.semaphore_signal(
                barrier, inc=1, device_id={axis: j}, device_id_type=MESH
            ),
        )
    return barrier


def remote(src, dst, sems, kind, mine, axis, j):
    return pltpu.make_async_remote_copy(
        src_ref=src,
        dst_ref=dst,
        send_sem=sems.at[2 * kind, j],
        recv_sem=sems.at[2 * kind + 1, mine],
        device_id={axis: j},
        device_id_type=MESH,
    )


def wait_one(view, sem):
    pltpu.make_async_copy(view, view, sem).wait()


def arrived(view, sems, kind, axis, count):
    others(axis, count, lambda j: wait_one(view(j), sems.at[2 * kind + 1, j]))


def sent(view, sems, kind, axis, count):
    others(axis, count, lambda j: wait_one(view(j), sems.at[2 * kind, j]))


def piece(ref, h):
    first, count = chunk_tiles(h)
    return lambda j: ref.at[pl.ds(first, count), pl.ds(pl.multiple_of(j * 8, 8), 8), :]


def modes(ref):
    return lambda j: ref.at[pl.ds(pl.multiple_of(j * 2 * KX, 2 * KX), 2 * KX), :]


def swap(src, dst, sems, kind, axis, count):
    me = lax.axis_index(axis)
    others(axis, count, lambda j: remote(src(j), dst(me), sems, kind, me, axis, j).start())


def send_chunk(n, src_ref, dst_ref, sems, kind, h):
    me = lax.axis_index("pencil")
    swap(piece(src_ref, h), piece(dst_ref, h), sems, kind, "pencil", n)
    first, count = chunk_tiles(h)
    mine = pl.ds(pl.multiple_of(me * 8, 8), 8)
    dst_ref[first : first + count, mine, :] = src_ref[first : first + count, mine, :]


def x_analyse(r_ref, dx_ref, g_ref, d, h):
    first, count = chunk_tiles(h)
    high, low = halves(jnp.concatenate([r_ref[first + t] for t in range(count)], axis=1))
    table = dx_ref[...]
    both = nn(table, high)
    spectrum = both[: 2 * KX] + both[2 * KX :] + nn(table[: 2 * KX], low)
    width = KZ * C // d
    for i in range(d // 2):
        j = owner_order(d)[h * d // 2 + i]
        part = spectrum[:, i * width : (i + 1) * width]
        if width < LANES:
            part = jnp.concatenate([part, jnp.zeros((2 * KX, LANES - width), f32)], axis=1)
        g_ref[j * 2 * KX : (j + 1) * 2 * KX, :] = part


def x_synth(h_ref, ex_ref, mb_ref, d, h):
    width = KZ * C // d
    spectrum = jnp.concatenate(
        [
            h_ref[j * 2 * KX : (j + 1) * 2 * KX, 0:width]
            for j in owner_order(d)[h * d // 2 : (h + 1) * d // 2]
        ],
        axis=1,
    )
    high, low = halves(spectrum)
    rows = nn(ex_ref[...], jnp.concatenate([high, high, low], axis=0))
    first, count = chunk_tiles(h)
    for t in range(count):
        mb_ref[first + t] = rows[:, t * LANES : (t + 1) * LANES]


def pick(ref, kx, d):
    real = ref[pl.ds(kx, d, stride=2 * KX), :]
    imag = ref[pl.ds(KX + kx, d, stride=2 * KX), :]
    return real, imag


def stage_weights(w_ref, w5_ref, wc_ref):
    for ri in range(2):
        for kz in range(2):
            for c in range(C):
                part = w_ref[ri, 0, kz, :, c * C : (c + 1) * C]
                parts = [part]
                if kz:
                    parts = [jnp.zeros((KX, C), f32), part]
                rest = LANES - C * len(parts)
                if rest:
                    parts = parts + [jnp.zeros((KX, rest), f32)]
                w5_ref[ri, kz, pl.ds(c, KX, stride=C), :] = jnp.concatenate(parts, axis=1)

    def pack(kx, carry):
        rows = pl.ds(pl.multiple_of(kx * C, 8), C)
        for ri in range(2):
            parts = [w5_ref[ri, 0, rows, :], w5_ref[ri, 1, rows, :]]
            if LANES > 2 * C:
                parts.append(jnp.zeros((LANES - 2 * C, LANES), f32))
            high, low = halves(jnp.concatenate(parts, axis=0))
            wc_ref[kx, 0:LANES, ri * LANES : (ri + 1) * LANES] = high
            wc_ref[kx, LANES : 2 * LANES, ri * LANES : (ri + 1) * LANES] = low
        return carry

    lax.fori_loop(0, KX, pack, 0)


def mix_modes(h_ref, wc_ref, g2_ref, d):
    def mix(kx, carry):
        real, imag = pick(h_ref, kx, d)
        high, low = halves(jnp.concatenate([real, imag], axis=0))
        left = jnp.concatenate(
            [
                jnp.concatenate([high, high], axis=1),
                jnp.concatenate([low, jnp.zeros_like(low)], axis=1),
            ],
            axis=0,
        )
        both = nn(left, wc_ref[kx])
        both = both[: 2 * d] + both[2 * d :]
        g2_ref[pl.ds(kx, d, stride=2 * KX), :] = both[:d, :LANES] - both[d:, LANES:]
        g2_ref[pl.ds(KX + kx, d, stride=2 * KX), :] = both[:d, LANES:] + both[d:, :LANES]
        return carry

    lax.fori_loop(0, KX, mix, 0, unroll=16)


def stacked(h_ref, kx, d):
    real, imag = pick(h_ref, kx, d)
    return halves(
        jnp.concatenate(
            [
                jnp.concatenate([real, imag], axis=1),
                jnp.concatenate([imag, -real], axis=1),
            ],
            axis=0,
        )
    )


def adjoint_modes(h_ref, wc_ref, g2_ref, d):
    def adjoint(kx, carry):
        high, low = stacked(h_ref, kx, d)
        both = nt(jnp.concatenate([high, low], axis=0), wc_ref[kx])
        total = both[: 2 * d, :LANES] + both[: 2 * d, LANES:] + both[2 * d :, :LANES]
        g2_ref[pl.ds(kx, d, stride=2 * KX), :] = total[:d]
        g2_ref[pl.ds(KX + kx, d, stride=2 * KX), :] = total[d:]
        return carry

    lax.fori_loop(0, KX, adjoint, 0, unroll=16)


def weight_grad(spec_ref, grad_ref, w5_ref, out_ref, d):
    def one(kx, carry):
        high, low = stacked(grad_ref, kx, d)
        real, imag = pick(spec_ref, kx, d)
        shigh, slow = halves(jnp.concatenate([real, imag], axis=0))
        product = tn(
            jnp.concatenate([shigh, slow, shigh], axis=0),
            jnp.concatenate([high, high, low], axis=0),
        )
        rows = pl.ds(pl.multiple_of(kx * C, 8), C)
        for ri in range(2):
            for kz in range(2):
                w5_ref[ri, kz, rows, :] = product[
                    kz * C : (kz + 1) * C, ri * LANES : (ri + 1) * LANES
                ]
        return carry

    lax.fori_loop(0, KX, one, 0, unroll=4)
    group = 8
    for ri in range(2):
        for kz in range(2):
            for first in range(0, C, group):
                out_ref[ri, 0, kz, :, first * C : (first + group) * C] = jnp.concatenate(
                    [
                        w5_ref[ri, kz, pl.ds(c, KX, stride=C), :][:, kz * C : (kz + 1) * C]
                        for c in range(first, first + group)
                    ],
                    axis=1,
                )


def mode_round(n, d, bufs, tables, psem, dsem, base, between, mixer, extra):
    r_ref, g_ref, h_ref, g2_ref, h2_ref, mb_ref, rb_ref = bufs
    dx_ref, ex_ref = tables
    sample = lax.axis_index("dp")
    out, back = base // 2, base // 2 + 1
    own = pl.ds(pl.multiple_of(sample * 2 * KX, 2 * KX), 2 * KX)

    def forward(h):
        arrived(piece(r_ref, h), psem, base + h, "pencil", n)
        x_analyse(r_ref, dx_ref, g_ref, d, h)

        def to_owner(j):
            @pl.when(half_of(j, d) == h)
            def _():
                remote(modes(g_ref)(j), modes(h_ref)(sample), dsem, out, sample, "dp", j).start()

        others("dp", d, to_owner)

    def mix(h):
        @pl.when(half_of(sample, d) == h)
        def _():
            h_ref[own, :] = g_ref[own, :]
            arrived(modes(h_ref), dsem, out, "dp", d)
            mixer(h_ref, g2_ref)
            swap(modes(g2_ref), modes(h2_ref), dsem, back, "dp", d)
            h2_ref[own, :] = g2_ref[own, :]

    def backward(h):
        def from_owner(j):
            @pl.when(half_of(j, d) == h)
            def _():
                wait_one(modes(h2_ref)(j), dsem.at[2 * back + 1, j])

        others("dp", d, from_owner)
        x_synth(h2_ref, ex_ref, mb_ref, d, h)
        send_chunk(n, mb_ref, rb_ref, psem, base + 2 + h, h)

    between()
    forward(0)
    mix(0)
    forward(1)
    extra()
    backward(0)
    mix(1)
    backward(1)


def main_kernel(
    n, d,
    x_hbm, go_hbm, w_hbm, wl_ref, bdz_ref, bdzg_ref, dy_ref, ey_ref, dx_ref, ex_ref,
    out_ref, gs_out, gl_out,
    x_ref, go_ref, s_ref, p_ref, w_ref, w5_ref, wc_ref, q_ref, q2_ref, o_ref, b_ref,
    msg1_ref, r1_ref, g1_ref, h1_ref, g21_ref, h21_ref, mb1_ref, rb1_ref,
    msg2_ref, r2_ref, g2_ref, h2_ref, g22_ref, h22_ref, mb2_ref, rb2_ref,
    gl_ref, glr_ref, glp_ref, gld_ref, glt_ref, glf_ref,
    psem, dsem, qsem, esem, load_sem,
):
    me, sample = lax.axis_index("pencil"), lax.axis_index("dp")
    tiles = C // 8
    keeper = me < tiles
    blocks = Y // GROUP
    parts = 4
    width = Y * Z // parts
    barrier = enter(n, d)
    loads = []
    for i in range(parts):
        view = (slice(None), slice(None), pl.ds(i * width, width))
        loads.append(
            pltpu.make_async_copy(x_hbm.at[view], x_ref.at[view], load_sem.at[i])
        )
    loads.append(pltpu.make_async_copy(w_hbm, w_ref, load_sem.at[parts]))
    loads.append(pltpu.make_async_copy(go_hbm, go_ref, load_sem.at[parts + 1]))
    for load in loads:
        load.start()
    weights = wl_ref[...].astype(f32)
    mixing = local_matrix(weights.T)

    def analyse(values_ref, table_ref, h, first, last):
        def one(block, carry):
            z_forward(cells(values_ref, block), table_ref[h], q_ref, block, h)
            return carry

        lax.fori_loop(first, last, one, 0, unroll=8)

    for h in range(2):
        for i in range(parts):
            if h == 0:
                loads[i].wait()
            analyse(x_ref, bdz_ref, h, i * blocks // parts, (i + 1) * blocks // parts)
        y_to_message(q_ref, dy_ref, o_ref, msg1_ref, h)
        if h == 0:
            pl.semaphore_wait(barrier, n + d - 2)
        send_chunk(n, msg1_ref, r1_ref, psem, h, h)

    def stage():
        loads[parts].wait()
        stage_weights(w_ref, w5_ref, wc_ref)

    mode_round(
        n, d,
        (r1_ref, g1_ref, h1_ref, g21_ref, h21_ref, mb1_ref, rb1_ref),
        (dx_ref, ex_ref), psem, dsem, 0, stage,
        lambda src, dst: mix_modes(src, wc_ref, dst, d),
        lambda: None,
    )
    loads[parts + 1].wait()

    def strip(block):
        return pl.ds(pl.multiple_of(block * GROUP * Z, GROUP * Z), GROUP * Z)

    def synthesize(rb_ref, kind, table_ref, matrix, values_ref, finish):
        def begin(block, carry):
            p_ref[:, strip(block)] = z_backward(q2_ref, table_ref, block, 0) + nn(
                matrix, cells(values_ref, block)
            )
            return carry

        def end(block, carry):
            total = p_ref[:, strip(block)] + z_backward(q2_ref, table_ref, block, 1)
            finish(block, total)
            return carry

        for h, loop in enumerate((begin, end)):
            arrived(piece(rb_ref, h), psem, kind + h, "pencil", n)
            message_to_y(rb_ref, ey_ref, b_ref, q2_ref, h)
            lax.fori_loop(0, blocks, loop, 0, unroll=4)

    def slopes(block, preact):
        half = (cells(go_ref, block).astype(f32) * gelu_slope(preact)).astype(bf16)
        s_ref[:, :, strip(block)] = half.reshape(ROWS, C, GROUP * Z)

    synthesize(rb1_ref, 2, bdzg_ref, mixing, x_ref, slopes)
    for h in range(2):
        analyse(s_ref, bdzg_ref, h, 0, blocks)
        y_to_message(q_ref, dy_ref, o_ref, msg2_ref, h)
        send_chunk(n, msg2_ref, r2_ref, psem, 4 + h, h)

    def local_sum():
        gl_ref[...] = jnp.zeros_like(gl_ref)
        total = nt(x_ref[0], s_ref[0])
        for x in range(1, ROWS):
            total = total + nt(x_ref[x], s_ref[x])
        gl_ref[:, :, 0:C] = total.reshape(tiles, 8, C)

        def to_keeper(j):
            @pl.when(j < tiles)
            def _():
                remote(gl_ref.at[j], glr_ref.at[me], qsem, 0, me, "pencil", j).start()

        others("pencil", n, to_keeper)

    def local_reduce():
        @pl.when(keeper)
        def _():
            glr_ref[me] = gl_ref[me]
            arrived(lambda j: glr_ref.at[j], qsem, 0, "pencil", n)
            glp_ref[...] = jnp.sum(glr_ref[...], axis=0)
            others(
                "dp",
                d,
                lambda j: remote(glp_ref, gld_ref.at[sample], esem, 0, sample, "dp", j).start(),
            )
            gld_ref[sample] = glp_ref[...]

    def local_spread():
        @pl.when(keeper)
        def _():
            arrived(lambda j: gld_ref.at[j], esem, 0, "dp", d)
            glt_ref[...] = jnp.sum(gld_ref[...], axis=0)
            others(
                "pencil",
                n,
                lambda j: remote(glt_ref, glf_ref.at[me], qsem, 1, me, "pencil", j).start(),
            )
            glf_ref[me] = glt_ref[...]

    mode_round(
        n, d,
        (r2_ref, g2_ref, h2_ref, g22_ref, h22_ref, mb2_ref, rb2_ref),
        (dx_ref, ex_ref), psem, dsem, 4, local_sum,
        lambda src, dst: adjoint_modes(src, wc_ref, dst, d),
        local_reduce,
    )
    local_spread()
    weight_grad(h1_ref, h2_ref, w5_ref, gs_out, d)
    for base, (first, modes1, modes2, second) in (
        (0, (msg1_ref, g1_ref, g21_ref, mb1_ref)),
        (4, (msg2_ref, g2_ref, g22_ref, mb2_ref)),
    ):
        for h in range(2):
            sent(piece(first, h), psem, base + h, "pencil", n)
            sent(piece(second, h), psem, base + 2 + h, "pencil", n)
        sent(modes(modes1), dsem, base // 2, "dp", d)
        sent(modes(modes2), dsem, base // 2 + 1, "dp", d)

    def keeper_sent(j):
        @pl.when(j < tiles)
        def _():
            wait_one(gl_ref.at[j], qsem.at[0, j])
            wait_one(glf_ref.at[j], qsem.at[3, j])

    others("pencil", n, keeper_sent)
    gl_out[...] = glf_ref[...].reshape(C, LANES)[:, :C]

    @pl.when(keeper)
    def _():
        sent(lambda j: glp_ref, esem, 0, "dp", d)
        sent(lambda j: glt_ref, qsem, 1, "pencil", n)

    def gradient(block, total):
        out_ref[:, :, strip(block)] = total.astype(bf16).reshape(ROWS, C, GROUP * Z)

    synthesize(rb2_ref, 6, bdz_ref, local_matrix(weights), s_ref, gradient)


def params(**extra):
    return {
        "compiler_params": pltpu.CompilerParams(vmem_limit_bytes=LIMIT, **extra),
        "cost_estimate": pl.CostEstimate(
            flops=1_000_000_000, bytes_accessed=4_000_000, transcendentals=0
        ),
    }


def local(n, d, field_in, grad_out, w_spec, w_local):
    sds = jax.ShapeDtypeStruct
    lane_tiles = KZ * C // LANES
    values, upstream = field_in[0], grad_out[0]
    cells_shape = values.shape
    ones = np.ones((KZ,))
    scale = z_scale()
    bdz = by_half(z_table(ones, d))
    bdz_grad = by_half(z_table(scale, d))
    dy = tall(y_forward())
    ey = wide3(y_forward().T)
    dx = tall(x_forward())
    ex = wide3(x_forward().T)

    q_shape = pltpu.VMEM((KZ, Y * 2, ROWS * C), f32)
    q2_shape = pltpu.VMEM((KZ, Y * 2, 2 * LANES), f32)
    o_shape = pltpu.VMEM((KZ, 2 * KY, ROWS * C), f32)
    b_shape = pltpu.VMEM((KZ, 2 * KY, 2 * LANES), f32)
    mode_shape = pltpu.VMEM((d * 2 * KX, LANES), f32)
    message_shape = pltpu.VMEM((lane_tiles, n * 8, LANES), f32)
    exchange = [message_shape] * 2 + [mode_shape] * 4 + [message_shape] * 2
    tile = pltpu.VMEM((8, LANES), f32)
    tile_count = C // 8
    anywhere = pl.BlockSpec(memory_space=pl.ANY)
    vmem = pl.BlockSpec(memory_space=pltpu.VMEM)
    grad_in, grad_spec, grad_local = pl.pallas_call(
        functools.partial(main_kernel, n, d),
        out_shape=(sds(cells_shape, bf16), sds(w_spec.shape, f32), sds((C, C), f32)),
        in_specs=[anywhere] * 3 + [vmem] * 7,
        out_specs=(vmem, vmem, vmem),
        scratch_shapes=[
            pltpu.VMEM(cells_shape, bf16),
            pltpu.VMEM(cells_shape, bf16),
            pltpu.VMEM(cells_shape, bf16),
            pltpu.VMEM((ROWS * C, Y * Z), f32),
            pltpu.VMEM(w_spec.shape, f32),
            pltpu.VMEM((2, 2, KX * C, LANES), f32),
            pltpu.VMEM((KX, 2 * LANES, 2 * LANES), bf16),
            q_shape,
            q2_shape,
            o_shape,
            b_shape,
        ]
        + exchange * 2
        + [
            pltpu.VMEM((tile_count, 8, LANES), f32),
            pltpu.VMEM((n, 8, LANES), f32),
            tile,
            pltpu.VMEM((d, 8, LANES), f32),
            tile,
            pltpu.VMEM((tile_count, 8, LANES), f32),
            pltpu.SemaphoreType.DMA((16, n)),
            pltpu.SemaphoreType.DMA((8, d)),
            pltpu.SemaphoreType.DMA((4, n)),
            pltpu.SemaphoreType.DMA((2, d)),
            pltpu.SemaphoreType.DMA((6,)),
        ],
        name="spectral_backward",
        **params(collective_id=0, has_side_effects=True),
    )(values, upstream, w_spec, w_local, bdz, bdz_grad, dy, ey, dx, ex)
    return grad_in[None], grad_spec, grad_local


def solution(mesh):
    n, d = mesh.shape["pencil"], mesh.shape["dp"]
    placed = (
        P("dp", "pencil", None, None),
        P("dp", "pencil", None, None),
        P(None, "pencil", "dp", None, None),
        P(),
    )
    return jax.shard_map(
        functools.partial(local, n, d),
        mesh=mesh,
        in_specs=placed,
        out_specs=(P("dp", "pencil", None, None), P(None, "pencil", "dp", None, None), P()),
        check_vma=False,
    )
```

```python
import functools

import jax
import jax.numpy as jnp
import ml_dtypes
import numpy as np
from jax import lax
from jax.experimental import pallas as pl
from jax.experimental.pallas import tpu as pltpu
from jax.sharding import PartitionSpec as P

X = 128
Y = 128
Z = 64
C = 48
KX = 32
KY = 32
KZ = 16
ROWS = 4
GROUP = 4
LANES = 128
LIMIT = 56 * 1024 * 1024

MESH = pl.DeviceIdType.MESH
f32 = jnp.float32
bf16 = jnp.bfloat16


def split(table):
    high = table.astype(np.float32).astype(ml_dtypes.bfloat16)
    low = (table - high.astype(np.float64)).astype(np.float32).astype(ml_dtypes.bfloat16)
    return high, low


def signed(count):
    freqs = np.arange(count)
    return np.where(freqs < count // 2, freqs, freqs - count)


def forward_table(length, count):
    angles = 2.0 * np.pi * (np.outer(signed(count), np.arange(length)) % length) / length
    cos, sin = np.cos(angles), np.sin(angles)
    table = np.zeros((2, count, length, 2))
    table[0, :, :, 0] = cos
    table[0, :, :, 1] = sin
    table[1, :, :, 0] = -sin
    table[1, :, :, 1] = cos
    return table.reshape(2 * count, length, 2)


def half_of(sample, d):
    return (sample // max(d // 4, 1)) % 2


def owner_order(d):
    return sorted(range(d), key=lambda j: (half_of(j, d), j))


def kz_order(d):
    return np.array([2 * j + k for j in owner_order(d) for k in range(2)])


def z_table(scale, d):
    order = kz_order(d)
    scale = scale[order]
    angles = 2.0 * np.pi * (np.outer(order, np.arange(Z)) % Z) / Z
    table = np.zeros((KZ, GROUP, 2, GROUP, Z))
    for place in range(GROUP):
        table[:, place, 0, place] = np.cos(angles) * scale[:, None]
        table[:, place, 1, place] = -np.sin(angles) * scale[:, None]
    return table.reshape(KZ * GROUP * 2, GROUP * Z)


def z_scale():
    return np.where(np.arange(KZ) == 0, 1.0, 2.0) / float(X * Y * Z)


def tall(table):
    return np.concatenate(split(table), axis=0)


def by_half(table):
    rows = table.shape[0] // 2
    return np.stack([tall(table[:rows]), tall(table[rows:])])


def wide3(table):
    high, low = split(table)
    return np.concatenate([high, low, high], axis=1)


def y_forward():
    return forward_table(Y, KY).reshape(2 * KY, Y * 2)


def x_forward():
    table = forward_table(X, KX).reshape(2 * KX, X // ROWS, ROWS, 2)
    return table.transpose(0, 1, 3, 2).reshape(2 * KX, X * 2)


def nt(left, right):
    return lax.dot_general(left, right, (((1,), (1,)), ((), ())), preferred_element_type=f32)


def tn(left, right):
    return lax.dot_general(left, right, (((0,), (0,)), ((), ())), preferred_element_type=f32)


def nn(left, right):
    return jnp.dot(left, right, preferred_element_type=f32)


def halves(values):
    high = values.astype(bf16)
    low = (values - high.astype(f32)).astype(bf16)
    return high, low


def cells(ref, block):
    return ref[:, :, pl.ds(pl.multiple_of(block * GROUP * Z, GROUP * Z), GROUP * Z)].reshape(
        ROWS * C, GROUP * Z
    )


def z_forward(values, table, q_ref, block, h):
    rows = KZ * GROUP
    both = nt(table, values)
    part = both[:rows] + both[rows:]
    q_ref[h * KZ // 2 : (h + 1) * KZ // 2, pl.ds(pl.multiple_of(block * 8, 8), 8), :] = (
        part.reshape(KZ // 2, 8, ROWS * C)
    )


def y_to_message(q_ref, dy_ref, o_ref, msg_ref, h):
    table = dy_ref[...]
    span = range(h * KZ // 2, (h + 1) * KZ // 2)
    for kz in span:
        both = nn(table, q_ref[kz].astype(bf16))
        o_ref[kz] = both[: 2 * KY] + both[2 * KY :]
    first, count = chunk_tiles(h)
    for ri in range(2):
        for x in range(ROWS):
            row = jnp.concatenate(
                [o_ref[kz, ri * KY : (ri + 1) * KY, x * C : (x + 1) * C] for kz in span], axis=1
            )
            for t in range(count):
                msg_ref[first + t, pl.ds(ri * ROWS + x, KY, stride=8), :] = row[
                    :, t * LANES : (t + 1) * LANES
                ]


def message_to_y(rb_ref, ey_ref, b_ref, q_ref, h):
    first, count = chunk_tiles(h)
    span = range(h * KZ // 2, (h + 1) * KZ // 2)
    for kz in span if ROWS * C < b_ref.shape[2] else ():
        b_ref[kz, :, ROWS * C :] = jnp.zeros((2 * KY, b_ref.shape[2] - ROWS * C), f32)
    for ri in range(2):
        for x in range(ROWS):
            row = jnp.concatenate(
                [
                    rb_ref[first + t, pl.ds(ri * ROWS + x, KY, stride=8), :]
                    for t in range(count)
                ],
                axis=1,
            )
            for i, kz in enumerate(span):
                b_ref[kz, ri * KY : (ri + 1) * KY, x * C : (x + 1) * C] = row[
                    :, i * C : (i + 1) * C
                ]
    table = ey_ref[...]
    for kz in span:
        high, low = halves(b_ref[kz])
        q_ref[kz] = nn(table, jnp.concatenate([high, high, low], axis=0))


def z_backward(q_ref, table, block):
    part = q_ref[:, pl.ds(pl.multiple_of(block * 8, 8), 8), :]
    part = part.reshape(KZ * 8, q_ref.shape[2])
    turned = part.T[: ROWS * C].astype(bf16)
    return nn(jnp.concatenate([turned, turned], axis=1), table)


def chunk_tiles(h):
    count = KZ * C // LANES // 2
    return h * count, count


def gelu_slope(values):
    size = jnp.abs(values)
    bell = jnp.exp(values * values * -0.5)
    t = 1.0 / (1.0 + (0.3275911 * 0.7071067811865476) * size)
    poly = 0.5 * 1.061405429
    poly = poly * t + 0.5 * -1.453152027
    poly = poly * t + 0.5 * 1.421413741
    poly = poly * t + 0.5 * -0.284496736
    poly = poly * t + 0.5 * 0.254829592
    tail = poly * t * bell
    cumul = jnp.where(values >= 0.0, 1.0 - tail, tail)
    return cumul + values * bell * 0.3989422804014327


def local_matrix(weights):
    rows = []
    for x in range(ROWS):
        parts = [weights]
        if x:
            parts = [jnp.zeros((C, x * C), f32)] + parts
        if x < ROWS - 1:
            parts = parts + [jnp.zeros((C, (ROWS - 1 - x) * C), f32)]
        rows.append(jnp.concatenate(parts, axis=1))
    return jnp.concatenate(rows, axis=0).astype(bf16)


def last_kernel(
    rb_ref, s_ref, wl_ref, ey_ref, bdzs_ref, gs_ref, gl_ref,
    out_ref, gs_out, gl_out, b_ref, q2_ref, mix_ref,
):
    part = pl.program_id(0)
    gs_out[...] = gs_ref[...]
    blocks = s_ref.shape[2] // (GROUP * Z)

    @pl.when(part == 0)
    def _():
        gl_out[...] = gl_ref[...]
        mix_ref[...] = local_matrix(wl_ref[...].astype(f32))
        for h in range(2):
            message_to_y(rb_ref, ey_ref, b_ref, q2_ref, h)

    synth = bdzs_ref[...]
    mixing = mix_ref[...]

    def step(block, carry):
        values = cells(s_ref, block)
        total = z_backward(q2_ref, synth, part * blocks + block) + nn(mixing, values)
        out_ref[:, :, pl.ds(pl.multiple_of(block * GROUP * Z, GROUP * Z), GROUP * Z)] = (
            total.astype(bf16).reshape(ROWS, C, GROUP * Z)
        )
        return carry

    lax.fori_loop(0, blocks, step, 0, unroll=True)


def others(axis, count, body):
    me = lax.axis_index(axis)

    def step(k, carry):
        body(lax.rem(me + k, count))
        return carry

    lax.fori_loop(1, count, step, 0)


def enter(n, d):
    barrier = pltpu.get_barrier_semaphore()
    for axis, count in (("pencil", n), ("dp", d)):
        others(
            axis,
            count,
            lambda j, axis=axis: pl.semaphore_signal(
                barrier, inc=1, device_id={axis: j}, device_id_type=MESH
            ),
        )
    return barrier


def remote(src, dst, sems, kind, mine, axis, j):
    return pltpu.make_async_remote_copy(
        src_ref=src,
        dst_ref=dst,
        send_sem=sems.at[2 * kind, j],
        recv_sem=sems.at[2 * kind + 1, mine],
        device_id={axis: j},
        device_id_type=MESH,
    )


def wait_one(view, sem):
    pltpu.make_async_copy(view, view, sem).wait()


def arrived(view, sems, kind, axis, count):
    others(axis, count, lambda j: wait_one(view(j), sems.at[2 * kind + 1, j]))


def sent(view, sems, kind, axis, count):
    others(axis, count, lambda j: wait_one(view(j), sems.at[2 * kind, j]))


def piece(ref, h):
    first, count = chunk_tiles(h)
    return lambda j: ref.at[pl.ds(first, count), pl.ds(pl.multiple_of(j * 8, 8), 8), :]


def modes(ref):
    return lambda j: ref.at[pl.ds(pl.multiple_of(j * 2 * KX, 2 * KX), 2 * KX), :]


def swap(src, dst, sems, kind, axis, count):
    me = lax.axis_index(axis)
    others(axis, count, lambda j: remote(src(j), dst(me), sems, kind, me, axis, j).start())


def send_chunk(n, src_ref, dst_ref, sems, kind, h, own_sem=None):
    me = lax.axis_index("pencil")
    src, dst = piece(src_ref, h), piece(dst_ref, h)

    def send(j):
        pltpu.make_async_remote_copy(
            src_ref=src(j),
            dst_ref=dst(me),
            send_sem=sems.at[2 * kind],
            recv_sem=sems.at[2 * kind + 1],
            device_id={"pencil": j},
            device_id_type=MESH,
        ).start()

    others("pencil", n, send)
    if own_sem is not None:
        pltpu.make_async_copy(src(me), dst(me), own_sem).start()
        return
    first, count = chunk_tiles(h)
    mine = pl.ds(pl.multiple_of(me * 8, 8), 8)
    dst_ref[first : first + count, mine, :] = src_ref[first : first + count, mine, :]


def planes_wait(n, ref, sems, kind, h, received):
    first, count = chunk_tiles(h)
    wait_one(
        ref.at[pl.ds(first, count), pl.ds(0, (n - 1) * 8), :], sems.at[2 * kind + int(received)]
    )


def x_analyse(r_ref, dx_ref, g_ref, d, h):
    first, count = chunk_tiles(h)
    high, low = halves(jnp.concatenate([r_ref[first + t] for t in range(count)], axis=1))
    table = dx_ref[...]
    both = nn(table, high)
    spectrum = both[: 2 * KX] + both[2 * KX :] + nn(table[: 2 * KX], low)
    width = KZ * C // d
    for i in range(d // 2):
        j = owner_order(d)[h * d // 2 + i]
        part = spectrum[:, i * width : (i + 1) * width]
        if width < LANES:
            part = jnp.concatenate([part, jnp.zeros((2 * KX, LANES - width), f32)], axis=1)
        g_ref[j * 2 * KX : (j + 1) * 2 * KX, :] = part


def x_synth(h_ref, ex_ref, mb_ref, d, h):
    width = KZ * C // d
    spectrum = jnp.concatenate(
        [
            h_ref[j * 2 * KX : (j + 1) * 2 * KX, 0:width]
            for j in owner_order(d)[h * d // 2 : (h + 1) * d // 2]
        ],
        axis=1,
    )
    high, low = halves(spectrum)
    rows = nn(ex_ref[...], jnp.concatenate([high, high, low], axis=0))
    first, count = chunk_tiles(h)
    for t in range(count):
        mb_ref[first + t] = rows[:, t * LANES : (t + 1) * LANES]


def pick(ref, kx, d):
    real = ref[pl.ds(kx, d, stride=2 * KX), :]
    imag = ref[pl.ds(KX + kx, d, stride=2 * KX), :]
    return real, imag


def stage_weights(w_ref, w5_ref, wc_ref):
    for ri in range(2):
        for kz in range(2):
            for c in range(C):
                part = w_ref[ri, 0, kz, :, c * C : (c + 1) * C]
                parts = [part]
                if kz:
                    parts = [jnp.zeros((KX, C), f32), part]
                rest = LANES - C * len(parts)
                if rest:
                    parts = parts + [jnp.zeros((KX, rest), f32)]
                w5_ref[ri, kz, pl.ds(c, KX, stride=C), :] = jnp.concatenate(parts, axis=1)

    def pack(kx, carry):
        rows = pl.ds(pl.multiple_of(kx * C, 8), C)
        for ri in range(2):
            parts = [w5_ref[ri, 0, rows, :], w5_ref[ri, 1, rows, :]]
            if LANES > 2 * C:
                parts.append(jnp.zeros((LANES - 2 * C, LANES), f32))
            high, low = halves(jnp.concatenate(parts, axis=0))
            wc_ref[kx, 0:LANES, ri * LANES : (ri + 1) * LANES] = high
            wc_ref[kx, LANES : 2 * LANES, ri * LANES : (ri + 1) * LANES] = low
        return carry

    lax.fori_loop(0, KX, pack, 0)


def mix_modes(h_ref, wc_ref, g2_ref, d):
    def mix(kx, carry):
        real, imag = pick(h_ref, kx, d)
        high, low = halves(jnp.concatenate([real, imag], axis=0))
        left = jnp.concatenate(
            [
                jnp.concatenate([high, high], axis=1),
                jnp.concatenate([low, jnp.zeros_like(low)], axis=1),
            ],
            axis=0,
        )
        both = nn(left, wc_ref[kx])
        both = both[: 2 * d] + both[2 * d :]
        g2_ref[pl.ds(kx, d, stride=2 * KX), :] = both[:d, :LANES] - both[d:, LANES:]
        g2_ref[pl.ds(KX + kx, d, stride=2 * KX), :] = both[:d, LANES:] + both[d:, :LANES]
        return carry

    lax.fori_loop(0, KX, mix, 0, unroll=16)


def stacked(h_ref, kx, d):
    real, imag = pick(h_ref, kx, d)
    return halves(
        jnp.concatenate(
            [
                jnp.concatenate([real, imag], axis=1),
                jnp.concatenate([imag, -real], axis=1),
            ],
            axis=0,
        )
    )


def adjoint_modes(h_ref, wc_ref, g2_ref, d):
    def adjoint(kx, carry):
        high, low = stacked(h_ref, kx, d)
        both = nt(jnp.concatenate([high, low], axis=0), wc_ref[kx])
        total = both[: 2 * d, :LANES] + both[: 2 * d, LANES:] + both[2 * d :, :LANES]
        g2_ref[pl.ds(kx, d, stride=2 * KX), :] = total[:d]
        g2_ref[pl.ds(KX + kx, d, stride=2 * KX), :] = total[d:]
        return carry

    lax.fori_loop(0, KX, adjoint, 0, unroll=16)


def weight_grad(spec_ref, grad_ref, w5_ref, out_ref, d):
    def one(kx, carry):
        high, low = stacked(grad_ref, kx, d)
        real, imag = pick(spec_ref, kx, d)
        shigh, slow = halves(jnp.concatenate([real, imag], axis=0))
        product = tn(
            jnp.concatenate([shigh, slow, shigh], axis=0),
            jnp.concatenate([high, high, low], axis=0),
        )
        rows = pl.ds(pl.multiple_of(kx * C, 8), C)
        for ri in range(2):
            for kz in range(2):
                w5_ref[ri, kz, rows, :] = product[
                    kz * C : (kz + 1) * C, ri * LANES : (ri + 1) * LANES
                ]
        return carry

    lax.fori_loop(0, KX, one, 0, unroll=4)
    group = 8
    for ri in range(2):
        for kz in range(2):
            for first in range(0, C, group):
                out_ref[ri, 0, kz, :, first * C : (first + group) * C] = jnp.concatenate(
                    [
                        w5_ref[ri, kz, pl.ds(c, KX, stride=C), :][:, kz * C : (kz + 1) * C]
                        for c in range(first, first + group)
                    ],
                    axis=1,
                )


def mode_round(n, d, bufs, tables, psem, dsem, base, between, mixer, extra, own_sem=None):
    r_ref, g_ref, h_ref, g2_ref, h2_ref, mb_ref, rb_ref = bufs
    dx_ref, ex_ref = tables
    sample = lax.axis_index("dp")
    out, back = base // 2, base // 2 + 1
    own = pl.ds(pl.multiple_of(sample * 2 * KX, 2 * KX), 2 * KX)

    def forward(h):
        planes_wait(n, r_ref, psem, base + h, h, True)
        x_analyse(r_ref, dx_ref, g_ref, d, h)

        def to_owner(j):
            @pl.when(half_of(j, d) == h)
            def _():
                remote(modes(g_ref)(j), modes(h_ref)(sample), dsem, out, sample, "dp", j).start()

        others("dp", d, to_owner)

    def mix(h):
        @pl.when(half_of(sample, d) == h)
        def _():
            h_ref[own, :] = g_ref[own, :]
            arrived(modes(h_ref), dsem, out, "dp", d)
            mixer(h_ref, g2_ref)
            swap(modes(g2_ref), modes(h2_ref), dsem, back, "dp", d)
            h2_ref[own, :] = g2_ref[own, :]

    def backward(h):
        def from_owner(j):
            @pl.when(half_of(j, d) == h)
            def _():
                wait_one(modes(h2_ref)(j), dsem.at[2 * back + 1, j])

        others("dp", d, from_owner)
        x_synth(h2_ref, ex_ref, mb_ref, d, h)
        send_chunk(
            n, mb_ref, rb_ref, psem, base + 2 + h, h, None if own_sem is None else own_sem.at[h]
        )

    between()
    forward(0)
    mix(0)
    forward(1)
    extra()
    backward(0)
    mix(1)
    backward(1)


def main_kernel(
    n, d,
    x_hbm, go_hbm, w_hbm, wl_ref, bdz_ref, bdzs_ref, bdzg_ref, dy_ref, ey_ref, dx_ref, ex_ref,
    s_hbm, rb_hbm, gs_hbm, gl_hbm,
    x_ref, go_ref, s_ref, p_ref, gs_ref, glo_ref, w_ref, w5_ref, wc_ref, q_ref, q2_ref, o_ref, b_ref,
    msg1_ref, r1_ref, g1_ref, h1_ref, g21_ref, h21_ref, mb1_ref, rb1_ref,
    msg2_ref, r2_ref, g2_ref, h2_ref, g22_ref, h22_ref, mb2_ref,
    gl_ref, glr_ref, glp_ref, gld_ref, glt_ref, glf_ref,
    psem, dsem, qsem, esem, load_sem,
):
    me, sample = lax.axis_index("pencil"), lax.axis_index("dp")
    tiles = C // 8
    keeper = me < tiles
    blocks = Y // GROUP
    parts = 4
    width = Y * Z // parts
    barrier = enter(n, d)
    loads = []
    for i in range(parts):
        view = (slice(None), slice(None), pl.ds(i * width, width))
        loads.append(
            pltpu.make_async_copy(x_hbm.at[view], x_ref.at[view], load_sem.at[i])
        )
    loads.append(pltpu.make_async_copy(w_hbm, w_ref, load_sem.at[parts]))
    loads.append(pltpu.make_async_copy(go_hbm, go_ref, load_sem.at[parts + 1]))
    for load in loads:
        load.start()
    mixing = local_matrix(wl_ref[...].astype(f32).T)

    def strip(block):
        return pl.ds(pl.multiple_of(block * GROUP * Z, GROUP * Z), GROUP * Z)

    def analyse(values_ref, table_ref, h, first, last):
        def one(block, carry):
            z_forward(cells(values_ref, block), table_ref[h], q_ref, block, h)
            return carry

        lax.fori_loop(first, last, one, 0, unroll=8)

    for h in range(2):
        for i in range(parts):
            if h == 0:
                loads[i].wait()
            analyse(x_ref, bdz_ref, h, i * blocks // parts, (i + 1) * blocks // parts)
        y_to_message(q_ref, dy_ref, o_ref, msg1_ref, h)
        if h == 0:
            pl.semaphore_wait(barrier, n + d - 2)
        send_chunk(n, msg1_ref, r1_ref, psem, h, h)

    def stage():
        def product(block, carry):
            p_ref[:, strip(block)] = nn(mixing, cells(x_ref, block))
            return carry

        lax.fori_loop(0, blocks, product, 0, unroll=8)
        loads[parts].wait()
        stage_weights(w_ref, w5_ref, wc_ref)

    mode_round(
        n, d,
        (r1_ref, g1_ref, h1_ref, g21_ref, h21_ref, mb1_ref, rb1_ref),
        (dx_ref, ex_ref), psem, dsem, 0, stage,
        lambda src, dst: mix_modes(src, wc_ref, dst, d),
        lambda: None,
    )
    loads[parts + 1].wait()
    for h in range(2):
        planes_wait(n, rb1_ref, psem, 2 + h, h, True)
        message_to_y(rb1_ref, ey_ref, b_ref, q2_ref, h)
    synth = bdzs_ref[...]

    def slopes(block, carry):
        preact = p_ref[:, strip(block)] + z_backward(q2_ref, synth, block)
        half = (cells(go_ref, block).astype(f32) * gelu_slope(preact)).astype(bf16)
        s_ref[:, :, strip(block)] = half.reshape(ROWS, C, GROUP * Z)
        return carry

    lax.fori_loop(0, blocks, slopes, 0, unroll=8)
    for h in range(2):
        analyse(s_ref, bdzg_ref, h, 0, blocks)
        y_to_message(q_ref, dy_ref, o_ref, msg2_ref, h)
        send_chunk(n, msg2_ref, r2_ref, psem, 4 + h, h)
    store = pltpu.make_async_copy(s_ref, s_hbm, load_sem.at[0])
    store.start()

    def local_sum():
        gl_ref[...] = jnp.zeros_like(gl_ref)
        total = nt(x_ref[0], s_ref[0])
        for x in range(1, ROWS):
            total = total + nt(x_ref[x], s_ref[x])
        gl_ref[:, :, 0:C] = total.reshape(tiles, 8, C)

        def to_keeper(j):
            @pl.when(j < tiles)
            def _():
                remote(gl_ref.at[j], glr_ref.at[me], qsem, 0, me, "pencil", j).start()

        others("pencil", n, to_keeper)

    def local_reduce():
        @pl.when(keeper)
        def _():
            glr_ref[me] = gl_ref[me]
            arrived(lambda j: glr_ref.at[j], qsem, 0, "pencil", n)
            glp_ref[...] = jnp.sum(glr_ref[...], axis=0)
            others(
                "dp",
                d,
                lambda j: remote(glp_ref, gld_ref.at[sample], esem, 0, sample, "dp", j).start(),
            )
            gld_ref[sample] = glp_ref[...]

    def local_spread():
        @pl.when(keeper)
        def _():
            arrived(lambda j: gld_ref.at[j], esem, 0, "dp", d)
            glt_ref[...] = jnp.sum(gld_ref[...], axis=0)
            others(
                "pencil",
                n,
                lambda j: remote(glt_ref, glf_ref.at[me], qsem, 1, me, "pencil", j).start(),
            )
            glf_ref[me] = glt_ref[...]

    mode_round(
        n, d,
        (r2_ref, g2_ref, h2_ref, g22_ref, h22_ref, mb2_ref, rb_hbm),
        (dx_ref, ex_ref), psem, dsem, 4, local_sum,
        lambda src, dst: adjoint_modes(src, wc_ref, dst, d),
        local_reduce,
        load_sem.at[pl.ds(1, 2)],
    )
    local_spread()
    weight_grad(h1_ref, h2_ref, w5_ref, gs_ref, d)
    stores = [
        pltpu.make_async_copy(gs_ref, gs_hbm, load_sem.at[3]),
        pltpu.make_async_copy(glo_ref, gl_hbm, load_sem.at[4]),
    ]
    stores[0].start()
    for base, (first, modes1, modes2, second) in (
        (0, (msg1_ref, g1_ref, g21_ref, mb1_ref)),
        (4, (msg2_ref, g2_ref, g22_ref, mb2_ref)),
    ):
        for h in range(2):
            planes_wait(n, first, psem, base + h, h, False)
            planes_wait(n, second, psem, base + 2 + h, h, False)
        sent(modes(modes1), dsem, base // 2, "dp", d)
        sent(modes(modes2), dsem, base // 2 + 1, "dp", d)

    def keeper_sent(j):
        @pl.when(j < tiles)
        def _():
            wait_one(gl_ref.at[j], qsem.at[0, j])
            wait_one(glf_ref.at[j], qsem.at[3, j])

    others("pencil", n, keeper_sent)
    glo_ref[...] = glf_ref[...].reshape(C, LANES)[:, :C]
    stores[1].start()

    @pl.when(keeper)
    def _():
        sent(lambda j: glp_ref, esem, 0, "dp", d)
        sent(lambda j: glt_ref, qsem, 1, "pencil", n)

    store.wait()
    for one in stores:
        one.wait()
    for h in range(2):
        own = piece(mb2_ref, h)(me)
        pltpu.make_async_copy(own, piece(rb_hbm, h)(me), load_sem.at[1 + h]).wait()
        planes_wait(n, rb_hbm, psem, 6 + h, h, True)


def params(**extra):
    return {
        "compiler_params": pltpu.CompilerParams(vmem_limit_bytes=LIMIT, **extra),
        "cost_estimate": pl.CostEstimate(
            flops=1_000_000_000, bytes_accessed=4_000_000, transcendentals=0
        ),
    }


def local(n, d, field_in, grad_out, w_spec, w_local):
    sds = jax.ShapeDtypeStruct
    lane_tiles = KZ * C // LANES
    values, upstream = field_in[0], grad_out[0]
    cells_shape = values.shape
    ones = np.ones((KZ,))
    scale = z_scale()
    bdz = by_half(z_table(ones, d))
    bdz_grad = by_half(z_table(scale, d))
    synth = tall(z_table(scale, d))
    synth_plain = tall(z_table(ones, d))
    dy = tall(y_forward())
    ey = wide3(y_forward().T)
    dx = tall(x_forward())
    ex = wide3(x_forward().T)

    message = sds((lane_tiles, n * 8, LANES), f32)
    q_shape = pltpu.VMEM((KZ, Y * 2, ROWS * C), f32)
    q2_shape = pltpu.VMEM((KZ, Y * 2, 2 * LANES), f32)
    o_shape = pltpu.VMEM((KZ, 2 * KY, ROWS * C), f32)
    b_shape = pltpu.VMEM((KZ, 2 * KY, 2 * LANES), f32)
    mode_shape = pltpu.VMEM((d * 2 * KX, LANES), f32)
    message_shape = pltpu.VMEM((lane_tiles, n * 8, LANES), f32)
    exchange = [message_shape] * 2 + [mode_shape] * 4 + [message_shape] * 2
    tile = pltpu.VMEM((8, LANES), f32)
    tile_count = C // 8
    anywhere = pl.BlockSpec(memory_space=pl.ANY)
    vmem = pl.BlockSpec(memory_space=pltpu.VMEM)
    slopes, rb, grad_spec, grad_local = pl.pallas_call(
        functools.partial(main_kernel, n, d),
        out_shape=(
            sds(cells_shape, bf16),
            message,
            sds(w_spec.shape, f32),
            sds((C, C), f32),
        ),
        in_specs=[anywhere] * 3 + [vmem] * 8,
        out_specs=(anywhere,) * 4,
        scratch_shapes=[
            pltpu.VMEM(cells_shape, bf16),
            pltpu.VMEM(cells_shape, bf16),
            pltpu.VMEM(cells_shape, bf16),
            pltpu.VMEM((ROWS * C, Y * Z), f32),
            pltpu.VMEM(w_spec.shape, f32),
            pltpu.VMEM((C, C), f32),
            pltpu.VMEM(w_spec.shape, f32),
            pltpu.VMEM((2, 2, KX * C, LANES), f32),
            pltpu.VMEM((KX, 2 * LANES, 2 * LANES), bf16),
            q_shape,
            q2_shape,
            o_shape,
            b_shape,
        ]
        + exchange + exchange[:-1]
        + [
            pltpu.VMEM((tile_count, 8, LANES), f32),
            pltpu.VMEM((n, 8, LANES), f32),
            tile,
            pltpu.VMEM((d, 8, LANES), f32),
            tile,
            pltpu.VMEM((tile_count, 8, LANES), f32),
            pltpu.SemaphoreType.DMA((16,)),
            pltpu.SemaphoreType.DMA((8, d)),
            pltpu.SemaphoreType.DMA((4, n)),
            pltpu.SemaphoreType.DMA((2, d)),
            pltpu.SemaphoreType.DMA((6,)),
        ],
        name="spectral_backward",
        **params(collective_id=0, has_side_effects=True),
    )(values, upstream, w_spec, w_local, bdz, synth, bdz_grad, dy, ey, dx, ex)
    parts = 4
    strip = pl.BlockSpec((ROWS, C, Y * Z // parts), lambda i: (0, 0, i))
    whole = pl.BlockSpec(memory_space=pltpu.VMEM)
    modes_strip = pl.BlockSpec(
        w_spec.shape[:3] + (KX // parts, C * C), lambda i: (0, 0, 0, i, 0)
    )
    grad_in, grad_spec, grad_local = pl.pallas_call(
        last_kernel,
        out_shape=(sds(cells_shape, bf16), sds(w_spec.shape, f32), sds((C, C), f32)),
        grid=(parts,),
        in_specs=[whole, strip, whole, whole, whole, modes_strip, whole],
        out_specs=(strip, modes_strip, whole),
        scratch_shapes=[b_shape, q2_shape, pltpu.VMEM((ROWS * C, ROWS * C), bf16)],
        name="plane_synthesis",
        **params(),
    )(rb, slopes, w_local, ey, synth_plain, grad_spec, grad_local)
    return grad_in[None], grad_spec, grad_local


def solution(mesh):
    n, d = mesh.shape["pencil"], mesh.shape["dp"]
    placed = (
        P("dp", "pencil", None, None),
        P("dp", "pencil", None, None),
        P(None, "pencil", "dp", None, None),
        P(),
    )
    return jax.shard_map(
        functools.partial(local, n, d),
        mesh=mesh,
        in_specs=placed,
        out_specs=(P("dp", "pencil", None, None), P(None, "pencil", "dp", None, None), P()),
        check_vma=False,
    )
```

```python
import functools

import jax
import jax.numpy as jnp
import ml_dtypes
import numpy as np
from jax import lax
from jax.experimental import pallas as pl
from jax.experimental.pallas import tpu as pltpu
from jax.sharding import PartitionSpec as P

X = 128
Y = 128
Z = 64
C = 48
KX = 32
KY = 32
KZ = 16
ROWS = 4
GROUP = 4
LANES = 128
LIMIT = 56 * 1024 * 1024

MESH = pl.DeviceIdType.MESH
f32 = jnp.float32
bf16 = jnp.bfloat16


def split(table):
    high = table.astype(np.float32).astype(ml_dtypes.bfloat16)
    low = (table - high.astype(np.float64)).astype(np.float32).astype(ml_dtypes.bfloat16)
    return high, low


def signed(count):
    freqs = np.arange(count)
    return np.where(freqs < count // 2, freqs, freqs - count)


def forward_table(length, count):
    angles = 2.0 * np.pi * (np.outer(signed(count), np.arange(length)) % length) / length
    cos, sin = np.cos(angles), np.sin(angles)
    table = np.zeros((2, count, length, 2))
    table[0, :, :, 0] = cos
    table[0, :, :, 1] = sin
    table[1, :, :, 0] = -sin
    table[1, :, :, 1] = cos
    return table.reshape(2 * count, length, 2)


def half_of(sample, d):
    return (sample // max(d // 4, 1)) % 2


def owner_order(d):
    return sorted(range(d), key=lambda j: (half_of(j, d), j))


def kz_order(d):
    return np.array([2 * j + k for j in owner_order(d) for k in range(2)])


def z_table(scale, d):
    order = kz_order(d)
    scale = scale[order]
    angles = 2.0 * np.pi * (np.outer(order, np.arange(Z)) % Z) / Z
    table = np.zeros((KZ, GROUP, 2, GROUP, Z))
    for place in range(GROUP):
        table[:, place, 0, place] = np.cos(angles) * scale[:, None]
        table[:, place, 1, place] = -np.sin(angles) * scale[:, None]
    return table.reshape(KZ * GROUP * 2, GROUP * Z)


def z_scale():
    return np.where(np.arange(KZ) == 0, 1.0, 2.0) / float(X * Y * Z)


def tall(table):
    return np.concatenate(split(table), axis=0)


def by_half(table):
    rows = table.shape[0] // 2
    return np.stack([tall(table[:rows]), tall(table[rows:])])


def wide3(table):
    high, low = split(table)
    return np.concatenate([high, low, high], axis=1)


def y_forward():
    return forward_table(Y, KY).reshape(2 * KY, Y * 2)


def x_forward():
    table = forward_table(X, KX).reshape(2 * KX, X // ROWS, ROWS, 2)
    return table.transpose(0, 1, 3, 2).reshape(2 * KX, X * 2)


def nt(left, right):
    return lax.dot_general(left, right, (((1,), (1,)), ((), ())), preferred_element_type=f32)


def tn(left, right):
    return lax.dot_general(left, right, (((0,), (0,)), ((), ())), preferred_element_type=f32)


def nn(left, right):
    return jnp.dot(left, right, preferred_element_type=f32)


def halves(values):
    high = values.astype(bf16)
    low = (values - high.astype(f32)).astype(bf16)
    return high, low


def cells(ref, block):
    return ref[:, :, pl.ds(pl.multiple_of(block * GROUP * Z, GROUP * Z), GROUP * Z)].reshape(
        ROWS * C, GROUP * Z
    )


def z_forward(values, table, q_ref, block, h):
    rows = KZ * GROUP
    both = nt(table, values)
    part = both[:rows] + both[rows:]
    q_ref[h * KZ // 2 : (h + 1) * KZ // 2, pl.ds(pl.multiple_of(block * 8, 8), 8), :] = (
        part.reshape(KZ // 2, 8, ROWS * C)
    )


def y_to_message(q_ref, dy_ref, o_ref, msg_ref, h):
    table = dy_ref[...]
    span = range(h * KZ // 2, (h + 1) * KZ // 2)
    for kz in span:
        both = nn(table, q_ref[kz].astype(bf16))
        o_ref[kz] = both[: 2 * KY] + both[2 * KY :]
    first, count = chunk_tiles(h)
    for ri in range(2):
        for x in range(ROWS):
            row = jnp.concatenate(
                [o_ref[kz, ri * KY : (ri + 1) * KY, x * C : (x + 1) * C] for kz in span], axis=1
            )
            for t in range(count):
                msg_ref[first + t, pl.ds(ri * ROWS + x, KY, stride=8), :] = row[
                    :, t * LANES : (t + 1) * LANES
                ]


def message_to_y(rb_ref, ey_ref, b_ref, q_ref, h):
    first, count = chunk_tiles(h)
    span = range(h * KZ // 2, (h + 1) * KZ // 2)
    for kz in span if ROWS * C < b_ref.shape[2] else ():
        b_ref[kz, :, ROWS * C :] = jnp.zeros((2 * KY, b_ref.shape[2] - ROWS * C), f32)
    for ri in range(2):
        for x in range(ROWS):
            row = jnp.concatenate(
                [
                    rb_ref[first + t, pl.ds(ri * ROWS + x, KY, stride=8), :]
                    for t in range(count)
                ],
                axis=1,
            )
            for i, kz in enumerate(span):
                b_ref[kz, ri * KY : (ri + 1) * KY, x * C : (x + 1) * C] = row[
                    :, i * C : (i + 1) * C
                ]
    table = ey_ref[...]
    for kz in span:
        high, low = halves(b_ref[kz])
        q_ref[kz] = nn(table, jnp.concatenate([high, high, low], axis=0))


def z_backward(q_ref, table, block):
    part = q_ref[:, pl.ds(pl.multiple_of(block * 8, 8), 8), :]
    part = part.reshape(KZ * 8, q_ref.shape[2])
    turned = part.T[: ROWS * C].astype(bf16)
    return nn(jnp.concatenate([turned, turned], axis=1), table)


def chunk_tiles(h):
    count = KZ * C // LANES // 2
    return h * count, count


def gelu_slope(values):
    size = jnp.abs(values)
    bell = jnp.exp(values * values * -0.5)
    t = 1.0 / (1.0 + (0.3275911 * 0.7071067811865476) * size)
    poly = 0.5 * 1.061405429
    poly = poly * t + 0.5 * -1.453152027
    poly = poly * t + 0.5 * 1.421413741
    poly = poly * t + 0.5 * -0.284496736
    poly = poly * t + 0.5 * 0.254829592
    tail = poly * t * bell
    cumul = jnp.where(values >= 0.0, 1.0 - tail, tail)
    return cumul + values * bell * 0.3989422804014327


def local_matrix(weights):
    rows = []
    for x in range(ROWS):
        parts = [weights]
        if x:
            parts = [jnp.zeros((C, x * C), f32)] + parts
        if x < ROWS - 1:
            parts = parts + [jnp.zeros((C, (ROWS - 1 - x) * C), f32)]
        rows.append(jnp.concatenate(parts, axis=1))
    return jnp.concatenate(rows, axis=0).astype(bf16)


def last_kernel(
    rb_ref, s_ref, wl_ref, ey_ref, bdzs_ref, gs_ref, gl_ref,
    out_ref, gs_out, gl_out, b_ref, q2_ref, mix_ref,
):
    part = pl.program_id(0)
    gs_out[...] = gs_ref[...]
    blocks = s_ref.shape[2] // (GROUP * Z)

    @pl.when(part == 0)
    def _():
        gl_out[...] = gl_ref[...]
        mix_ref[...] = local_matrix(wl_ref[...].astype(f32))
        for h in range(2):
            message_to_y(rb_ref, ey_ref, b_ref, q2_ref, h)

    synth = bdzs_ref[...]
    mixing = mix_ref[...]

    def step(block, carry):
        values = cells(s_ref, block)
        total = z_backward(q2_ref, synth, part * blocks + block) + nn(mixing, values)
        out_ref[:, :, pl.ds(pl.multiple_of(block * GROUP * Z, GROUP * Z), GROUP * Z)] = (
            total.astype(bf16).reshape(ROWS, C, GROUP * Z)
        )
        return carry

    lax.fori_loop(0, blocks, step, 0, unroll=True)


def others(axis, count, body):
    me = lax.axis_index(axis)

    def step(k, carry):
        body(lax.rem(me + k, count))
        return carry

    lax.fori_loop(1, count, step, 0)


def enter(n, d):
    barrier = pltpu.get_barrier_semaphore()
    for axis, count in (("pencil", n), ("dp", d)):
        others(
            axis,
            count,
            lambda j, axis=axis: pl.semaphore_signal(
                barrier, inc=1, device_id={axis: j}, device_id_type=MESH
            ),
        )
    return barrier


def remote(src, dst, sems, kind, mine, axis, j):
    return pltpu.make_async_remote_copy(
        src_ref=src,
        dst_ref=dst,
        send_sem=sems.at[2 * kind, j],
        recv_sem=sems.at[2 * kind + 1, mine],
        device_id={axis: j},
        device_id_type=MESH,
    )


def wait_one(view, sem):
    pltpu.make_async_copy(view, view, sem).wait()


def arrived(view, sems, kind, axis, count):
    others(axis, count, lambda j: wait_one(view(j), sems.at[2 * kind + 1, j]))


def sent(view, sems, kind, axis, count):
    others(axis, count, lambda j: wait_one(view(j), sems.at[2 * kind, j]))


def piece(ref, h):
    first, count = chunk_tiles(h)
    return lambda j: ref.at[pl.ds(first, count), pl.ds(pl.multiple_of(j * 8, 8), 8), :]


def modes(ref):
    return lambda j: ref.at[pl.ds(pl.multiple_of(j * 2 * KX, 2 * KX), 2 * KX), :]


def swap(src, dst, sems, kind, axis, count):
    me = lax.axis_index(axis)
    others(axis, count, lambda j: remote(src(j), dst(me), sems, kind, me, axis, j).start())


def send_chunk(n, src_ref, dst_ref, sems, kind, h, own_sem=None):
    me = lax.axis_index("pencil")
    src, dst = piece(src_ref, h), piece(dst_ref, h)

    def send(j):
        pltpu.make_async_remote_copy(
            src_ref=src(j),
            dst_ref=dst(me),
            send_sem=sems.at[2 * kind],
            recv_sem=sems.at[2 * kind + 1],
            device_id={"pencil": j},
            device_id_type=MESH,
        ).start()

    others("pencil", n, send)
    if own_sem is not None:
        pltpu.make_async_copy(src(me), dst(me), own_sem).start()
        return
    first, count = chunk_tiles(h)
    mine = pl.ds(pl.multiple_of(me * 8, 8), 8)
    dst_ref[first : first + count, mine, :] = src_ref[first : first + count, mine, :]


def planes_wait(n, ref, sems, kind, h, received):
    first, count = chunk_tiles(h)
    wait_one(
        ref.at[pl.ds(first, count), pl.ds(0, (n - 1) * 8), :], sems.at[2 * kind + int(received)]
    )


def x_analyse(r_ref, dx_ref, g_ref, d, h):
    first, count = chunk_tiles(h)
    high, low = halves(jnp.concatenate([r_ref[first + t] for t in range(count)], axis=1))
    table = dx_ref[...]
    both = nn(table, high)
    spectrum = both[: 2 * KX] + both[2 * KX :] + nn(table[: 2 * KX], low)
    width = KZ * C // d
    for i in range(d // 2):
        j = owner_order(d)[h * d // 2 + i]
        part = spectrum[:, i * width : (i + 1) * width]
        if width < LANES:
            part = jnp.concatenate([part, jnp.zeros((2 * KX, LANES - width), f32)], axis=1)
        g_ref[j * 2 * KX : (j + 1) * 2 * KX, :] = part


def x_synth(h_ref, ex_ref, mb_ref, d, h):
    width = KZ * C // d
    spectrum = jnp.concatenate(
        [
            h_ref[j * 2 * KX : (j + 1) * 2 * KX, 0:width]
            for j in owner_order(d)[h * d // 2 : (h + 1) * d // 2]
        ],
        axis=1,
    )
    high, low = halves(spectrum)
    rows = nn(ex_ref[...], jnp.concatenate([high, high, low], axis=0))
    first, count = chunk_tiles(h)
    for t in range(count):
        mb_ref[first + t] = rows[:, t * LANES : (t + 1) * LANES]


def pick(ref, kx, d):
    real = ref[pl.ds(kx, d, stride=2 * KX), :]
    imag = ref[pl.ds(KX + kx, d, stride=2 * KX), :]
    return real, imag


def stage_weights(w_ref, w5_ref, wc_ref):
    for ri in range(2):
        for kz in range(2):
            for c in range(C):
                part = w_ref[ri, 0, kz, :, c * C : (c + 1) * C]
                parts = [part]
                if kz:
                    parts = [jnp.zeros((KX, C), f32), part]
                rest = LANES - C * len(parts)
                if rest:
                    parts = parts + [jnp.zeros((KX, rest), f32)]
                w5_ref[ri, kz, pl.ds(c, KX, stride=C), :] = jnp.concatenate(parts, axis=1)

    def pack(kx, carry):
        rows = pl.ds(pl.multiple_of(kx * C, 8), C)
        for ri in range(2):
            parts = [w5_ref[ri, 0, rows, :], w5_ref[ri, 1, rows, :]]
            if LANES > 2 * C:
                parts.append(jnp.zeros((LANES - 2 * C, LANES), f32))
            high, low = halves(jnp.concatenate(parts, axis=0))
            wc_ref[kx, 0:LANES, ri * LANES : (ri + 1) * LANES] = high
            wc_ref[kx, LANES : 2 * LANES, ri * LANES : (ri + 1) * LANES] = low
        return carry

    lax.fori_loop(0, KX, pack, 0)


def mix_modes(h_ref, wc_ref, g2_ref, d):
    def mix(kx, carry):
        real, imag = pick(h_ref, kx, d)
        high, low = halves(jnp.concatenate([real, imag], axis=0))
        left = jnp.concatenate(
            [
                jnp.concatenate([high, high], axis=1),
                jnp.concatenate([low, jnp.zeros_like(low)], axis=1),
            ],
            axis=0,
        )
        both = nn(left, wc_ref[kx])
        both = both[: 2 * d] + both[2 * d :]
        g2_ref[pl.ds(kx, d, stride=2 * KX), :] = both[:d, :LANES] - both[d:, LANES:]
        g2_ref[pl.ds(KX + kx, d, stride=2 * KX), :] = both[:d, LANES:] + both[d:, :LANES]
        return carry

    lax.fori_loop(0, KX, mix, 0, unroll=True)


def stacked(h_ref, kx, d):
    real, imag = pick(h_ref, kx, d)
    return halves(
        jnp.concatenate(
            [
                jnp.concatenate([real, imag], axis=1),
                jnp.concatenate([imag, -real], axis=1),
            ],
            axis=0,
        )
    )


def adjoint_modes(h_ref, wc_ref, g2_ref, d):
    def adjoint(kx, carry):
        high, low = stacked(h_ref, kx, d)
        both = nt(jnp.concatenate([high, low], axis=0), wc_ref[kx])
        total = both[: 2 * d, :LANES] + both[: 2 * d, LANES:] + both[2 * d :, :LANES]
        g2_ref[pl.ds(kx, d, stride=2 * KX), :] = total[:d]
        g2_ref[pl.ds(KX + kx, d, stride=2 * KX), :] = total[d:]
        return carry

    lax.fori_loop(0, KX, adjoint, 0, unroll=True)


def weight_grad(spec_ref, grad_ref, w5_ref, out_ref, d):
    def one(kx, carry):
        high, low = stacked(grad_ref, kx, d)
        real, imag = pick(spec_ref, kx, d)
        shigh, slow = halves(jnp.concatenate([real, imag], axis=0))
        product = tn(
            jnp.concatenate([shigh, slow, shigh], axis=0),
            jnp.concatenate([high, high, low], axis=0),
        )
        rows = pl.ds(pl.multiple_of(kx * C, 8), C)
        for ri in range(2):
            for kz in range(2):
                w5_ref[ri, kz, rows, :] = product[
                    kz * C : (kz + 1) * C, ri * LANES : (ri + 1) * LANES
                ]
        return carry

    lax.fori_loop(0, KX, one, 0, unroll=4)
    group = 8
    for ri in range(2):
        for kz in range(2):
            for first in range(0, C, group):
                out_ref[ri, 0, kz, :, first * C : (first + group) * C] = jnp.concatenate(
                    [
                        w5_ref[ri, kz, pl.ds(c, KX, stride=C), :][:, kz * C : (kz + 1) * C]
                        for c in range(first, first + group)
                    ],
                    axis=1,
                )


def mode_round(n, d, bufs, tables, psem, dsem, base, between, mixer, extra, own_sem=None):
    r_ref, g_ref, h_ref, g2_ref, h2_ref, mb_ref, rb_ref = bufs
    dx_ref, ex_ref = tables
    sample = lax.axis_index("dp")
    out, back = base // 2, base // 2 + 1
    own = pl.ds(pl.multiple_of(sample * 2 * KX, 2 * KX), 2 * KX)

    def forward(h):
        planes_wait(n, r_ref, psem, base + h, h, True)
        x_analyse(r_ref, dx_ref, g_ref, d, h)

        def to_owner(j):
            @pl.when(half_of(j, d) == h)
            def _():
                remote(modes(g_ref)(j), modes(h_ref)(sample), dsem, out, sample, "dp", j).start()

        others("dp", d, to_owner)

    def mix(h):
        @pl.when(half_of(sample, d) == h)
        def _():
            h_ref[own, :] = g_ref[own, :]
            arrived(modes(h_ref), dsem, out, "dp", d)
            mixer(h_ref, g2_ref)
            swap(modes(g2_ref), modes(h2_ref), dsem, back, "dp", d)
            h2_ref[own, :] = g2_ref[own, :]

    def backward(h):
        def from_owner(j):
            @pl.when(half_of(j, d) == h)
            def _():
                wait_one(modes(h2_ref)(j), dsem.at[2 * back + 1, j])

        others("dp", d, from_owner)
        x_synth(h2_ref, ex_ref, mb_ref, d, h)
        send_chunk(
            n, mb_ref, rb_ref, psem, base + 2 + h, h, None if own_sem is None else own_sem.at[h]
        )

    between()
    forward(0)
    mix(0)
    forward(1)
    extra()
    backward(0)
    mix(1)
    backward(1)


def main_kernel(
    n, d,
    x_hbm, go_hbm, w_hbm, wl_ref, bdz_ref, bdzs_ref, bdzg_ref, dy_ref, ey_ref, dx_ref, ex_ref,
    s_hbm, rb_hbm, gs_hbm, gl_hbm,
    x_ref, go_ref, s_ref, p_ref, gs_ref, glo_ref, w_ref, w5_ref, wc_ref, q_ref, q2_ref, o_ref, b_ref,
    msg1_ref, r1_ref, g1_ref, h1_ref, g21_ref, h21_ref, mb1_ref, rb1_ref,
    msg2_ref, r2_ref, g2_ref, h2_ref, g22_ref, h22_ref, mb2_ref,
    gl_ref, glr_ref, glp_ref, gld_ref, glt_ref, glf_ref,
    psem, dsem, qsem, esem, load_sem,
):
    me, sample = lax.axis_index("pencil"), lax.axis_index("dp")
    tiles = C // 8
    keeper = me < tiles
    blocks = Y // GROUP
    parts = 4
    width = Y * Z // parts
    barrier = enter(n, d)
    loads = []
    for i in range(parts):
        view = (slice(None), slice(None), pl.ds(i * width, width))
        loads.append(
            pltpu.make_async_copy(x_hbm.at[view], x_ref.at[view], load_sem.at[i])
        )
    loads.append(pltpu.make_async_copy(w_hbm, w_ref, load_sem.at[parts]))
    loads.append(pltpu.make_async_copy(go_hbm, go_ref, load_sem.at[parts + 1]))
    for load in loads:
        load.start()
    mixing = local_matrix(wl_ref[...].astype(f32).T)

    def strip(block):
        return pl.ds(pl.multiple_of(block * GROUP * Z, GROUP * Z), GROUP * Z)

    def analyse(values_ref, table_ref, h, first, last):
        def one(block, carry):
            z_forward(cells(values_ref, block), table_ref[h], q_ref, block, h)
            return carry

        lax.fori_loop(first, last, one, 0, unroll=8)

    for h in range(2):
        for i in range(parts):
            if h == 0:
                loads[i].wait()
            analyse(x_ref, bdz_ref, h, i * blocks // parts, (i + 1) * blocks // parts)
        y_to_message(q_ref, dy_ref, o_ref, msg1_ref, h)
        if h == 0:
            pl.semaphore_wait(barrier, n + d - 2)
        send_chunk(n, msg1_ref, r1_ref, psem, h, h)

    def stage():
        def product(block, carry):
            p_ref[:, strip(block)] = nn(mixing, cells(x_ref, block))
            return carry

        lax.fori_loop(0, blocks, product, 0, unroll=8)
        loads[parts].wait()
        stage_weights(w_ref, w5_ref, wc_ref)

    mode_round(
        n, d,
        (r1_ref, g1_ref, h1_ref, g21_ref, h21_ref, mb1_ref, rb1_ref),
        (dx_ref, ex_ref), psem, dsem, 0, stage,
        lambda src, dst: mix_modes(src, wc_ref, dst, d),
        lambda: None,
    )
    loads[parts + 1].wait()
    for h in range(2):
        planes_wait(n, rb1_ref, psem, 2 + h, h, True)
        message_to_y(rb1_ref, ey_ref, b_ref, q2_ref, h)
    synth = bdzs_ref[...]

    def slopes(block, carry):
        preact = p_ref[:, strip(block)] + z_backward(q2_ref, synth, block)
        half = (cells(go_ref, block).astype(f32) * gelu_slope(preact)).astype(bf16)
        s_ref[:, :, strip(block)] = half.reshape(ROWS, C, GROUP * Z)
        return carry

    lax.fori_loop(0, blocks, slopes, 0, unroll=8)
    for h in range(2):
        analyse(s_ref, bdzg_ref, h, 0, blocks)
        y_to_message(q_ref, dy_ref, o_ref, msg2_ref, h)
        send_chunk(n, msg2_ref, r2_ref, psem, 4 + h, h)
    store = pltpu.make_async_copy(s_ref, s_hbm, load_sem.at[0])
    store.start()

    def local_sum():
        gl_ref[...] = jnp.zeros_like(gl_ref)
        total = nt(x_ref[0], s_ref[0])
        for x in range(1, ROWS):
            total = total + nt(x_ref[x], s_ref[x])
        gl_ref[:, :, 0:C] = total.reshape(tiles, 8, C)

        def to_keeper(j):
            @pl.when(j < tiles)
            def _():
                remote(gl_ref.at[j], glr_ref.at[me], qsem, 0, me, "pencil", j).start()

        others("pencil", n, to_keeper)

    def local_reduce():
        @pl.when(keeper)
        def _():
            glr_ref[me] = gl_ref[me]
            arrived(lambda j: glr_ref.at[j], qsem, 0, "pencil", n)
            glp_ref[...] = jnp.sum(glr_ref[...], axis=0)
            others(
                "dp",
                d,
                lambda j: remote(glp_ref, gld_ref.at[sample], esem, 0, sample, "dp", j).start(),
            )
            gld_ref[sample] = glp_ref[...]

    def local_spread():
        @pl.when(keeper)
        def _():
            arrived(lambda j: gld_ref.at[j], esem, 0, "dp", d)
            glt_ref[...] = jnp.sum(gld_ref[...], axis=0)
            others(
                "pencil",
                n,
                lambda j: remote(glt_ref, glf_ref.at[me], qsem, 1, me, "pencil", j).start(),
            )
            glf_ref[me] = glt_ref[...]

    mode_round(
        n, d,
        (r2_ref, g2_ref, h2_ref, g22_ref, h22_ref, mb2_ref, rb_hbm),
        (dx_ref, ex_ref), psem, dsem, 4, local_sum,
        lambda src, dst: adjoint_modes(src, wc_ref, dst, d),
        local_reduce,
        load_sem.at[pl.ds(1, 2)],
    )
    local_spread()
    weight_grad(h1_ref, h2_ref, w5_ref, gs_ref, d)
    stores = [
        pltpu.make_async_copy(gs_ref, gs_hbm, load_sem.at[3]),
        pltpu.make_async_copy(glo_ref, gl_hbm, load_sem.at[4]),
    ]
    stores[0].start()
    for base, (first, modes1, modes2, second) in (
        (0, (msg1_ref, g1_ref, g21_ref, mb1_ref)),
        (4, (msg2_ref, g2_ref, g22_ref, mb2_ref)),
    ):
        for h in range(2):
            planes_wait(n, first, psem, base + h, h, False)
            planes_wait(n, second, psem, base + 2 + h, h, False)
        sent(modes(modes1), dsem, base // 2, "dp", d)
        sent(modes(modes2), dsem, base // 2 + 1, "dp", d)

    def keeper_sent(j):
        @pl.when(j < tiles)
        def _():
            wait_one(gl_ref.at[j], qsem.at[0, j])
            wait_one(glf_ref.at[j], qsem.at[3, j])

    others("pencil", n, keeper_sent)
    glo_ref[...] = glf_ref[...].reshape(C, LANES)[:, :C]
    stores[1].start()

    @pl.when(keeper)
    def _():
        sent(lambda j: glp_ref, esem, 0, "dp", d)
        sent(lambda j: glt_ref, qsem, 1, "pencil", n)

    store.wait()
    for one in stores:
        one.wait()
    for h in range(2):
        own = piece(mb2_ref, h)(me)
        pltpu.make_async_copy(own, piece(rb_hbm, h)(me), load_sem.at[1 + h]).wait()
        planes_wait(n, rb_hbm, psem, 6 + h, h, True)


def params(**extra):
    return {
        "compiler_params": pltpu.CompilerParams(vmem_limit_bytes=LIMIT, **extra),
        "cost_estimate": pl.CostEstimate(
            flops=1_000_000_000, bytes_accessed=4_000_000, transcendentals=0
        ),
    }


def local(n, d, field_in, grad_out, w_spec, w_local):
    sds = jax.ShapeDtypeStruct
    lane_tiles = KZ * C // LANES
    values, upstream = field_in[0], grad_out[0]
    cells_shape = values.shape
    ones = np.ones((KZ,))
    scale = z_scale()
    bdz = by_half(z_table(ones, d))
    bdz_grad = by_half(z_table(scale, d))
    synth = tall(z_table(scale, d))
    synth_plain = tall(z_table(ones, d))
    dy = tall(y_forward())
    ey = wide3(y_forward().T)
    dx = tall(x_forward())
    ex = wide3(x_forward().T)

    message = sds((lane_tiles, n * 8, LANES), f32)
    q_shape = pltpu.VMEM((KZ, Y * 2, ROWS * C), f32)
    q2_shape = pltpu.VMEM((KZ, Y * 2, 2 * LANES), f32)
    o_shape = pltpu.VMEM((KZ, 2 * KY, ROWS * C), f32)
    b_shape = pltpu.VMEM((KZ, 2 * KY, 2 * LANES), f32)
    mode_shape = pltpu.VMEM((d * 2 * KX, LANES), f32)
    message_shape = pltpu.VMEM((lane_tiles, n * 8, LANES), f32)
    exchange = [message_shape] * 2 + [mode_shape] * 4 + [message_shape] * 2
    tile = pltpu.VMEM((8, LANES), f32)
    tile_count = C // 8
    anywhere = pl.BlockSpec(memory_space=pl.ANY)
    vmem = pl.BlockSpec(memory_space=pltpu.VMEM)
    slopes, rb, grad_spec, grad_local = pl.pallas_call(
        functools.partial(main_kernel, n, d),
        out_shape=(
            sds(cells_shape, bf16),
            message,
            sds(w_spec.shape, f32),
            sds((C, C), f32),
        ),
        in_specs=[anywhere] * 3 + [vmem] * 8,
        out_specs=(anywhere,) * 4,
        scratch_shapes=[
            pltpu.VMEM(cells_shape, bf16),
            pltpu.VMEM(cells_shape, bf16),
            pltpu.VMEM(cells_shape, bf16),
            pltpu.VMEM((ROWS * C, Y * Z), f32),
            pltpu.VMEM(w_spec.shape, f32),
            pltpu.VMEM((C, C), f32),
            pltpu.VMEM(w_spec.shape, f32),
            pltpu.VMEM((2, 2, KX * C, LANES), f32),
            pltpu.VMEM((KX, 2 * LANES, 2 * LANES), bf16),
            q_shape,
            q2_shape,
            o_shape,
            b_shape,
        ]
        + exchange + exchange[:-1]
        + [
            pltpu.VMEM((tile_count, 8, LANES), f32),
            pltpu.VMEM((n, 8, LANES), f32),
            tile,
            pltpu.VMEM((d, 8, LANES), f32),
            tile,
            pltpu.VMEM((tile_count, 8, LANES), f32),
            pltpu.SemaphoreType.DMA((16,)),
            pltpu.SemaphoreType.DMA((8, d)),
            pltpu.SemaphoreType.DMA((4, n)),
            pltpu.SemaphoreType.DMA((2, d)),
            pltpu.SemaphoreType.DMA((6,)),
        ],
        name="spectral_backward",
        **params(collective_id=0, has_side_effects=True),
    )(values, upstream, w_spec, w_local, bdz, synth, bdz_grad, dy, ey, dx, ex)
    parts = 2
    strip = pl.BlockSpec((ROWS, C, Y * Z // parts), lambda i: (0, 0, i))
    whole = pl.BlockSpec(memory_space=pltpu.VMEM)
    modes_strip = pl.BlockSpec(
        w_spec.shape[:3] + (KX // parts, C * C), lambda i: (0, 0, 0, i, 0)
    )
    grad_in, grad_spec, grad_local = pl.pallas_call(
        last_kernel,
        out_shape=(sds(cells_shape, bf16), sds(w_spec.shape, f32), sds((C, C), f32)),
        grid=(parts,),
        in_specs=[whole, strip, whole, whole, whole, modes_strip, whole],
        out_specs=(strip, modes_strip, whole),
        scratch_shapes=[b_shape, q2_shape, pltpu.VMEM((ROWS * C, ROWS * C), bf16)],
        name="plane_synthesis",
        **params(),
    )(rb, slopes, w_local, ey, synth_plain, grad_spec, grad_local)
    return grad_in[None], grad_spec, grad_local


def solution(mesh):
    n, d = mesh.shape["pencil"], mesh.shape["dp"]
    placed = (
        P("dp", "pencil", None, None),
        P("dp", "pencil", None, None),
        P(None, "pencil", "dp", None, None),
        P(),
    )
    return jax.shard_map(
        functools.partial(local, n, d),
        mesh=mesh,
        in_specs=placed,
        out_specs=(P("dp", "pencil", None, None), P(None, "pencil", "dp", None, None), P()),
        check_vma=False,
    )
```
